32 devices in a mesh: section: 2 (over core), dp: 16 (over z, y, x).
Axes of the slice: x: 2, y: 2, z: 4, core: 2. Of those that a mesh axis runs over, the one named last changes fastest.
Arguments:
- inputs: bfloat16 [2, 192, 24, 1024], P('section', 'dp'), may hold values from -6 to 6
- counts: int32 [2, 192], P('section', 'dp'), may hold values from 1 to 24, as said below
- cotangent: bfloat16 [192, 24, 1000], P('dp', None, 'section'), may hold values from -6 to 6
- lstm_master: float32 [2, 2048, 4096], P('section', 'dp'), may hold values from -0.125 to 0.125
- lstm_copy: bfloat16 [2, 2048, 4096], P('section', 'dp')
- lstm_first: float32 [2, 2048, 4096], P('section', 'dp')
- lstm_second: float32 [2, 2048, 4096], P('section', 'dp')
- mats_master: float32 [3, 1024, 2048], P(None, None, ('section', 'dp')), may hold values from -0.1875 to 0.1875
- mats_copy: bfloat16 [3, 1024, 2048], P(None, None, ('section', 'dp')), may hold values from -0.1875 to 0.1875
- mats_first: float32 [3, 1024, 2048], P(None, None, ('section', 'dp'))
- mats_second: float32 [3, 1024, 2048], P(None, None, ('section', 'dp'))
- out_master: float32 [1024, 1000], P('dp', 'section'), may hold values from -0.1875 to 0.1875
- out_copy: bfloat16 [1024, 1000], P('dp', 'section'), may hold values from -0.1875 to 0.1875
- out_first: float32 [1024, 1000], P('dp', 'section')
- out_second: float32 [1024, 1000], P('dp', 'section')
- vec_master: float32 [8, 2048], P(None, ('section', 'dp'))
- vec_first: float32 [8, 2048], P(None, ('section', 'dp'))
- vec_second: float32 [8, 2048], P(None, ('section', 'dp'))
Outputs:
- logits: bfloat16 [192, 24, 1000], P('dp', None, 'section')
- grad_inputs: float32 [2, 192, 24, 1024], P('section', 'dp')
- lstm_new: float32 [2, 2048, 4096], P('section', 'dp')
- lstm_first_new: float32 [2, 2048, 4096], P('section', 'dp')
- lstm_second_new: float32 [2, 2048, 4096], P('section', 'dp')
- lstm_copy_new: bfloat16 [2, 2048, 4096], P('section', 'dp')
- mats_new: float32 [3, 1024, 2048], P(None, None, ('section', 'dp'))
- mats_first_new: float32 [3, 1024, 2048], P(None, None, ('section', 'dp'))
- mats_second_new: float32 [3, 1024, 2048], P(None, None, ('section', 'dp'))
- mats_copy_new: bfloat16 [3, 1024, 2048], P(None, None, ('section', 'dp'))
- out_new: float32 [1024, 1000], P('dp', 'section')
- out_first_new: float32 [1024, 1000], P('dp', 'section')
- out_second_new: float32 [1024, 1000], P('dp', 'section')
- out_copy_new: bfloat16 [1024, 1000], P('dp', 'section')
- vec_new: float32 [8, 2048], P(None, ('section', 'dp'))
- vec_first_new: float32 [8, 2048], P(None, ('section', 'dp'))
- vec_second_new: float32 [8, 2048], P(None, ('section', 'dp'))
The draws below stay inside these ranges and needn't reach their ends.
Inputs may be any that keep to these rules, and one draw needn't show every extreme that they name: counts[0, u] frames and counts[1, u] labels of utterance u; the first utterance of each aligned block of 12 has 24 of both.
All inputs are finite; a program needn't handle non-finite values.
Results may differ from the reference program's by a relative error of at most 0.012.
The reference program's roundings to bfloat16 on the way count: a program that leaves them out, or rounds other values in their place, can miss the bound.
Values may be sent and summed in bfloat16 or wider, within the bound.
A program may use at most 256 MiB of HBM per device.

```python
import math
import jax
import jax.numpy as jnp
from jax import lax

D = 1024
VOCAB = 1000
UMAX = 24
UTT_DEV = 12
STEP = 5
UTTS = 192
N_DP = 16


GRAD_LSTM = 0.03


GRAD_LSTM_SECOND = 0.08


GRAD_OUT = 0.45


def first_moment(key, extent, scale):
    values = jax.random.normal(key, extent, jnp.float32)
    return values * scale / 9.0


def second_moment(key, extent, scale):
    factors = jnp.exp(jax.random.uniform(key, extent, jnp.float32, math.log(0.5), math.log(8.0)))
    return factors * scale * scale / 999.0


def base_scale():
    return math.sqrt(UTTS * UMAX)


def mats_factor():
    return jnp.array([0.05, 0.05, 0.15], jnp.float32)[:, None, None] * base_scale()


def vec_factor():
    return jnp.array([0.05, 0.05, 0.1, 0.1, 0.1, 0.3, 0.3, 0.5], jnp.float32)[:, None] * base_scale()


def vec_second_factor():
    return jnp.array([0.25, 0.25, 0.2, 0.2, 0.2, 0.3, 0.3, 0.5], jnp.float32)[:, None] * base_scale()


def draw_counts(key, part):
    key = jax.random.fold_in(key, 5)
    lowest = max(1, UMAX // 4)
    values = jax.random.randint(key, (2, UTTS), lowest, UMAX + 1)
    position = jnp.arange(UTTS)
    return jnp.where(position[None, :] % UTT_DEV == 0, UMAX, values).astype(jnp.int32)


def draw_lstm_copy(key, part):
    key = jax.random.fold_in(key, 51)
    entry_key, column_key = jax.random.split(key)
    spread = (2 * D) ** (-0.5)
    values = jax.random.normal(entry_key, (2, 2 * D, 4 * D), jnp.float32) * spread
    columns = jax.random.normal(column_key, (4 * D,), jnp.float32) * spread
    first_section = jnp.arange(2)[:, None, None] == 0
    input_rows = jnp.arange(2 * D)[None, :, None] < D
    return jnp.where(first_section & input_rows, values + columns[None, None, :], values).astype(jnp.bfloat16)


def draw_lstm_first(key, part):
    key = jax.random.fold_in(key, 11)
    return first_moment(key, (2, 2 * D, 4 * D), GRAD_LSTM * base_scale())


def draw_lstm_second(key, part):
    key = jax.random.fold_in(key, 12)
    return second_moment(key, (2, 2 * D, 4 * D), GRAD_LSTM_SECOND * base_scale())


def draw_mats_first(key, part):
    key = jax.random.fold_in(key, 21)
    return first_moment(key, (3, D, 2 * D), mats_factor())


def draw_mats_second(key, part):
    key = jax.random.fold_in(key, 22)
    return second_moment(key, (3, D, 2 * D), mats_factor())


def draw_out_first(key, part):
    key = jax.random.fold_in(key, 31)
    return first_moment(key, (D, VOCAB), GRAD_OUT * base_scale())


def draw_out_second(key, part):
    key = jax.random.fold_in(key, 32)
    return second_moment(key, (D, VOCAB), GRAD_OUT * base_scale())


def draw_vec_master(key, part):
    key = jax.random.fold_in(key, 41)
    noise_key, gain_key = jax.random.split(key)
    row_scale = jnp.array([0.2, 0.2, 0.2, 0.2, 0.2, 0.5, 0.1, 0.2], jnp.float32)[:, None]
    values = jax.random.normal(noise_key, (8, 2 * D), jnp.float32) * row_scale
    gains = jax.random.uniform(gain_key, (2 * D,), jnp.float32, 0.5, 1.5)
    column = jnp.arange(2 * D)
    norm_row = jnp.where(column < D, gains, values[4])
    return values.at[4].set(norm_row)


def draw_vec_first(key, part):
    key = jax.random.fold_in(key, 42)
    return first_moment(key, (8, 2 * D), vec_factor())


def draw_vec_second(key, part):
    key = jax.random.fold_in(key, 43)
    return second_moment(key, (8, 2 * D), vec_second_factor())


def block_scale(key, shape, cuts, least, top_value):
    level, own = 1.0, jax.random.fold_in(key, 6)
    for axis_at, blocks in cuts:
        draws = jnp.exp(jax.random.uniform(jax.random.fold_in(own, axis_at), (blocks,), jnp.float32, least / len(cuts), top_value / len(cuts)))
        level = level * jnp.repeat(draws, shape[axis_at] // blocks).reshape([-1 if axis == axis_at else 1 for axis in range(len(shape))])
    return level


def normal_values(stream_key, shape, width, reach, cuts=(), dtype=jnp.bfloat16):
    values = width * jax.random.normal(stream_key, shape, jnp.float32)
    if cuts:
        values = values * block_scale(stream_key, shape, cuts, -0.22, 0.18)
    return jnp.clip(values, -reach, reach).astype(dtype)


def setup_inputs(seed: int = 0) -> dict:
    seeds = jax.random.split(jax.random.key(seed), 19)
    return {
        "inputs": normal_values(seeds[0], (2, UTTS, UMAX, D), 1.0, 6.0, ((0, 2), (1, 16))),
        "counts": draw_counts(jax.random.fold_in(seeds[18], 71), 0),
        "cotangent": normal_values(seeds[2], (UTTS, UMAX, VOCAB), 1.0, 6.0, ((0, 16), (2, 2))),
        "lstm_master": normal_values(seeds[3], (2, 2 * D, 4 * D), (2 * D) ** -0.5, 0.125, ((0, 2), (1, 16)), jnp.float32),
        "lstm_copy": draw_lstm_copy(jax.random.fold_in(seeds[18], 71), 0),
        "lstm_first": draw_lstm_first(jax.random.fold_in(seeds[18], 71), 0),
        "lstm_second": draw_lstm_second(jax.random.fold_in(seeds[18], 71), 0),
        "mats_master": normal_values(seeds[7], (3, D, 2 * D), D ** -0.5, 0.1875, ((2, 32),), jnp.float32),
        "mats_copy": normal_values(seeds[8], (3, D, 2 * D), D ** -0.5, 0.1875, ((2, 32),)),
        "mats_first": draw_mats_first(jax.random.fold_in(seeds[18], 71), 0),
        "mats_second": draw_mats_second(jax.random.fold_in(seeds[18], 71), 0),
        "out_master": normal_values(seeds[11], (D, VOCAB), D ** -0.5, 0.1875, ((0, 16), (1, 2)), jnp.float32),
        "out_copy": normal_values(seeds[12], (D, VOCAB), D ** -0.5, 0.1875, ((0, 16), (1, 2))),
        "out_first": draw_out_first(jax.random.fold_in(seeds[18], 71), 0),
        "out_second": draw_out_second(jax.random.fold_in(seeds[18], 71), 0),
        "vec_master": draw_vec_master(jax.random.fold_in(seeds[18], 71), 0),
        "vec_first": draw_vec_first(jax.random.fold_in(seeds[18], 71), 0),
        "vec_second": draw_vec_second(jax.random.fold_in(seeds[18], 71), 0),
    }


NORM_EPS = 1e-05
ENERGY_OFFSET = -4.0
BETA_ONE = 0.9
BETA_TWO = 0.999
ADAM_EPS = 1e-08
WEIGHT_DECAY = 0.01
RATE_LSTM = 0.05
RATE_MATRIX = 0.02
RATE_VECTOR = 0.3
HIGH = lax.Precision.HIGHEST

@jax.custom_vjp
def low(v):
    return lax.optimization_barrier(v.astype(jnp.bfloat16)).astype(jnp.float32)

@jax.custom_vjp
def low_back(v):
    return v

def low_keep(v):
    return (low(v), None)

def low_pass(kept, grad):
    return (grad,)

def back_keep(v):
    return (v, None)

def back_low(kept, grad):
    return (low(grad),)
low.defvjp(low_keep, low_pass)
low_back.defvjp(back_keep, back_low)

def energies(queries, keys, shifts, weights):

    def single(operands):
        query_rows, key_rows = operands
        squash_all = jnp.tanh(query_rows[:, None, :] + key_rows[None, :, :] + shifts)
        return jnp.einsum('ijk,k->ij', squash_all, weights, precision=HIGH)
    return lax.map(jax.checkpoint(single), (queries, keys))

def align(queries, keys, shifts, weights, frame_mask):
    half_width = queries.shape[-1] // 2
    length = queries.shape[1]
    monotone = energies(queries[..., :half_width], keys[..., :half_width], shifts[:half_width], weights[:half_width]) + ENERGY_OFFSET
    windowed = energies(queries[..., half_width:], keys[..., half_width:], shifts[half_width:], weights[half_width:])
    frame_rows = frame_mask[:, None, :]
    select = jax.nn.sigmoid(monotone) * frame_rows
    leave_rate = jax.nn.softplus(monotone) * frame_rows
    row_index = lax.broadcasted_iota(jnp.int32, (length, length), 0)
    col_index = lax.broadcasted_iota(jnp.int32, (length, length), 1)
    before = (row_index < col_index).astype(jnp.float32)
    cumulated = jnp.einsum('uij,jl->uil', leave_rate, before, precision=HIGH)
    below = row_index >= col_index
    spacing = jnp.where(below, cumulated[:, :, :, None] - cumulated[:, :, None, :], 0.0)
    transfer = jnp.exp(-spacing) * below.astype(jnp.float32)
    first_slot = (col_index[0] == 0).astype(jnp.float32)
    initial = jnp.broadcast_to(first_slot, (queries.shape[0], length))

    def advance(previous, items):
        moving, probable = items
        waiting = jnp.einsum('ujk,uk->uj', moving, previous, precision=HIGH)
        current = probable * waiting
        return (current, current)
    _, alignments = lax.scan(advance, initial, (jnp.swapaxes(transfer, 0, 1), jnp.swapaxes(select, 0, 1)))
    alignment = jnp.swapaxes(alignments, 0, 1)
    earlier = jnp.concatenate([windowed[..., :1], windowed[..., :-1]], -1)
    later = jnp.concatenate([windowed[..., 1:], windowed[..., -1:]], -1)
    own_factor = jnp.where(col_index[0] == 0, 1.0, jax.nn.sigmoid(windowed - earlier))
    next_alignment = jnp.concatenate([alignment[..., 1:], jnp.zeros_like(alignment[..., :1])], -1)
    return alignment * own_factor + next_alignment * jax.nn.sigmoid(windowed - later)

def recur(sequence, weight, bias):
    batch_size = sequence.shape[0]
    model_width = sequence.shape[2]

    def advance(carried, inflow):
        hidden, cell_state = carried
        joined = jnp.concatenate([inflow, hidden], -1)
        gate_sums = low_back(jnp.dot(joined, weight, precision=HIGH) + bias)
        cell_new = jax.nn.sigmoid(gate_sums[:, model_width:2 * model_width]) * cell_state + jax.nn.sigmoid(gate_sums[:, :model_width]) * jnp.tanh(gate_sums[:, 2 * model_width:3 * model_width])
        hidden_new = low(jax.nn.sigmoid(gate_sums[:, 3 * model_width:]) * jnp.tanh(cell_new))
        return ((hidden_new, cell_new), hidden_new)
    zeros_state = jnp.zeros((batch_size, model_width), jnp.float32)
    _, hiddens = lax.scan(advance, (zeros_state, zeros_state), jnp.swapaxes(sequence, 0, 1))
    return jnp.swapaxes(hiddens, 0, 1)

def forward(params, frames, labels_in, frame_mask):
    lstm_weight, mats_weight, out_weight, vectors = params
    model_width = frames.shape[-1]
    center = frames - lax.optimization_barrier(jnp.mean(frames, -1, keepdims=True))
    scaled = center * lax.rsqrt(lax.optimization_barrier(jnp.mean(center * center, -1, keepdims=True)) + NORM_EPS)
    normed = low(scaled * vectors[4, :model_width] + vectors[4, model_width:])
    encoded = recur(normed, lstm_weight[0], vectors[0:2].reshape(-1))
    memory = low_back(low(frames + encoded))
    decoded = recur(labels_in, lstm_weight[1], vectors[2:4].reshape(-1))
    queries = low_back(jnp.einsum('uld,de->ule', decoded, mats_weight[0], precision=HIGH))
    keys = low_back(jnp.einsum('uld,de->ule', memory, mats_weight[1], precision=HIGH))
    weights_beta = low(align(queries, keys, vectors[5], vectors[6], frame_mask))
    context = low_back(low(jnp.einsum('uik,ukd->uid', weights_beta, memory, precision=HIGH)))
    joined = jnp.concatenate([decoded, context], -1)
    before_tanh = low_back(jnp.einsum('uie,oe->uio', joined, mats_weight[2], precision=HIGH) + vectors[7, :model_width])
    squashed = low(jnp.tanh(before_tanh))
    vocab = out_weight.shape[1]
    return jnp.einsum('uio,ov->uiv', squashed, out_weight, precision=HIGH) + vectors[7, model_width:model_width + vocab]

def adamw(master, first, second, grad, rate):
    first_new = BETA_ONE * first + (1.0 - BETA_ONE) * grad
    second_new = BETA_TWO * second + (1.0 - BETA_TWO) * grad * grad
    first_hat = first_new / (1.0 - BETA_ONE ** STEP)
    second_hat = second_new / (1.0 - BETA_TWO ** STEP)
    master_new = master - rate * (first_hat / (jnp.sqrt(second_hat) + ADAM_EPS) + WEIGHT_DECAY * master)
    return (master_new, first_new, second_new)

def reference(inputs, counts, cotangent, lstm_master, lstm_copy, lstm_first, lstm_second, mats_master, mats_copy, mats_first, mats_second, out_master, out_copy, out_first, out_second, vec_master, vec_first, vec_second):
    params = (lstm_copy.astype(jnp.float32), mats_copy.astype(jnp.float32), out_copy.astype(jnp.float32), low(vec_master))
    slot_index = lax.broadcasted_iota(jnp.int32, (2, UTTS, UMAX), 2)
    slot_mask = (slot_index < counts[:, :, None]).astype(jnp.float32)
    frames = inputs[0].astype(jnp.float32)
    labels_in = inputs[1].astype(jnp.float32)
    grad_out = cotangent.astype(jnp.float32) * slot_mask[1][:, :, None]

    def regroup(array):
        return array.reshape((N_DP, UTT_DEV) + array.shape[1:])
    zero_grads = jax.tree.map(jnp.zeros_like, params)

    def visit(summed, items):
        frame_rows, label_rows, mask_rows, grad_rows = items

        def partial_forward(param_set, frame_part, label_part):
            return forward(param_set, frame_part, label_part, mask_rows)
        logits_here, pullback = jax.vjp(partial_forward, params, frame_rows, label_rows)
        param_grads, frame_grads, label_grads = pullback(grad_rows)
        return (jax.tree.map(jnp.add, summed, param_grads), (logits_here.astype(jnp.bfloat16), frame_grads, label_grads))
    sums, (logits, frame_grads, label_grads) = lax.scan(visit, zero_grads, (regroup(frames), regroup(labels_in), regroup(slot_mask[0]), regroup(grad_out)))
    logits = logits.reshape(UTTS, UMAX, VOCAB)
    grad_inputs = jnp.stack([frame_grads.reshape(UTTS, UMAX, D), label_grads.reshape(UTTS, UMAX, D)])
    lstm_new, lstm_first_new, lstm_second_new = adamw(lstm_master, lstm_first, lstm_second, sums[0], RATE_LSTM)
    mats_new, mats_first_new, mats_second_new = adamw(mats_master, mats_first, mats_second, sums[1], RATE_MATRIX)
    out_new, out_first_new, out_second_new = adamw(out_master, out_first, out_second, sums[2], RATE_MATRIX)
    vec_new, vec_first_new, vec_second_new = adamw(vec_master, vec_first, vec_second, sums[3], RATE_VECTOR)
    return (logits, grad_inputs, lstm_new, lstm_first_new, lstm_second_new, lstm_new.astype(jnp.bfloat16), mats_new, mats_first_new, mats_second_new, mats_new.astype(jnp.bfloat16), out_new, out_first_new, out_second_new, out_new.astype(jnp.bfloat16), vec_new, vec_first_new, vec_second_new)
```

```python
import functools
import jax
import jax.numpy as jnp
from jax import lax
from jax.experimental import pallas as pl
from jax.experimental.pallas import tpu as pltpu

ROWS = 16
LANES = 128
ENERGY_OFFSET = -4.0
VMEM_SPEC = pl.BlockSpec(memory_space=pltpu.VMEM)
SMEM_SPEC = pl.BlockSpec(memory_space=pltpu.SMEM)
VMEM_LIMIT = 60 * 1024 * 1024


def contract(left, right, left_dim, right_dim):
    return lax.dot_general(
        left, right, (((left_dim,), (right_dim,)), ((), ())), preferred_element_type=jnp.float32
    )


def lstm_forward_kernel(x_ref, w_ref, b_ref, act_ref, cell_ref, h_ref, state):
    width = x_ref.shape[1]
    steps = x_ref.shape[0] // ROWS
    for q in range(4):
        columns = slice(q * width, (q + 1) * width)
        act_ref[:, columns] = (
            jnp.dot(x_ref[...], w_ref[:width, columns], preferred_element_type=jnp.float32)
            + b_ref[:, columns]
        )
    state[...] = jnp.zeros_like(state)
    cell_ref[:ROWS] = jnp.zeros((ROWS, width), jnp.float32)

    def step(t, carry):
        rows = pl.ds(pl.multiple_of(t * ROWS, ROWS), ROWS)
        after = pl.ds(pl.multiple_of((t + 1) * ROWS, ROWS), ROWS)
        hidden = state[...]

        def gate(q):
            columns = slice(q * width, (q + 1) * width)
            return act_ref[rows, columns] + jnp.dot(
                hidden, w_ref[width:, columns], preferred_element_type=jnp.float32
            )

        in_gate = jax.nn.sigmoid(gate(0))
        forget = jax.nn.sigmoid(gate(1))
        candidate = jnp.tanh(gate(2))
        cell = forget * cell_ref[rows] + in_gate * candidate
        out_gate = jax.nn.sigmoid(gate(3))
        hidden_new = (out_gate * jnp.tanh(cell)).astype(jnp.bfloat16)
        act_ref[rows, :width] = in_gate
        act_ref[rows, width : 2 * width] = forget
        act_ref[rows, 2 * width : 3 * width] = candidate
        act_ref[rows, 3 * width :] = out_gate
        cell_ref[after] = cell
        h_ref[rows] = hidden_new
        state[...] = hidden_new
        return carry

    lax.fori_loop(0, steps, step, 0)


def lstm_forward(x, weight, bias):
    rows, width = x.shape
    return pl.pallas_call(
        lstm_forward_kernel,
        out_shape=(
            jax.ShapeDtypeStruct((rows, 4 * width), jnp.float32),
            jax.ShapeDtypeStruct((rows + ROWS, width), jnp.float32),
            jax.ShapeDtypeStruct((rows, width), jnp.bfloat16),
        ),
        in_specs=[VMEM_SPEC] * 3,
        out_specs=(VMEM_SPEC,) * 3,
        scratch_shapes=[pltpu.VMEM((ROWS, width), jnp.bfloat16)],
        compiler_params=pltpu.CompilerParams(vmem_limit_bytes=VMEM_LIMIT),
    )(x, weight, bias)


def lstm_backward_kernel(act_ref, cell_ref, outer_ref, wt_ref, dpre_ref, state, held):
    width = outer_ref.shape[1]
    steps = outer_ref.shape[0] // ROWS
    state[...] = jnp.zeros_like(state)
    held[...] = jnp.zeros_like(held)

    def step(k, carry):
        t = steps - 1 - k
        rows = pl.ds(pl.multiple_of(t * ROWS, ROWS), ROWS)
        after = pl.ds(pl.multiple_of((t + 1) * ROWS, ROWS), ROWS)
        hidden_total = outer_ref[rows] + jnp.dot(
            state[...], wt_ref[...], preferred_element_type=jnp.float32
        )
        in_gate = act_ref[rows, :width]
        forget = act_ref[rows, width : 2 * width]
        candidate = act_ref[rows, 2 * width : 3 * width]
        out_gate = act_ref[rows, 3 * width :]
        squash = jnp.tanh(cell_ref[after])
        cell_total = held[...] + hidden_total * out_gate * (1.0 - squash * squash)
        held[...] = cell_total * forget
        grads = jnp.concatenate(
            [
                cell_total * candidate * in_gate * (1.0 - in_gate),
                cell_total * cell_ref[rows] * forget * (1.0 - forget),
                cell_total * in_gate * (1.0 - candidate * candidate),
                hidden_total * squash * out_gate * (1.0 - out_gate),
            ],
            -1,
        ).astype(jnp.bfloat16)
        state[...] = grads
        dpre_ref[rows] = grads
        return carry

    lax.fori_loop(0, steps, step, 0)


def lstm_backward(act, cell, outer, weight_t):
    rows, width = outer.shape
    return pl.pallas_call(
        lstm_backward_kernel,
        out_shape=jax.ShapeDtypeStruct((rows, 4 * width), jnp.bfloat16),
        in_specs=[VMEM_SPEC] * 4,
        out_specs=VMEM_SPEC,
        scratch_shapes=[
            pltpu.VMEM((ROWS, 4 * width), jnp.bfloat16),
            pltpu.VMEM((ROWS, width), jnp.float32),
        ],
        compiler_params=pltpu.CompilerParams(vmem_limit_bytes=VMEM_LIMIT),
    )(act, cell, outer, weight_t)


def attention_kernel(
    frames_ref,
    labels_ref,
    mask_ref,
    dec_ref,
    mem_ref,
    m0_ref,
    m1_ref,
    m2_ref,
    vec_ref,
    pull_ref,
    squash_ref,
    context_ref,
    dz_ref,
    dq_ref,
    dk_ref,
    ddec_ref,
    dmem_ref,
    dvec_ref,
    q_s,
    k_s,
    mem_s,
    ctx_s,
    dqa_s,
    dka_s,
    e_s,
    sel_s,
    prob_s,
    pow_s,
    w_s,
    a_s,
    own_s,
    nxt_s,
    g_s,
    d_s,
    bc_s,
):
    rows, width = dec_ref.shape
    utts = frames_ref.shape[0]
    length = rows // utts
    low = jnp.bfloat16
    f32 = jnp.float32
    lane = lax.broadcasted_iota(jnp.int32, (length, LANES), 1)
    lane_block = lax.broadcasted_iota(jnp.int32, (length, 8, LANES), 2)

    q_s[...] = jnp.dot(dec_ref[...], m0_ref[...], preferred_element_type=f32) + vec_ref[5:6]
    k_s[...] = jnp.dot(mem_ref[...], m1_ref[...], preferred_element_type=f32)
    mem_s[...] = mem_ref[...].astype(f32)
    e_s[...] = jnp.zeros_like(e_s)
    d_s[...] = jnp.zeros_like(d_s)

    tile = 256
    group = 4

    for u in range(utts):
        at = u * length

        def energy_step(block, sums, at=at):
            base = block * group
            for offset in range(group):
                j = base + offset
                row = k_s[pl.ds(at + j, 1), :]
                for head in range(2):
                    total = jnp.zeros((length, LANES), f32)
                    for c in range(width // LANES):
                        columns = slice(head * width + c * LANES, head * width + (c + 1) * LANES)
                        total = total + jnp.tanh(
                            q_s[at : at + length, columns] + row[:, columns]
                        ) * vec_ref[6:7, columns]
                    value = jnp.sum(total, -1, keepdims=True)
                    sums = tuple(
                        jnp.where(lane == j, value, s) if h == head else s
                        for h, s in enumerate(sums)
                    )
            return sums

        blocks = (frames_ref[u] + (group - 1)) // group
        zero = jnp.zeros((length, LANES), f32)
        mono, window = lax.fori_loop(0, blocks, energy_step, (zero, zero))
        e_s[0, :, u, :] = mono
        e_s[1, :, u, :] = window

    mask = mask_ref[...][None]
    mono = e_s[0] + ENERGY_OFFSET
    window = e_s[1]
    chosen = jax.nn.sigmoid(mono)
    inside = (lane_block < length).astype(f32)
    sel_s[...] = chosen * mask
    leave = (jnp.maximum(mono, 0.0) + jnp.log1p(jnp.exp(-jnp.abs(mono)))) * mask
    prob = jnp.exp(-leave) * inside
    prob_s[...] = prob

    def right(value, distance):
        return pltpu.roll(value, distance, value.ndim - 1)

    def left(value, distance):
        return pltpu.roll(value, LANES - distance, value.ndim - 1)

    power = jnp.where(lane_block >= 1, right(prob, 1), 0.0) * inside
    for n in range(5):
        pow_s[n] = power
        if n < 4:
            power = jnp.where(lane_block >= 2 ** (n + 1), power * right(power, 2**n), 0.0)

    lane_row = lax.broadcasted_iota(jnp.int32, (8, LANES), 1)

    def align_step(i, before):
        total = before
        for n in range(5):
            total = total + pow_s[n, i] * right(total, 2**n)
        w_s[i] = total
        now = sel_s[i] * total
        a_s[i] = now
        return now

    lax.fori_loop(0, length, align_step, jnp.where(lane_row == 0, 1.0, 0.0).astype(f32))

    aligned = a_s[...]
    own = jnp.where(lane_block == 0, 1.0, jax.nn.sigmoid(window - right(window, 1)))
    nxt = jax.nn.sigmoid(window - left(window, 1))
    own_s[...] = own
    nxt_s[...] = nxt
    beta = aligned * own + jnp.where(lane_block < length - 1, left(aligned, 1), 0.0) * nxt
    g_s[...] = beta

    for u in range(utts):
        at = u * length
        weights = g_s[:, u, :].astype(low)[:, :length]
        ctx_s[at : at + length] = jnp.dot(
            weights, mem_s[at : at + length].astype(low), preferred_element_type=f32
        )
    context_ref[...] = ctx_s[...].astype(low)

    squash = jnp.tanh(
        contract(dec_ref[...], m2_ref[:, :width], 1, 1)
        + contract(context_ref[...], m2_ref[:, width:], 1, 1)
        + vec_ref[7:8, :width]
    )
    squash_ref[...] = squash.astype(low)
    dz = (pull_ref[...] * (1.0 - squash * squash)).astype(low)
    dz_ref[...] = dz
    dvec_ref[...] = jnp.zeros_like(dvec_ref)
    dvec_ref[7:8, :width] = jnp.sum(dz.astype(f32), 0, keepdims=True)
    ddec_ref[...] = jnp.dot(dz, m2_ref[:, :width], preferred_element_type=f32)
    ctx_s[...] = (
        jnp.dot(dz, m2_ref[:, width:], preferred_element_type=f32).astype(low).astype(f32)
    )

    pad = jnp.zeros((length, LANES - length), f32)
    for u in range(utts):
        at = u * length
        weights = g_s[:, u, :].astype(low)[:, :length]
        pulled = ctx_s[at : at + length].astype(low)
        beta_grad = contract(pulled, mem_s[at : at + length].astype(low), 1, 1)
        e_s[0, :, u, :] = jnp.concatenate([beta_grad, pad], -1)
        mem_s[at : at + length] = contract(weights, pulled, 0, 0)

    beta_grad = e_s[0]
    own = own_s[...]
    nxt = nxt_s[...]
    g_s[...] = beta_grad * own + jnp.where(lane_block >= 1, right(beta_grad * nxt, 1), 0.0)
    aligned = a_s[...]
    from_own = jnp.where(lane_block >= 1, beta_grad * aligned * own * (1.0 - own), 0.0)
    from_next = (
        beta_grad
        * jnp.where(lane_block < length - 1, left(aligned, 1), 0.0)
        * nxt
        * (1.0 - nxt)
    )
    d_s[1] = (from_own - left(from_own, 1) + from_next - right(from_next, 1)) * inside

    prob = prob_s[...]
    power = jnp.where(lane_block < length - 1, prob, 0.0)
    for n in range(5):
        pow_s[n] = power
        if n < 4:
            power = power * left(power, 2**n)

    def retreat_step(k, after):
        i = length - 1 - k
        grad_align = g_s[i] + after
        e_s[0, i] = grad_align
        total = sel_s[i] * grad_align
        for n in range(5):
            total = total + pow_s[n, i] * left(total, 2**n)
        e_s[1, i] = total
        return total

    lax.fori_loop(0, length, retreat_step, jnp.zeros((8, LANES), f32))
    reached = w_s[...]
    grad_select = reached * e_s[0]
    grad_prob = reached * jnp.where(lane_block < length - 1, left(e_s[1], 1), 0.0)
    chosen = sel_s[...]
    d_s[0] = grad_select * chosen * (1.0 - chosen) - grad_prob * prob * chosen

    dka_s[...] = jnp.zeros_like(dka_s)

    def energy_back(u, dvec):
        at = pl.multiple_of(u * length, 8)
        for head in range(2):
            grads = d_s[head, :, pl.ds(u, 1), :].reshape(length, LANES)
            for j in range(length):
                bc_s[head, j] = jnp.broadcast_to(grads[:, j : j + 1], (length, LANES))
        count = (frames_ref[u] + 1) // 2
        for c in range(2 * width // tile):
            columns = slice(c * tile, (c + 1) * tile)
            head = c * tile // width
            q_now = q_s[pl.ds(at, length), columns]

            def back_step(block, sums, head=head, columns=columns, q_now=q_now):
                dq, dw = sums
                for offset in range(2):
                    j = block * 2 + offset
                    squash_all = jnp.tanh(q_now + k_s[pl.ds(at + j, 1), columns])
                    grad = bc_s[head, j]
                    grad = jnp.concatenate([grad] * (tile // LANES), -1)
                    scaled = grad * squash_all
                    dw = dw + scaled
                    moved = grad - scaled * squash_all
                    dq = dq + moved
                    dka_s[pl.ds(at + j, 1), columns] = jnp.sum(moved, 0, keepdims=True)
                return (dq, dw)

            zero = jnp.zeros((length, tile), f32)
            dq, dw = lax.fori_loop(0, count, back_step, (zero, zero))
            dq = dq * vec_ref[6:7, columns]
            dqa_s[pl.ds(at, length), columns] = dq
            dvec_ref[5:6, columns] += jnp.sum(dq, 0, keepdims=True)
            dvec_ref[6:7, columns] += jnp.sum(dw, 0, keepdims=True)
        return dvec

    lax.fori_loop(0, utts, energy_back, 0)
    dq_ref[...] = dqa_s[...].astype(low)
    dk_ref[...] = (dka_s[...] * vec_ref[6:7]).astype(low)
    ddec_ref[...] += contract(dq_ref[...], m0_ref[...], 1, 1)
    dmem_ref[...] = (mem_s[...] + contract(dk_ref[...], m1_ref[...], 1, 1)).astype(low)


def attention(frames, labels, decoded, memory, mats, vectors, pull):
    rows, width = decoded.shape
    utts = frames.shape[0]
    length = rows // utts
    lane = lax.broadcasted_iota(jnp.int32, (8, LANES), 1)
    padded = jnp.concatenate([frames, jnp.zeros((8 - utts,), frames.dtype)])
    mask = (lane < padded[:, None]).astype(jnp.float32)
    low, f32 = jnp.bfloat16, jnp.float32
    small = (length, 8, LANES)
    return pl.pallas_call(
        attention_kernel,
        out_shape=(
            jax.ShapeDtypeStruct((rows, width), low),
            jax.ShapeDtypeStruct((rows, width), low),
            jax.ShapeDtypeStruct((rows, width), low),
            jax.ShapeDtypeStruct((rows, 2 * width), low),
            jax.ShapeDtypeStruct((rows, 2 * width), low),
            jax.ShapeDtypeStruct((rows, width), f32),
            jax.ShapeDtypeStruct((rows, width), low),
            jax.ShapeDtypeStruct((8, 2 * width), f32),
        ),
        in_specs=[SMEM_SPEC] * 2 + [VMEM_SPEC] * 8,
        out_specs=(VMEM_SPEC,) * 8,
        scratch_shapes=[
            pltpu.VMEM((rows, 2 * width), f32),
            pltpu.VMEM((rows, 2 * width), f32),
            pltpu.VMEM((rows, width), f32),
            pltpu.VMEM((rows, width), f32),
            pltpu.VMEM((rows, 2 * width), f32),
            pltpu.VMEM((rows, 2 * width), f32),
            pltpu.VMEM((2,) + small, f32),
            pltpu.VMEM(small, f32),
            pltpu.VMEM(small, f32),
            pltpu.VMEM((5,) + small, f32),
            pltpu.VMEM(small, f32),
            pltpu.VMEM(small, f32),
            pltpu.VMEM(small, f32),
            pltpu.VMEM(small, f32),
            pltpu.VMEM(small, f32),
            pltpu.VMEM((2,) + small, f32),
            pltpu.VMEM((2, length, length, LANES), f32),
        ],
        compiler_params=pltpu.CompilerParams(vmem_limit_bytes=VMEM_LIMIT),
    )(frames, labels, mask, decoded, memory, mats[0], mats[1], mats[2], vectors, pull)


from jax.sharding import PartitionSpec as P

STEP = 5
NORM_EPS = 1e-05
BETA_ONE = 0.9
BETA_TWO = 0.999
ADAM_EPS = 1e-08
WEIGHT_DECAY = 0.01
RATE_LSTM = 0.05
RATE_MATRIX = 0.02
RATE_VECTOR = 0.3


def swapped(block):
    return lax.ppermute(block, "section", [(0, 1), (1, 0)])


def adamw(master, first, second, grad, rate):
    first_new = BETA_ONE * first + (1.0 - BETA_ONE) * grad
    second_new = BETA_TWO * second + (1.0 - BETA_TWO) * grad * grad
    first_hat = first_new / (1.0 - BETA_ONE**STEP)
    second_hat = second_new / (1.0 - BETA_TWO**STEP)
    master_new = master - rate * (
        first_hat / (jnp.sqrt(second_hat) + ADAM_EPS) + WEIGHT_DECAY * master
    )
    return (master_new, first_new, second_new)


def slot_major(block):
    batch_size, length, width = block.shape
    padded = jnp.pad(jnp.swapaxes(block, 0, 1), ((0, 0), (0, ROWS - batch_size), (0, 0)))
    return padded.reshape(length * ROWS, width)


def utt_major(block, batch_size):
    width = block.shape[-1]
    return jnp.swapaxes(block.reshape(-1, ROWS, width)[:, :batch_size], 0, 1)


def local(
    inputs,
    counts,
    cotangent,
    lstm_master,
    lstm_copy,
    lstm_first,
    lstm_second,
    mats_master,
    mats_copy,
    mats_first,
    mats_second,
    out_master,
    out_copy,
    out_first,
    out_second,
    vec_master,
    vec_first,
    vec_second,
):
    low, f32 = jnp.bfloat16, jnp.float32
    section_index = lax.axis_index("section")
    on_encoder = section_index == 0
    lstm_full, out_half = (
        lax.all_gather(lstm_copy, "dp", axis=1, tiled=True),
        lax.all_gather(out_copy, "dp", axis=0, tiled=True),
    )
    mats_full, vectors_low = (
        lax.all_gather(mats_copy, ("section", "dp"), axis=2, tiled=True),
        lax.all_gather(vec_master.astype(low), ("section", "dp"), axis=1, tiled=True),
    )
    out_full = lax.all_gather(out_half, "section", axis=1, tiled=True)
    vectors = vectors_low.astype(f32)
    weight = lstm_full[0]
    model_width = weight.shape[0] // 2
    vocab_half = out_half.shape[1]
    sequence = inputs[0]
    batch_size, length, _ = sequence.shape
    half = batch_size // 2

    def traded(block):
        kept = jnp.where(on_encoder, block[:half], block[half:])
        other = swapped(jnp.where(on_encoder, block[half:], block[:half]))
        return jnp.where(on_encoder, kept, other), jnp.where(on_encoder, other, kept)

    def returned(from_encoder, from_decoder):
        kept = jnp.where(on_encoder, from_encoder, from_decoder)
        other = swapped(jnp.where(on_encoder, from_decoder, from_encoder))
        return jnp.where(
            on_encoder,
            jnp.concatenate([kept, other], 0),
            jnp.concatenate([other, kept], 0),
        )

    frames, labels = traded(counts[0])
    label_mask = (
        lax.broadcasted_iota(jnp.int32, (half, length), 1) < labels[:, None]
    ).astype(f32)
    grad_low, grad_high = traded(cotangent)
    grad_logits = jnp.concatenate([grad_low, grad_high], -1) * label_mask[:, :, None].astype(low)
    grad_logits = grad_logits.reshape(half * length, -1)
    pull = contract(grad_logits, out_full, 1, 1)

    raw_values = sequence.astype(f32)
    norm_gain = vectors[4, :model_width]
    center = raw_values - jnp.mean(raw_values, -1, keepdims=True)
    spread = lax.rsqrt(jnp.mean(center * center, -1, keepdims=True) + NORM_EPS)
    scaled = center * spread
    normed = jnp.where(
        on_encoder, scaled * norm_gain + vectors[4, model_width:], raw_values
    ).astype(low)
    bias_here = lax.dynamic_slice_in_dim(vectors, 2 * section_index, 2, 0).reshape(1, -1)
    x_rows = slot_major(normed)
    act, cell, h_rows = lstm_forward(x_rows, weight, bias_here)
    states = utt_major(h_rows, batch_size)
    result = jnp.where(on_encoder, raw_values + states.astype(f32), states.astype(f32)).astype(low)
    memory, decoded = traded(result)
    decoded = decoded.reshape(-1, model_width)
    memory = memory.reshape(-1, model_width)
    squashed, context, dz, dq, dk, ddec, dmem, vec_rows = attention(
        frames, labels, decoded, memory, mats_full, vectors, pull
    )
    vocab = 2 * vocab_half
    logits = (
        jnp.dot(squashed, out_full, preferred_element_type=f32)
        + vectors[7, model_width : model_width + vocab]
    ).astype(low)
    logits = logits.reshape(half, length, vocab)
    logits = returned(logits[..., :vocab_half], logits[..., vocab_half:])
    out_grad = contract(squashed, grad_logits, 0, 0)
    out_bias_grad = jnp.sum(grad_logits, 0, dtype=f32)
    mats_grad = jnp.stack(
        [
            contract(decoded, dq, 0, 0),
            contract(memory, dk, 0, 0),
            jnp.concatenate([contract(dz, decoded, 0, 0), contract(dz, context, 0, 0)], 1),
        ]
    )
    outer = returned(dmem, ddec.astype(low)).reshape(batch_size, length, model_width)
    outer = outer.astype(f32)
    weight_t = jnp.swapaxes(weight[model_width:], 0, 1)
    dpre = lstm_backward(act, cell, slot_major(outer), weight_t)
    h_before = jnp.concatenate([jnp.zeros_like(h_rows[:ROWS]), h_rows[:-ROWS]], 0)
    weight_grad = jnp.concatenate([contract(x_rows, dpre, 0, 0), contract(h_before, dpre, 0, 0)], 0)
    bias_grad = jnp.sum(dpre, 0, dtype=f32)
    input_grad = utt_major(contract(dpre, weight[:model_width], 1, 1), batch_size)
    gain_grad = jnp.sum(input_grad * scaled, (0, 1))
    shift_grad_norm = jnp.sum(input_grad, (0, 1))
    scaled_grad = input_grad * norm_gain
    norm_back = spread * (
        scaled_grad
        - jnp.mean(scaled_grad, -1, keepdims=True)
        - scaled * jnp.mean(scaled_grad * scaled, -1, keepdims=True)
    )
    inputs_grad = jnp.where(on_encoder, norm_back + outer, input_grad)
    lstm_rows = lax.dynamic_update_slice(
        jnp.zeros((4, 2 * model_width), f32), bias_grad.reshape(2, -1), (2 * section_index, 0)
    )
    norm_row = jnp.where(on_encoder, jnp.concatenate([gain_grad, shift_grad_norm]), 0.0)
    logit_row = jnp.pad(out_bias_grad, (model_width, model_width - vocab))
    vector_grad = jnp.concatenate(
        [lstm_rows, norm_row[None], vec_rows[5:7], (vec_rows[7] + logit_row)[None]], 0
    )
    out_grad = out_grad.reshape(model_width, 2, vocab_half)
    lstm_sum = lax.psum_scatter(
        weight_grad.astype(low)[None], "dp", scatter_dimension=1, tiled=True
    ).astype(f32)
    out_sum = lax.psum_scatter(
        jnp.swapaxes(out_grad, 0, 1).astype(low), "section", scatter_dimension=0, tiled=True
    )[0]
    out_sum = lax.psum_scatter(out_sum, "dp", scatter_dimension=0, tiled=True).astype(f32)
    mats_sum = lax.psum_scatter(
        mats_grad.astype(low), ("section", "dp"), scatter_dimension=2, tiled=True
    ).astype(f32)
    vector_sum = lax.psum_scatter(vector_grad, ("section", "dp"), scatter_dimension=1, tiled=True)
    lstm_new, lstm_first_new, lstm_second_new = adamw(
        lstm_master, lstm_first, lstm_second, lstm_sum, RATE_LSTM
    )
    mats_new, mats_first_new, mats_second_new = adamw(
        mats_master, mats_first, mats_second, mats_sum, RATE_MATRIX
    )
    out_new, out_first_new, out_second_new = adamw(
        out_master, out_first, out_second, out_sum, RATE_MATRIX
    )
    vec_new, vec_first_new, vec_second_new = adamw(
        vec_master, vec_first, vec_second, vector_sum, RATE_VECTOR
    )
    return (
        logits,
        inputs_grad[None],
        lstm_new,
        lstm_first_new,
        lstm_second_new,
        lstm_new.astype(low),
        mats_new,
        mats_first_new,
        mats_second_new,
        mats_new.astype(low),
        out_new,
        out_first_new,
        out_second_new,
        out_new.astype(low),
        vec_new,
        vec_first_new,
        vec_second_new,
    )


def solution(mesh):
    lstm = P("section", "dp", None)
    mats = P(None, None, ("section", "dp"))
    out = P("dp", "section")
    vec = P(None, ("section", "dp"))
    logits = P("dp", None, "section")
    rows = P("section", "dp", None, None)
    return jax.shard_map(
        local,
        mesh=mesh,
        in_specs=(rows, P("section", "dp"), logits) + (lstm,) * 4 + (mats,) * 4 + (out,) * 4 + (vec,) * 3,
        out_specs=(logits, rows) + (lstm,) * 4 + (mats,) * 4 + (out,) * 4 + (vec,) * 3,
        check_vma=False,
    )
```

```python
import functools
import jax
import jax.numpy as jnp
from jax import lax
from jax.experimental import pallas as pl
from jax.experimental.pallas import tpu as pltpu
from jax.sharding import PartitionSpec as P

ROWS = 16
LANES = 128
ENERGY_OFFSET = -4.0
VMEM_SPEC = pl.BlockSpec(memory_space=pltpu.VMEM)
SMEM_SPEC = pl.BlockSpec(memory_space=pltpu.SMEM)
VMEM_LIMIT = 60 * 1024 * 1024


def contract(left, right, left_dim, right_dim):
    return lax.dot_general(
        left, right, (((left_dim,), (right_dim,)), ((), ())), preferred_element_type=jnp.float32
    )


def attention_kernel(
    frames_ref,
    mask_ref,
    dec_ref,
    mem_ref,
    mats_ref,
    vec_ref,
    out_ref,
    bias_ref,
    gl_ref,
    squash_ref,
    context_ref,
    dz_ref,
    dq_ref,
    dk_ref,
    ddec_ref,
    dmem_ref,
    dvec_ref,
    logits_ref,
    gsum_ref,
    q_s,
    k_s,
    mem_s,
    ctx_s,
    dqa_s,
    dka_s,
    e_s,
    sel_s,
    prob_s,
    pow_s,
    w_s,
    a_s,
    own_s,
    nxt_s,
    g_s,
    d_s,
    bc_s,
):
    rows, width = dec_ref.shape
    utts = frames_ref.shape[0]
    length = rows // utts
    low = jnp.bfloat16
    f32 = jnp.float32
    lane = lax.broadcasted_iota(jnp.int32, (length, LANES), 1)
    lane_block = lax.broadcasted_iota(jnp.int32, (length, 8, LANES), 2)

    q_s[...] = contract(dec_ref[...], mats_ref[0], 1, 1) + vec_ref[5:6]
    k_s[...] = contract(mem_ref[...], mats_ref[1], 1, 1)
    mem_s[...] = mem_ref[...].astype(f32)
    e_s[...] = jnp.zeros_like(e_s)
    d_s[...] = jnp.zeros_like(d_s)

    tile = 256
    group = 4

    for u in range(utts):
        at = u * length

        def energy_step(block, sums, at=at):
            base = block * group
            for offset in range(group):
                j = base + offset
                row = k_s[pl.ds(at + j, 1), :]
                for head in range(2):
                    total = jnp.zeros((length, LANES), f32)
                    for c in range(width // LANES):
                        columns = slice(head * width + c * LANES, head * width + (c + 1) * LANES)
                        total = total + jnp.tanh(
                            q_s[at : at + length, columns] + row[:, columns]
                        ) * vec_ref[6:7, columns]
                    value = jnp.sum(total, -1, keepdims=True)
                    sums = tuple(
                        jnp.where(lane == j, value, s) if h == head else s
                        for h, s in enumerate(sums)
                    )
            return sums

        blocks = (frames_ref[u] + (group - 1)) // group
        zero = jnp.zeros((length, LANES), f32)
        mono, window = lax.fori_loop(0, blocks, energy_step, (zero, zero))
        e_s[0, :, u, :] = mono
        e_s[1, :, u, :] = window

    mask = mask_ref[...][None]
    mono = e_s[0] + ENERGY_OFFSET
    window = e_s[1]
    chosen = jax.nn.sigmoid(mono)
    inside = (lane_block < length).astype(f32)
    sel_s[...] = chosen * mask
    leave = (jnp.maximum(mono, 0.0) + jnp.log1p(jnp.exp(-jnp.abs(mono)))) * mask
    prob = jnp.exp(-leave) * inside
    prob_s[...] = prob

    def right(value, distance):
        return pltpu.roll(value, distance, value.ndim - 1)

    def left(value, distance):
        return pltpu.roll(value, LANES - distance, value.ndim - 1)

    power = jnp.where(lane_block >= 1, right(prob, 1), 0.0) * inside
    for n in range(5):
        pow_s[n] = power
        if n < 4:
            power = jnp.where(lane_block >= 2 ** (n + 1), power * right(power, 2**n), 0.0)

    lane_row = lax.broadcasted_iota(jnp.int32, (8, LANES), 1)

    def align_step(i, before):
        total = before
        for n in range(5):
            total = total + pow_s[n, i] * right(total, 2**n)
        w_s[i] = total
        now = sel_s[i] * total
        a_s[i] = now
        return now

    lax.fori_loop(0, length, align_step, jnp.where(lane_row == 0, 1.0, 0.0).astype(f32))

    aligned = a_s[...]
    own = jnp.where(lane_block == 0, 1.0, jax.nn.sigmoid(window - right(window, 1)))
    nxt = jax.nn.sigmoid(window - left(window, 1))
    own_s[...] = own
    nxt_s[...] = nxt
    beta = aligned * own + jnp.where(lane_block < length - 1, left(aligned, 1), 0.0) * nxt
    g_s[...] = beta

    for u in range(utts):
        at = u * length
        weights = g_s[:, u, :].astype(low)[:, :length]
        ctx_s[at : at + length] = jnp.dot(
            weights, mem_s[at : at + length].astype(low), preferred_element_type=f32
        )
    context_ref[...] = ctx_s[...].astype(low)

    squash = jnp.tanh(
        jnp.dot(dec_ref[...], mats_ref[2, :width], preferred_element_type=f32)
        + jnp.dot(context_ref[...], mats_ref[2, width:], preferred_element_type=f32)
        + vec_ref[7:8, :width]
    )
    squash_ref[...] = squash.astype(low)
    pull = contract(gl_ref[0], out_ref[0], 1, 1) + contract(gl_ref[1], out_ref[1], 1, 1)
    dz = (pull * (1.0 - squash * squash)).astype(low)
    dz_ref[...] = dz
    dvec_ref[...] = jnp.zeros_like(dvec_ref)
    dvec_ref[7:8, :width] = jnp.sum(dz.astype(f32), 0, keepdims=True)
    for h in range(2):
        logits_ref[h] = (
            jnp.dot(squash_ref[...], out_ref[h], preferred_element_type=f32) + bias_ref[h : h + 1]
        ).astype(low)
        gsum_ref[h : h + 1] = jnp.sum(gl_ref[h].astype(f32), 0, keepdims=True)
    ddec_ref[...] = contract(dz, mats_ref[2, :width], 1, 1)
    ctx_s[...] = contract(dz, mats_ref[2, width:], 1, 1).astype(low).astype(f32)

    pad = jnp.zeros((length, LANES - length), f32)
    for u in range(utts):
        at = u * length
        weights = g_s[:, u, :].astype(low)[:, :length]
        pulled = ctx_s[at : at + length].astype(low)
        beta_grad = contract(pulled, mem_s[at : at + length].astype(low), 1, 1)
        e_s[0, :, u, :] = jnp.concatenate([beta_grad, pad], -1)
        mem_s[at : at + length] = contract(weights, pulled, 0, 0)

    beta_grad = e_s[0]
    own = own_s[...]
    nxt = nxt_s[...]
    g_s[...] = beta_grad * own + jnp.where(lane_block >= 1, right(beta_grad * nxt, 1), 0.0)
    aligned = a_s[...]
    from_own = jnp.where(lane_block >= 1, beta_grad * aligned * own * (1.0 - own), 0.0)
    from_next = (
        beta_grad
        * jnp.where(lane_block < length - 1, left(aligned, 1), 0.0)
        * nxt
        * (1.0 - nxt)
    )
    d_s[1] = (from_own - left(from_own, 1) + from_next - right(from_next, 1)) * inside

    prob = prob_s[...]
    power = jnp.where(lane_block < length - 1, prob, 0.0)
    for n in range(5):
        pow_s[n] = power
        if n < 4:
            power = power * left(power, 2**n)

    def retreat_step(k, after):
        i = length - 1 - k
        grad_align = g_s[i] + after
        e_s[0, i] = grad_align
        total = sel_s[i] * grad_align
        for n in range(5):
            total = total + pow_s[n, i] * left(total, 2**n)
        e_s[1, i] = total
        return total

    lax.fori_loop(0, length, retreat_step, jnp.zeros((8, LANES), f32))
    reached = w_s[...]
    grad_select = reached * e_s[0]
    grad_prob = reached * jnp.where(lane_block < length - 1, left(e_s[1], 1), 0.0)
    chosen = sel_s[...]
    d_s[0] = grad_select * chosen * (1.0 - chosen) - grad_prob * prob * chosen

    dka_s[...] = jnp.zeros_like(dka_s)

    def energy_back(u, dvec):
        at = pl.multiple_of(u * length, 8)
        for head in range(2):
            grads = d_s[head, :, pl.ds(u, 1), :].reshape(length, LANES)
            for j in range(length):
                bc_s[head, j] = jnp.broadcast_to(grads[:, j : j + 1], (length, LANES))
        count = (frames_ref[u] + 1) // 2
        for c in range(2 * width // tile):
            columns = slice(c * tile, (c + 1) * tile)
            head = c * tile // width
            q_now = q_s[pl.ds(at, length), columns]

            def back_step(block, sums, head=head, columns=columns, q_now=q_now):
                dq, dw = sums
                for offset in range(2):
                    j = block * 2 + offset
                    squash_all = jnp.tanh(q_now + k_s[pl.ds(at + j, 1), columns])
                    grad = bc_s[head, j]
                    grad = jnp.concatenate([grad] * (tile // LANES), -1)
                    scaled = grad * squash_all
                    dw = dw + scaled
                    moved = grad - scaled * squash_all
                    dq = dq + moved
                    dka_s[pl.ds(at + j, 1), columns] = jnp.sum(moved, 0, keepdims=True)
                return (dq, dw)

            zero = jnp.zeros((length, tile), f32)
            dq, dw = lax.fori_loop(0, count, back_step, (zero, zero))
            dq = dq * vec_ref[6:7, columns]
            dqa_s[pl.ds(at, length), columns] = dq
            dvec_ref[5:6, columns] += jnp.sum(dq, 0, keepdims=True)
            dvec_ref[6:7, columns] += jnp.sum(dw, 0, keepdims=True)
        return dvec

    lax.fori_loop(0, utts, energy_back, 0)
    for h in range(2):
        columns = slice(h * width, (h + 1) * width)
        dq_ref[h] = dqa_s[:, columns].astype(low)
        dk_ref[h] = (dka_s[:, columns] * vec_ref[6:7, columns]).astype(low)
        ddec_ref[...] += jnp.dot(dq_ref[h], mats_ref[0, columns], preferred_element_type=f32)
        mem_s[...] += jnp.dot(dk_ref[h], mats_ref[1, columns], preferred_element_type=f32)
    dmem_ref[...] = mem_s[...].astype(low)


def attention(frames, decoded, memory, mats, vectors, outs, bias, gl):
    rows, width = decoded.shape
    utts = frames.shape[0]
    length = rows // utts
    lane = lax.broadcasted_iota(jnp.int32, (8, LANES), 1)
    padded = jnp.concatenate([frames, jnp.zeros((8 - utts,), frames.dtype)])
    mask = (lane < padded[:, None]).astype(jnp.float32)
    low, f32 = jnp.bfloat16, jnp.float32
    small = (length, 8, LANES)
    half_vocab = gl.shape[-1]
    return pl.pallas_call(
        attention_kernel,
        out_shape=(
            jax.ShapeDtypeStruct((rows, width), low),
            jax.ShapeDtypeStruct((rows, width), low),
            jax.ShapeDtypeStruct((rows, width), low),
            jax.ShapeDtypeStruct((2, rows, width), low),
            jax.ShapeDtypeStruct((2, rows, width), low),
            jax.ShapeDtypeStruct((rows, width), f32),
            jax.ShapeDtypeStruct((rows, width), low),
            jax.ShapeDtypeStruct((8, 2 * width), f32),
            jax.ShapeDtypeStruct((2, rows, half_vocab), low),
            jax.ShapeDtypeStruct((2, half_vocab), f32),
        ),
        in_specs=[SMEM_SPEC] + [VMEM_SPEC] * 8,
        out_specs=(VMEM_SPEC,) * 10,
        scratch_shapes=[
            pltpu.VMEM((rows, 2 * width), f32),
            pltpu.VMEM((rows, 2 * width), f32),
            pltpu.VMEM((rows, width), f32),
            pltpu.VMEM((rows, width), f32),
            pltpu.VMEM((rows, 2 * width), f32),
            pltpu.VMEM((rows, 2 * width), f32),
            pltpu.VMEM((2,) + small, f32),
            pltpu.VMEM(small, f32),
            pltpu.VMEM(small, f32),
            pltpu.VMEM((5,) + small, f32),
            pltpu.VMEM(small, f32),
            pltpu.VMEM(small, f32),
            pltpu.VMEM(small, f32),
            pltpu.VMEM(small, f32),
            pltpu.VMEM(small, f32),
            pltpu.VMEM((2,) + small, f32),
            pltpu.VMEM((2, length, length, LANES), f32),
        ],
        compiler_params=pltpu.CompilerParams(vmem_limit_bytes=VMEM_LIMIT),
    )(frames, mask, decoded, memory, mats, vectors, outs, bias, gl)


MESH_ID = pl.DeviceIdType.MESH
ANY_SPEC = pl.BlockSpec(memory_space=pl.ANY)
DP_LAYOUTS = {16: (4, 2, 1, 2), 128: (8, 4, 1, 32)}
LINE_STRIDE = 4


def flipped(value, k):
    result = value
    bit = 1
    while bit <= k:
        if k & bit:
            result = result + bit - 2 * bit * lax.rem(value // bit, 2)
        bit *= 2
    return result


class Place:
    def __init__(self, n_dp):
        self.line, self.side, stride_a, stride_b = DP_LAYOUTS[n_dp]
        self.core = lax.axis_index("section")
        self.chip = lax.axis_index("dp")
        self.z = lax.rem(self.chip // LINE_STRIDE, self.line)
        at_a = lax.rem(self.chip // stride_a, self.side)
        at_b = lax.rem(self.chip // stride_b, self.side)
        self.role = lax.rem(self.z, 2)
        moves_a = [(flipped(at_a, k) - at_a) * stride_a for k in range(self.side)]
        moves_b = [(flipped(at_b, k) - at_b) * stride_b for k in range(self.side)]
        core = self.core
        self.first = [a + (b - a) * core for a, b in zip(moves_a, moves_b)]
        self.second = [b + (a - b) * core for a, b in zip(moves_a, moves_b)]
        self.along = [(flipped(self.z, k) - self.z) * LINE_STRIDE for k in range(self.line)]

    def block(self, kz, kf=0, kg=0):
        return self.chip + self.along[kz] + self.first[kf] + self.second[kg]

    def other_block(self, kz, kf=0, kg=0):
        return self.chip + self.along[kz] + self.second[kf] + self.first[kg]

    def greet(self):
        barrier = pltpu.get_barrier_semaphore()
        peers = [(1 - self.core, self.chip)]
        for k in range(1, self.line):
            peers += [(0, self.chip + self.along[k]), (1, self.chip + self.along[k])]
        for k in range(1, self.side):
            peers += [(self.core, self.chip + self.first[k]), (self.core, self.chip + self.second[k])]
        for peer in peers:
            pl.semaphore_signal(barrier, inc=1, device_id=peer, device_id_type=MESH_ID)
        pl.semaphore_wait(barrier, len(peers))


def remote(source, target, send, receive, device):
    return pltpu.make_async_remote_copy(
        src_ref=source,
        dst_ref=target,
        send_sem=send,
        recv_sem=receive,
        device_id=device,
        device_id_type=MESH_ID,
    )


class Spread:
    def __init__(self, place, here, there, sems):
        self.place, self.here, self.there, self.sems = place, here, there, sems
        self.sent = []

    def send(self, target, device, send, receive):
        copy = remote(target, target, send, receive, device)
        copy.start()
        self.sent.append(copy)

    def arrived(self, target, semaphore):
        place = self.place
        remote(target, target, semaphore, semaphore, (1 - place.core, place.chip)).wait_recv()

    def to_second(self, kz, kf):
        place = self.place
        target = self.here(place.block(kz, kf))
        for kg in range(1, place.side):
            self.send(
                target,
                (place.core, place.chip + place.second[kg]),
                self.sems["gs"].at[kg, kf, kz],
                self.sems["gr"].at[kg, kf, kz],
            )

    def to_core(self, kz, kf, kg):
        place = self.place
        self.send(
            self.here(place.block(kz, kf, kg)),
            (1 - place.core, place.chip),
            self.sems["cs"].at[kg, kf, kz],
            self.sems["cr"].at[kg, kf, kz],
        )

    def stage_one(self, wait_line):
        place = self.place
        for kz in range(place.line):
            wait_line(kz)
            target = self.here(place.block(kz))
            for kf in range(1, place.side):
                self.send(
                    target,
                    (place.core, place.chip + place.first[kf]),
                    self.sems["fs"].at[kf, kz],
                    self.sems["fr"].at[kf, kz],
                )
            self.to_second(kz, 0)
            self.to_core(kz, 0, 0)

    def stage_two(self):
        place = self.place
        for kf in range(1, place.side):
            for kz in range(place.line):
                self.arrived(self.here(place.block(kz, kf)), self.sems["fr"].at[kf, kz])
                self.to_second(kz, kf)
                self.to_core(kz, kf, 0)

    def stage_three(self):
        place = self.place
        for kg in range(1, place.side):
            for kf in range(place.side):
                for kz in range(place.line):
                    self.arrived(self.here(place.block(kz, kf, kg)), self.sems["gr"].at[kg, kf, kz])
                    self.to_core(kz, kf, kg)

    def finish(self):
        place = self.place
        for kg in range(place.side):
            for kf in range(place.side):
                for kz in range(place.line):
                    self.arrived(self.there(place.other_block(kz, kf, kg)), self.sems["cr"].at[kg, kf, kz])

    def sent_all(self):
        for copy in self.sent:
            copy.wait_send()


def spread_sems(line, side):
    dma = pltpu.SemaphoreType.DMA
    return {
        "zs": dma((line, 2)),
        "zr": dma((line,)),
        "fs": dma((side, line)),
        "fr": dma((side, line)),
        "gs": dma((side, side, line)),
        "gr": dma((side, side, line)),
        "cs": dma((side, side, line)),
        "cr": dma((side, side, line)),
    }


def spread_even(place, source, at, sems):
    own = at(place.core, place.chip)
    spread = Spread(place, lambda block: at(place.core, block), lambda block: at(1 - place.core, block), sems)
    kept = pltpu.make_async_copy(source, own, sems["zr"].at[0])
    copies = [
        remote(source, own, sems["zs"].at[k, 0], sems["zr"].at[k], (place.core, place.chip + place.along[k]))
        for k in range(1, place.line)
    ]

    def begin():
        kept.start()
        for copy in copies:
            copy.start()
        spread.sent += copies

    def wait_line(kz):
        if kz == 0:
            kept.wait()
        else:
            spread.arrived(spread.here(place.block(kz)), sems["zr"].at[kz])

    spread.begin = begin
    spread.first_stage = lambda: spread.stage_one(wait_line)
    return spread


def spread_role(place, source, target, sems, rows, half):
    def columns(core):
        return pl.ds(pl.multiple_of(core * half, half), half)

    def at(block, core):
        return target.at[pl.ds(pl.multiple_of(block * rows, rows), rows), columns(core)]

    spread = Spread(
        place, lambda block: at(block, place.core), lambda block: at(block, 1 - place.core), sems
    )
    mine = place.role == place.core
    kept = pltpu.make_async_copy(source.at[:, columns(place.core)], at(place.chip, place.core), sems["zr"].at[0])
    cross = remote(
        source.at[:, columns(1 - place.core)],
        at(place.chip, 1 - place.core),
        sems["zs"].at[0, 0],
        sems["zr"].at[0],
        (1 - place.core, place.chip),
    )
    copies = [
        [
            remote(
                source.at[:, columns(core)],
                at(place.chip, core),
                sems["zs"].at[k, core],
                sems["zr"].at[k],
                (core, place.chip + place.along[k]),
            )
            for core in range(2)
        ]
        for k in range(1, place.line)
    ]

    def each(action):
        @pl.when(mine)
        def _():
            action(cross)
            for k in range(2, place.line, 2):
                for copy in copies[k - 1]:
                    action(copy)

        @pl.when(jnp.logical_not(mine))
        def _():
            for k in range(1, place.line, 2):
                for copy in copies[k - 1]:
                    action(copy)

    def begin():
        @pl.when(mine)
        def _():
            kept.start()

        each(lambda copy: copy.start())

    def wait_line(kz):
        if kz == 0:

            @pl.when(mine)
            def _():
                kept.wait()

            @pl.when(jnp.logical_not(mine))
            def _():
                spread.arrived(spread.here(place.chip), sems["zr"].at[0])

        else:
            spread.arrived(spread.here(place.block(kz)), sems["zr"].at[kz])

    def sent_line():
        each(lambda copy: copy.wait_send())

    spread.begin = begin
    spread.first_stage = lambda: spread.stage_one(wait_line)
    spread.sent_line = sent_line
    return spread


def forward_kernel(
    n_dp,
    base_ref,
    shard_ref,
    mats_ref,
    out_ref,
    vec_ref,
    act_ref,
    cell_ref,
    h_ref,
    x_ref,
    vectors_ref,
    w_out,
    mats_out,
    out_out,
    w_s,
    vec_s,
    state,
    keep_sem,
    sems_w,
    sems_m,
    sems_o,
    sems_v,
):
    width = base_ref.shape[1]
    steps = base_ref.shape[0] // ROWS
    place = Place(n_dp)
    place.greet()
    matrix = spread_role(place, shard_ref, w_s, sems_w, shard_ref.shape[0], 2 * width)
    mats = spread_even(place, mats_ref, lambda core, chip: mats_out.at[:, core, chip], sems_m)
    outs = spread_even(place, out_ref, lambda core, chip: out_out.at[core, chip], sems_o)
    vecs = spread_even(place, vec_ref, lambda core, chip: vec_s.at[core, chip], sems_v)
    state[...] = jnp.zeros_like(state)
    cell_ref[:ROWS] = jnp.zeros((ROWS, width), jnp.float32)
    vecs.begin()
    matrix.begin()
    matrix.first_stage()
    vecs.first_stage()
    matrix.stage_two()
    vecs.stage_two()
    matrix.stage_three()
    outs.begin()
    mats.begin()
    vecs.stage_three()
    vecs.finish()
    piece = 2 * width // (2 * n_dp)
    per_tile = LANES // piece
    for m in range(2 * width // LANES):
        tile = jnp.zeros((8, LANES), jnp.float32)
        for k in range(per_tile):
            index = m * per_tile + k
            block = vec_s[index // n_dp, index % n_dp]
            tile = tile + (pltpu.roll(block, k * piece, 1) if k else block)
        vectors_ref[:, m * LANES : (m + 1) * LANES] = tile
    encoder = place.role == 0
    gain = jnp.where(encoder, vectors_ref[4:5, :width], 1.0)
    shift = jnp.where(encoder, vectors_ref[4:5, width:], 0.0)
    x_ref[...] = (base_ref[...] * gain + shift).astype(jnp.bfloat16)
    matrix.finish()
    keep = pltpu.make_async_copy(w_s, w_out, keep_sem)
    keep.start()
    for q in range(4):
        columns = slice(q * width, (q + 1) * width)
        row = q // 2
        bias_columns = slice((q % 2) * width, (q % 2 + 1) * width)
        bias = jnp.where(
            encoder, vectors_ref[row : row + 1, bias_columns], vectors_ref[row + 2 : row + 3, bias_columns]
        )
        act_ref[:, columns] = (
            jnp.dot(x_ref[...], w_s[:width, columns], preferred_element_type=jnp.float32) + bias
        )

    def step(t, carry):
        rows = pl.ds(pl.multiple_of(t * ROWS, ROWS), ROWS)
        after = pl.ds(pl.multiple_of((t + 1) * ROWS, ROWS), ROWS)
        hidden = state[...]

        def gate(q):
            columns = slice(q * width, (q + 1) * width)
            return act_ref[rows, columns] + jnp.dot(
                hidden, w_s[width:, columns], preferred_element_type=jnp.float32
            )

        in_gate = jax.nn.sigmoid(gate(0))
        forget = jax.nn.sigmoid(gate(1))
        candidate = jnp.tanh(gate(2))
        cell = forget * cell_ref[rows] + in_gate * candidate
        out_gate = jax.nn.sigmoid(gate(3))
        hidden_new = (out_gate * jnp.tanh(cell)).astype(jnp.bfloat16)
        act_ref[rows, :width] = in_gate
        act_ref[rows, width : 2 * width] = forget
        act_ref[rows, 2 * width : 3 * width] = candidate
        act_ref[rows, 3 * width :] = out_gate
        cell_ref[after] = cell
        h_ref[rows] = hidden_new
        state[...] = hidden_new
        return carry

    first, second = steps * 3 // 8, steps * 3 // 4
    outs.first_stage()
    mats.first_stage()
    lax.fori_loop(0, first, step, 0)
    outs.stage_two()
    mats.stage_two()
    lax.fori_loop(first, second, step, 0)
    outs.stage_three()
    lax.fori_loop(second, steps, step, 0)
    mats.stage_three()
    outs.finish()
    mats.finish()
    keep.wait()
    matrix.sent_line()
    for spread in (matrix, vecs, outs, mats):
        spread.sent_all()


def forward(n_dp, base, shard, mats_block, out_block, vec_block):
    rows, width = base.shape
    low, f32 = jnp.bfloat16, jnp.float32
    line, side = DP_LAYOUTS[n_dp][:2]
    return pl.pallas_call(
        functools.partial(forward_kernel, n_dp),
        out_shape=(
            jax.ShapeDtypeStruct((rows, 4 * width), f32),
            jax.ShapeDtypeStruct((rows + ROWS, width), f32),
            jax.ShapeDtypeStruct((rows, width), low),
            jax.ShapeDtypeStruct((rows, width), low),
            jax.ShapeDtypeStruct((8, 2 * width), f32),
            jax.ShapeDtypeStruct((2 * width, 4 * width), low),
            jax.ShapeDtypeStruct((3, 2, n_dp) + mats_block.shape[1:], low),
            jax.ShapeDtypeStruct((2, n_dp) + out_block.shape, low),
        ),
        in_specs=[VMEM_SPEC, ANY_SPEC, ANY_SPEC, ANY_SPEC, VMEM_SPEC],
        out_specs=(VMEM_SPEC,) * 5 + (ANY_SPEC,) * 3,
        scratch_shapes=[
            pltpu.VMEM((2 * width, 4 * width), low),
            pltpu.VMEM((2, n_dp, 8, LANES), f32),
            pltpu.VMEM((ROWS, width), low),
            pltpu.SemaphoreType.DMA,
        ]
        + [spread_sems(line, side)] * 4,
        compiler_params=pltpu.CompilerParams(
            collective_id=1, has_side_effects=True, vmem_limit_bytes=VMEM_LIMIT
        ),
    )(base, shard, mats_block, out_block, vec_block)


class Fold:
    def __init__(self, place, part, stage, near, far, sems):
        self.place, self.part, self.stage, self.near, self.far, self.sems = place, part, stage, near, far, sems
        self.sent = []

    def send(self, source, target, device, send, receive):
        copy = remote(source, target, send, receive, device)
        copy.start()
        self.sent.append(copy)

    def arrived(self, target, semaphore):
        place = self.place
        remote(target, target, semaphore, semaphore, (1 - place.core, place.chip)).wait_recv()

    def stage_a(self):
        place = self.place
        for kg in range(1, place.side):
            for kf in reversed(range(place.side)):
                for kz in range(place.line):
                    source = self.stage.at[kg - 1, kf, kz]
                    source[...] = self.part(kz, kf, kg).astype(source.dtype)
                    self.send(
                        source,
                        self.near.at[kg - 1, kf, kz],
                        (place.core, place.chip + place.second[kg]),
                        self.sems["gs"].at[kg, kf, kz],
                        self.sems["gr"].at[kg, kf, kz],
                    )

    def stage_b(self):
        place = self.place
        for kf in reversed(range(place.side)):
            for kz in range(place.line):
                total = self.part(kz, kf, 0)
                for kg in range(1, place.side):
                    self.arrived(self.near.at[kg - 1, kf, kz], self.sems["gr"].at[kg, kf, kz])
                    total = total + self.near[kg - 1, kf, kz].astype(jnp.float32)
                source = self.near.at[0, kf, kz]
                source[...] = total.astype(source.dtype)
                if kf:
                    self.send(
                        source,
                        self.far.at[kf - 1, kz],
                        (place.core, place.chip + place.first[kf]),
                        self.sems["fs"].at[kf, kz],
                        self.sems["fr"].at[kf, kz],
                    )

    def summed(self, kz):
        place = self.place
        total = self.near[0, 0, kz].astype(jnp.float32)
        for kf in range(1, place.side):
            self.arrived(self.far.at[kf - 1, kz], self.sems["fr"].at[kf, kz])
            total = total + self.far[kf - 1, kz].astype(jnp.float32)
        source = self.far.at[0, kz]
        source[...] = total.astype(source.dtype)
        return source

    def sent_all(self):
        for copy in self.sent:
            copy.wait_send()


class FoldEven(Fold):
    def __init__(self, place, part, stage, near, far, end, sems):
        super().__init__(place, part, stage, near, far, sems)
        self.end = end

    def stage_c(self):
        place = self.place
        for kz in reversed(range(place.line)):
            source = self.summed(kz)
            if kz:
                self.send(
                    source,
                    self.end.at[kz - 1],
                    (place.core, place.chip + place.along[kz]),
                    self.sems["zs"].at[kz, 0],
                    self.sems["zr"].at[kz],
                )

    def result(self):
        place = self.place
        total = self.far[0, 0].astype(jnp.float32)
        for kz in range(1, place.line):
            self.arrived(self.end.at[kz - 1], self.sems["zr"].at[kz])
            total = total + self.end[kz - 1].astype(jnp.float32)
        return total


class FoldRole(Fold):
    def __init__(self, place, part, stage, near, far, end, sems):
        super().__init__(place, part, stage, near, far, sems)
        self.end = end

    def stage_c(self):
        place = self.place
        self.line_copies = []
        for kz in reversed(range(place.line)):
            source = self.summed(kz)
            if kz:
                copy = remote(
                    source,
                    self.end.at[place.core, kz],
                    self.sems["zs"].at[kz, 0],
                    self.sems["er"].at[place.core, kz],
                    (place.role, place.chip + place.along[kz]),
                )
                copy.start()
                self.sent.append(copy)
            else:
                self.last = source
                self.cross = remote(
                    source,
                    self.end.at[place.core, 0],
                    self.sems["zs"].at[0, 0],
                    self.sems["er"].at[place.core, 0],
                    (1 - place.core, place.chip),
                )

                @pl.when(place.core != place.role)
                def _():
                    self.cross.start()

    def result(self, sum_ref):
        place = self.place
        rows, half = self.end.shape[2:]
        mine = place.core == place.role

        def columns(core):
            return pl.ds(pl.multiple_of(core * half, half), half)

        def add(parity):
            sources = [kz for kz in range(place.line) if kz % 2 == parity]
            for core in range(2):
                total = jnp.zeros((rows, half), jnp.float32)
                for kz in sources:
                    if kz:
                        self.arrived(self.end.at[core, kz], self.sems["er"].at[core, kz])
                        total = total + self.end[core, kz].astype(jnp.float32)
                sum_ref[:, core * half : (core + 1) * half] = total

        @pl.when(mine)
        def _():
            add(0)
            own, other = columns(place.core), columns(1 - place.core)
            sum_ref[:, own] += self.last[...].astype(jnp.float32)
            self.arrived(self.end.at[1 - place.core, 0], self.sems["er"].at[1 - place.core, 0])
            sum_ref[:, other] += self.end[1 - place.core, 0].astype(jnp.float32)

        @pl.when(jnp.logical_not(mine))
        def _():
            add(1)
            self.cross.wait_send()


def fold_sems(line, side):
    dma = pltpu.SemaphoreType.DMA
    return {
        "gs": dma((side, side, line)),
        "gr": dma((side, side, line)),
        "fs": dma((side, line)),
        "fr": dma((side, line)),
        "zs": dma((line, 1)),
        "zr": dma((line,)),
        "er": dma((2, line)),
    }


def fold_buffers(line, side, shape, dtype):
    return [
        pltpu.VMEM((side - 1, side, line) + shape, dtype),
        pltpu.VMEM((side - 1, side, line) + shape, dtype),
        pltpu.VMEM((side - 1, line) + shape, dtype),
    ]


def backward_kernel(
    n_dp,
    act_ref,
    cell_ref,
    outer_ref,
    wt_ref,
    ht_ref,
    dq_ref,
    dk_ref,
    dec_ref,
    mem_ref,
    ctx_ref,
    dz_ref,
    sq_ref,
    gl_ref,
    dpre_ref,
    dpre_other,
    ht_other,
    mats_sum,
    out_sum,
    state,
    held,
    facts,
    facts_gl,
    g_mats,
    g_out,
    m_stage,
    m_near,
    m_far,
    m_end,
    o_stage,
    o_near,
    o_far,
    o_end,
    fact_sems,
    pre_sems,
    ht_sems,
    sems_m,
    sems_o,
):
    width = outer_ref.shape[1]
    steps = outer_ref.shape[0] // ROWS
    low, f32 = jnp.bfloat16, jnp.float32
    place = Place(n_dp)
    place.greet()
    core = place.core
    other = (1 - core, place.chip)
    sources = [dq_ref.at[1 - core], dk_ref.at[1 - core], dec_ref, mem_ref, ctx_ref, dz_ref, sq_ref]
    handed = [
        remote(source, facts.at[n], fact_sems.at[0, n], fact_sems.at[1, n], other)
        for n, source in enumerate(sources)
    ]
    handed.append(remote(gl_ref.at[1 - core], facts_gl, fact_sems.at[0, 7], fact_sems.at[1, 7], other))
    handed.append(remote(ht_ref, ht_other, ht_sems.at[0], ht_sems.at[1], other))
    for copy in handed:
        copy.start()
    state[...] = jnp.zeros_like(state)
    held[...] = jnp.zeros_like(held)

    def step(k, carry):
        t = steps - 1 - k
        rows = pl.ds(pl.multiple_of(t * ROWS, ROWS), ROWS)
        after = pl.ds(pl.multiple_of((t + 1) * ROWS, ROWS), ROWS)
        hidden_total = outer_ref[rows] + jnp.dot(
            state[...], wt_ref[...], preferred_element_type=f32
        )
        in_gate = act_ref[rows, :width]
        forget = act_ref[rows, width : 2 * width]
        candidate = act_ref[rows, 2 * width : 3 * width]
        out_gate = act_ref[rows, 3 * width :]
        squash = jnp.tanh(cell_ref[after])
        cell_total = held[...] + hidden_total * out_gate * (1.0 - squash * squash)
        held[...] = cell_total * forget
        grads = jnp.concatenate(
            [
                cell_total * candidate * in_gate * (1.0 - in_gate),
                cell_total * cell_ref[rows] * forget * (1.0 - forget),
                cell_total * in_gate * (1.0 - candidate * candidate),
                hidden_total * squash * out_gate * (1.0 - out_gate),
            ],
            -1,
        ).astype(low)
        state[...] = grads
        dpre_ref[rows] = grads
        return carry

    shares = 4
    share = steps // shares

    def hand_over(n):
        top = (steps - (n + 1) * share) * ROWS
        rows = slice(top, top + share * ROWS)
        columns = pl.ds(pl.multiple_of((1 - core) * 2 * width, 2 * width), 2 * width)
        copy = remote(
            dpre_ref.at[rows, columns], dpre_other.at[rows, :], pre_sems.at[0, n], pre_sems.at[1, n], other
        )
        copy.start()
        handed.append(copy)

    part_rows = g_mats.shape[1] // 3
    out_rows = g_out.shape[1]

    def matrices():
        for copy in handed[:8]:
            copy.wait_recv()
        joined = jnp.where(core == 0, dec_ref[...], ctx_ref[...])
        joined_other = jnp.where(core == 0, facts[2], facts[4])
        pairs = [
            (dq_ref[core], dec_ref[...], facts[0], facts[2]),
            (dk_ref[core], mem_ref[...], facts[1], facts[3]),
            (joined, dz_ref[...], joined_other, facts[5]),
        ]
        for m, (a, b, c, d) in enumerate(pairs):
            total = (contract(a, b, 0, 0) + contract(c, d, 0, 0)).astype(low)
            for block in range(n_dp):
                g_mats[block, m * part_rows : (m + 1) * part_rows] = total[
                    block * part_rows : (block + 1) * part_rows
                ]
        total = (contract(sq_ref[...], gl_ref[core], 0, 0) + contract(facts[6], facts_gl[...], 0, 0)).astype(low)
        for block in range(n_dp):
            g_out[block] = total[block * out_rows : (block + 1) * out_rows]

    mats = FoldEven(
        place, lambda kz, kf, kg: g_mats[place.block(kz, kf, kg)].astype(f32), m_stage, m_near, m_far, m_end, sems_m
    )
    outs = FoldEven(
        place, lambda kz, kf, kg: g_out[place.block(kz, kf, kg)].astype(f32), o_stage, o_near, o_far, o_end, sems_o
    )
    lax.fori_loop(0, share, step, 0)
    hand_over(0)
    matrices()
    mats.stage_a()
    outs.stage_a()
    lax.fori_loop(share, 2 * share, step, 0)
    hand_over(1)
    lax.fori_loop(2 * share, 3 * share, step, 0)
    hand_over(2)
    mats.stage_b()
    outs.stage_b()
    lax.fori_loop(3 * share, steps, step, 0)
    hand_over(3)
    mats.stage_c()
    outs.stage_c()
    mats_sum[...] = mats.result()
    out_sum[...] = outs.result()
    for copy in handed[8:]:
        copy.wait_recv()
    for copy in handed:
        copy.wait_send()
    mats.sent_all()
    outs.sent_all()


def backward(n_dp, act, cell, outer, weight_t, ht, facts):
    rows, width = outer.shape
    low, f32 = jnp.bfloat16, jnp.float32
    line, side = DP_LAYOUTS[n_dp][:2]
    utt_rows = facts[2].shape[0]
    half_vocab = facts[-1].shape[-1]
    mats_block = (3 * width // n_dp, width)
    out_block = (width // n_dp, half_vocab)
    dma = pltpu.SemaphoreType.DMA
    return pl.pallas_call(
        functools.partial(backward_kernel, n_dp),
        out_shape=(
            jax.ShapeDtypeStruct((rows, 4 * width), low),
            jax.ShapeDtypeStruct((rows, 2 * width), low),
            jax.ShapeDtypeStruct(ht.shape, low),
            jax.ShapeDtypeStruct(mats_block, f32),
            jax.ShapeDtypeStruct(out_block, f32),
        ),
        in_specs=[VMEM_SPEC] * 4 + [ANY_SPEC] + [VMEM_SPEC] * 8,
        out_specs=(VMEM_SPEC, VMEM_SPEC, ANY_SPEC, VMEM_SPEC, VMEM_SPEC),
        scratch_shapes=[
            pltpu.VMEM((ROWS, 4 * width), low),
            pltpu.VMEM((ROWS, width), f32),
            pltpu.VMEM((7, utt_rows, width), low),
            pltpu.VMEM((utt_rows, half_vocab), low),
            pltpu.VMEM((n_dp,) + mats_block, low),
            pltpu.VMEM((n_dp,) + out_block, low),
        ]
        + fold_buffers(line, side, mats_block, low)
        + [pltpu.VMEM((line - 1,) + mats_block, low)]
        + fold_buffers(line, side, out_block, low)
        + [pltpu.VMEM((line - 1,) + out_block, low)]
        + [dma((2, 8)), dma((2, 4)), dma((2,))]
        + [fold_sems(line, side)] * 2,
        compiler_params=pltpu.CompilerParams(
            collective_id=2, has_side_effects=True, vmem_limit_bytes=VMEM_LIMIT
        ),
    )(act, cell, outer, weight_t, ht, *facts)


def update_kernel(
    n_dp,
    batch,
    ht_ref,
    ht_other,
    dpre_ref,
    dpre_other,
    w_ref,
    base_ref,
    spread_ref,
    outer_ref,
    vectors_ref,
    dvec_ref,
    sum_ref,
    gin_ref,
    vec_sum,
    w_s,
    gin_s,
    gin_u,
    vec_s,
    vec_other,
    vec_parts,
    l_stage,
    l_near,
    l_far,
    l_end,
    v_stage,
    v_near,
    v_far,
    v_end,
    w_sem,
    gin_sems,
    vec_sems,
    sems_l,
    sems_v,
):
    width = base_ref.shape[1]
    steps = base_ref.shape[0] // ROWS
    low, f32 = jnp.bfloat16, jnp.float32
    place = Place(n_dp)
    load = pltpu.make_async_copy(w_ref.at[:width], w_s, w_sem)
    load.start()
    place.greet()
    core = place.core
    encoder = place.role == 0
    mine = core == place.role
    block_rows = sum_ref.shape[0]
    half = pl.ds(pl.multiple_of(core * 2 * width, 2 * width), 2 * width)

    def part(kz, kf, kg):
        rows = pl.ds(pl.multiple_of(place.block(kz, kf, kg) * block_rows, block_rows), block_rows)
        return jnp.dot(ht_ref[rows], dpre_ref[:, half], preferred_element_type=f32) + jnp.dot(
            ht_other[rows], dpre_other[...], preferred_element_type=f32
        )

    matrix = FoldRole(place, part, l_stage, l_near, l_far, l_end, sems_l)
    matrix.stage_a()

    load.wait()
    gin_s[...] = contract(dpre_ref[...], w_s[...], 1, 1)
    input_grad = gin_s[...]
    scaled = base_ref[...]
    vec_s[...] = dvec_ref[...]
    vec_s[4:5, :width] = jnp.where(encoder, jnp.sum(input_grad * scaled, 0, keepdims=True), 0.0)
    vec_s[4:5, width:] = jnp.where(encoder, jnp.sum(input_grad, 0, keepdims=True), 0.0)
    for q in range(4):
        columns = slice((q % 2) * width, (q % 2 + 1) * width)
        bias = jnp.sum(dpre_ref[:, q * width : (q + 1) * width].astype(f32), 0, keepdims=True)
        for role in range(2):
            row = 2 * role + q // 2
            vec_s[row : row + 1, columns] = jnp.where(place.role == role, bias, 0.0)

    @pl.when(encoder)
    def _():
        grads = gin_s[...] * vectors_ref[4:5, :width]
        values = base_ref[...]
        gin_s[...] = (
            spread_ref[...]
            * (
                grads
                - jnp.mean(grads, -1, keepdims=True)
                - values * jnp.mean(grads * values, -1, keepdims=True)
            )
            + outer_ref[...]
        )

    turned = gin_s[...].reshape(steps, ROWS, width)
    for u in range(batch):
        gin_u[u] = turned[:, u, :]
    kept = pltpu.make_async_copy(gin_u, gin_ref, gin_sems.at[0])
    handed = remote(gin_u, gin_ref, gin_sems.at[1], gin_sems.at[2], (1 - core, place.chip + place.along[1]))

    @pl.when(mine)
    def _():
        kept.start()

    @pl.when(jnp.logical_not(mine))
    def _():
        handed.start()

    own_half = pl.ds(pl.multiple_of(core * width, width), width)
    other_half = pl.ds(pl.multiple_of((1 - core) * width, width), width)
    trade = remote(
        vec_s.at[:, other_half], vec_other, vec_sems.at[0], vec_sems.at[1], (1 - core, place.chip)
    )
    trade.start()
    trade.wait_recv()
    total = vec_s[:, own_half] + vec_other[...]
    piece = width // n_dp
    per_tile = LANES // piece
    for block in range(n_dp):
        tile = total[:, (block // per_tile) * LANES : (block // per_tile + 1) * LANES]
        turn = (block % per_tile) * piece
        vec_parts[block] = pltpu.roll(tile, LANES - turn, 1) if turn else tile
    vecs = FoldEven(
        place, lambda kz, kf, kg: vec_parts[place.block(kz, kf, kg)], v_stage, v_near, v_far, v_end, sems_v
    )
    vecs.stage_a()
    matrix.stage_b()
    vecs.stage_b()
    matrix.stage_c()
    vecs.stage_c()
    matrix.result(sum_ref)
    vec_sum[...] = vecs.result()

    @pl.when(mine)
    def _():
        kept.wait()

    @pl.when(jnp.logical_not(mine))
    def _():
        handed.wait()

    trade.wait_send()
    matrix.sent_all()
    vecs.sent_all()


def update(n_dp, batch, ht, ht_other, dpre, dpre_other, weight, base, spread, outer, vectors, dvec):
    rows, width = base.shape
    steps = rows // ROWS
    low, f32 = jnp.bfloat16, jnp.float32
    line, side = DP_LAYOUTS[n_dp][:2]
    block_rows = 2 * width // n_dp
    block = (block_rows, 2 * width)
    dma = pltpu.SemaphoreType.DMA
    return pl.pallas_call(
        functools.partial(update_kernel, n_dp, batch),
        out_shape=(
            jax.ShapeDtypeStruct((block_rows, 4 * width), f32),
            jax.ShapeDtypeStruct((batch, steps, width), f32),
            jax.ShapeDtypeStruct((8, LANES), f32),
        ),
        in_specs=[VMEM_SPEC] * 4 + [ANY_SPEC] + [VMEM_SPEC] * 5,
        out_specs=(VMEM_SPEC, ANY_SPEC, VMEM_SPEC),
        scratch_shapes=[
            pltpu.VMEM((width, 4 * width), low),
            pltpu.VMEM((rows, width), f32),
            pltpu.VMEM((batch, steps, width), f32),
            pltpu.VMEM((8, 2 * width), f32),
            pltpu.VMEM((8, width), f32),
            pltpu.VMEM((n_dp, 8, LANES), f32),
        ]
        + fold_buffers(line, side, block, low)
        + [pltpu.VMEM((2, line) + block, low)]
        + fold_buffers(line, side, (8, LANES), f32)
        + [pltpu.VMEM((line - 1, 8, LANES), f32)]
        + [dma, dma((3,)), dma((2,))]
        + [fold_sems(line, side)] * 2,
        compiler_params=pltpu.CompilerParams(
            collective_id=3, has_side_effects=True, vmem_limit_bytes=VMEM_LIMIT
        ),
    )(ht, ht_other, dpre, dpre_other, weight, base, spread, outer, vectors, dvec)


STEP = 5
NORM_EPS = 1e-05
BETA_ONE = 0.9
BETA_TWO = 0.999
ADAM_EPS = 1e-08
WEIGHT_DECAY = 0.01
RATE_LSTM = 0.05
RATE_MATRIX = 0.02
RATE_VECTOR = 0.3
AXES = ("section", "dp")


def swapped(block):
    return lax.ppermute(block, "section", [(0, 1), (1, 0)])


def adamw(master, first, second, grad, rate):
    first_new = BETA_ONE * first + (1.0 - BETA_ONE) * grad
    second_new = BETA_TWO * second + (1.0 - BETA_TWO) * grad * grad
    first_hat = first_new / (1.0 - BETA_ONE**STEP)
    second_hat = second_new / (1.0 - BETA_TWO**STEP)
    master_new = master - rate * (
        first_hat / (jnp.sqrt(second_hat) + ADAM_EPS) + WEIGHT_DECAY * master
    )
    return (master_new, first_new, second_new)


def slot_major(block):
    batch_size, length, width = block.shape
    padded = jnp.pad(jnp.swapaxes(block, 0, 1), ((0, 0), (0, ROWS - batch_size), (0, 0)))
    return padded.reshape(length * ROWS, width)


def utt_major(block, batch_size):
    width = block.shape[-1]
    return jnp.swapaxes(block.reshape(-1, ROWS, width)[:, :batch_size], 0, 1)


def runner(chip, section, n_dp):
    if chip // LINE_STRIDE % 2 == section:
        return section * n_dp + chip
    return (1 - section) * n_dp + (chip ^ LINE_STRIDE)


def local(
    inputs,
    counts,
    cotangent,
    lstm_master,
    lstm_copy,
    lstm_first,
    lstm_second,
    mats_master,
    mats_copy,
    mats_first,
    mats_second,
    out_master,
    out_copy,
    out_first,
    out_second,
    vec_master,
    vec_first,
    vec_second,
):
    low, f32 = jnp.bfloat16, jnp.float32
    n_dp = lax.axis_size("dp")
    section_index = lax.axis_index("section")
    role = lax.rem(lax.axis_index("dp") // LINE_STRIDE, 2)
    on_first = section_index == 0
    as_encoder = role == 0
    at_home = section_index == role
    chips = range(n_dp)
    batch_size, length, model_width = inputs.shape[1:]
    half = batch_size // 2
    vocab_half = out_copy.shape[1]
    vocab_pad = -(-vocab_half // LANES) * LANES

    homes = [(s * n_dp + c, runner(c, s, n_dp)) for s in range(2) for c in chips]
    away = [pair for pair in homes if pair[0] != pair[1]]
    straight = [(runner(c, s, n_dp), s * n_dp + c) for s in range(2) for c in chips]
    crossed = [(runner(c, s, n_dp), (1 - s) * n_dp + c) for s in range(2) for c in chips]

    def traded(block):
        kept = jnp.where(on_first, block[:half], block[half:])
        other = swapped(jnp.where(on_first, block[half:], block[:half]))
        return jnp.where(on_first, kept, other), jnp.where(on_first, other, kept)

    def to_halves(block):
        low_half, high_half = block[:half], block[half:]
        one = lax.ppermute(jnp.where(as_encoder, low_half, high_half), AXES, straight)
        two = lax.ppermute(jnp.where(as_encoder, high_half, low_half), AXES, crossed)
        return jnp.where(on_first, one, two), jnp.where(on_first, two, one)

    def from_halves(from_encoder, from_decoder):
        one = lax.ppermute(
            jnp.where(on_first, from_encoder, from_decoder), AXES, [(b, a) for a, b in straight]
        )
        two = lax.ppermute(
            jnp.where(on_first, from_decoder, from_encoder), AXES, [(b, a) for a, b in crossed]
        )
        return jnp.where(
            as_encoder, jnp.concatenate([one, two], 0), jnp.concatenate([two, one], 0)
        )

    sequence = jnp.where(at_home, inputs[0], lax.ppermute(inputs[0], AXES, away))
    frames, labels = traded(counts[0])
    label_mask = lax.broadcasted_iota(jnp.int32, (half, length), 1) < labels[:, None]
    grad_low, grad_high = traded(cotangent)
    grad_logits = jnp.stack([grad_low, grad_high]) * label_mask[None, :, :, None].astype(low)
    grad_logits = jnp.pad(grad_logits, ((0, 0),) * 3 + ((0, vocab_pad - vocab_half),))
    grad_logits = grad_logits.reshape(2, half * length, vocab_pad)

    raw_values = sequence.astype(f32)
    center = raw_values - jnp.mean(raw_values, -1, keepdims=True)
    spread = lax.rsqrt(jnp.mean(center * center, -1, keepdims=True) + NORM_EPS)
    base = slot_major(jnp.where(as_encoder, center * spread, raw_values))
    spread = slot_major(spread)

    mats_block = jnp.swapaxes(mats_copy, 1, 2)
    out_block = jnp.pad(out_copy, ((0, 0), (0, vocab_pad - vocab_half)))
    piece = vec_master.shape[1]
    vec_block = jnp.pad(vec_master.astype(low).astype(f32), ((0, 0), (0, LANES - piece)))
    act, cell, h_rows, x_rows, vectors, weight, mats_full, out_full = forward(
        n_dp, base, lstm_copy[0], mats_block, out_block, vec_block
    )
    mats_full = mats_full.reshape(3, 2 * model_width, model_width)
    out_full = out_full.reshape(2, model_width, vocab_pad)

    states = utt_major(h_rows, batch_size).astype(f32)
    result = jnp.where(as_encoder, raw_values + states, states).astype(low)
    memory, decoded = to_halves(result)
    decoded = decoded.reshape(-1, model_width)
    memory = memory.reshape(-1, model_width)
    row = jnp.pad(vectors[7], (0, vocab_pad))
    bias = jnp.stack(
        [row[model_width + s * vocab_half : model_width + s * vocab_half + vocab_pad] for s in range(2)]
    )
    squashed, context, dz, dq, dk, ddec, dmem, vec_rows, logits, logit_sums = attention(
        frames, decoded, memory, mats_full, vectors, out_full, bias, grad_logits
    )
    logits = logits.reshape(2, half, length, vocab_pad)[..., :vocab_half]
    kept = jnp.where(on_first, logits[0], logits[1])
    other = swapped(jnp.where(on_first, logits[1], logits[0]))
    logits = jnp.concatenate([jnp.where(on_first, kept, other), jnp.where(on_first, other, kept)], 0)

    outer = from_halves(dmem, ddec.astype(low)).reshape(batch_size, length, model_width)
    outer = slot_major(outer).astype(f32)
    weight_t = jnp.swapaxes(weight[model_width:], 0, 1)
    h_before = jnp.concatenate([jnp.zeros_like(h_rows[:ROWS]), h_rows[:-ROWS]], 0)
    ht = jnp.concatenate([x_rows.T, h_before.T], 0)
    dpre, dpre_other, ht_other, mats_sum, out_sum = backward(
        n_dp, act, cell, outer, weight_t, ht, (dq, dk, decoded, memory, context, dz, squashed, grad_logits)
    )
    logit_row = jnp.concatenate(
        [
            jnp.zeros((model_width,), f32),
            logit_sums[0, :vocab_half],
            logit_sums[1, :vocab_half],
            jnp.zeros((model_width - 2 * vocab_half,), f32),
        ]
    )
    vec_rows = vec_rows + jnp.pad(logit_row[None], ((7, 0), (0, 0)))
    lstm_sum, inputs_grad, vec_sum = update(
        n_dp, batch_size, ht, ht_other, dpre, dpre_other, weight, base, spread, outer, vectors, vec_rows
    )
    mats_sum = jnp.swapaxes(mats_sum.reshape(3, -1, model_width), 1, 2)
    lstm_new, lstm_first_new, lstm_second_new = adamw(
        lstm_master, lstm_first, lstm_second, lstm_sum[None], RATE_LSTM
    )
    mats_new, mats_first_new, mats_second_new = adamw(
        mats_master, mats_first, mats_second, mats_sum, RATE_MATRIX
    )
    out_new, out_first_new, out_second_new = adamw(
        out_master, out_first, out_second, out_sum[:, :vocab_half], RATE_MATRIX
    )
    vec_new, vec_first_new, vec_second_new = adamw(
        vec_master, vec_first, vec_second, vec_sum[:, :piece], RATE_VECTOR
    )
    return (
        logits,
        inputs_grad[None],
        lstm_new,
        lstm_first_new,
        lstm_second_new,
        lstm_new.astype(low),
        mats_new,
        mats_first_new,
        mats_second_new,
        mats_new.astype(low),
        out_new,
        out_first_new,
        out_second_new,
        out_new.astype(low),
        vec_new,
        vec_first_new,
        vec_second_new,
    )


def solution(mesh):
    lstm = P("section", "dp", None)
    mats = P(None, None, ("section", "dp"))
    out = P("dp", "section")
    vec = P(None, ("section", "dp"))
    logits = P("dp", None, "section")
    rows = P("section", "dp", None, None)
    groups = (lstm,) * 4 + (mats,) * 4 + (out,) * 4 + (vec,) * 3
    return jax.shard_map(
        local,
        mesh=mesh,
        in_specs=(rows, P("section", "dp"), logits) + groups,
        out_specs=(logits, rows) + groups,
        check_vma=False,
    )
```

```python
import functools
import jax
import jax.numpy as jnp
from jax import lax
from jax.experimental import pallas as pl
from jax.experimental.pallas import tpu as pltpu
from jax.sharding import PartitionSpec as P

ROWS = 16
LANES = 128
ENERGY_OFFSET = -4.0
VMEM_SPEC = pl.BlockSpec(memory_space=pltpu.VMEM)
SMEM_SPEC = pl.BlockSpec(memory_space=pltpu.SMEM)
VMEM_LIMIT = 60 * 1024 * 1024


def contract(left, right, left_dim, right_dim):
    return lax.dot_general(
        left, right, (((left_dim,), (right_dim,)), ((), ())), preferred_element_type=jnp.float32
    )


def attention_kernel(
    frames_ref,
    mask_ref,
    dec_ref,
    mem_ref,
    mats_ref,
    vec_ref,
    out_ref,
    bias_ref,
    gl_ref,
    squash_ref,
    context_ref,
    dz_ref,
    dq_ref,
    dk_ref,
    ddec_ref,
    dmem_ref,
    dvec_ref,
    logits_ref,
    gsum_ref,
    q_s,
    k_s,
    mem_s,
    ctx_s,
    dqa_s,
    dka_s,
    e_s,
    sel_s,
    prob_s,
    pow_s,
    w_s,
    a_s,
    own_s,
    nxt_s,
    g_s,
    d_s,
    bc_s,
):
    rows, width = dec_ref.shape
    utts = frames_ref.shape[0]
    length = rows // utts
    low = jnp.bfloat16
    f32 = jnp.float32
    lane = lax.broadcasted_iota(jnp.int32, (length, LANES), 1)
    lane_block = lax.broadcasted_iota(jnp.int32, (length, 8, LANES), 2)

    q_s[...] = contract(dec_ref[...], mats_ref[0], 1, 1) + vec_ref[5:6]
    k_s[...] = contract(mem_ref[...], mats_ref[1], 1, 1)
    mem_s[...] = mem_ref[...].astype(f32)
    e_s[...] = jnp.zeros_like(e_s)
    d_s[...] = jnp.zeros_like(d_s)

    tile = 256
    group = 4

    for u in range(utts):
        at = u * length

        def energy_step(block, sums, at=at):
            base = block * group
            for offset in range(group):
                j = base + offset
                row = k_s[pl.ds(at + j, 1), :]
                for head in range(2):
                    total = jnp.zeros((length, LANES), f32)
                    for c in range(width // LANES):
                        columns = slice(head * width + c * LANES, head * width + (c + 1) * LANES)
                        total = total + jnp.tanh(
                            q_s[at : at + length, columns] + row[:, columns]
                        ) * vec_ref[6:7, columns]
                    value = jnp.sum(total, -1, keepdims=True)
                    sums = tuple(
                        jnp.where(lane == j, value, s) if h == head else s
                        for h, s in enumerate(sums)
                    )
            return sums

        blocks = (frames_ref[u] + (group - 1)) // group
        zero = jnp.zeros((length, LANES), f32)
        mono, window = lax.fori_loop(0, blocks, energy_step, (zero, zero))
        e_s[0, :, u, :] = mono
        e_s[1, :, u, :] = window

    mask = mask_ref[...][None]
    mono = e_s[0] + ENERGY_OFFSET
    window = e_s[1]
    chosen = jax.nn.sigmoid(mono)
    inside = (lane_block < length).astype(f32)
    sel_s[...] = chosen * mask
    leave = (jnp.maximum(mono, 0.0) + jnp.log1p(jnp.exp(-jnp.abs(mono)))) * mask
    prob = jnp.exp(-leave) * inside
    prob_s[...] = prob

    def right(value, distance):
        return pltpu.roll(value, distance, value.ndim - 1)

    def left(value, distance):
        return pltpu.roll(value, LANES - distance, value.ndim - 1)

    power = jnp.where(lane_block >= 1, right(prob, 1), 0.0) * inside
    for n in range(5):
        pow_s[n] = power
        if n < 4:
            power = jnp.where(lane_block >= 2 ** (n + 1), power * right(power, 2**n), 0.0)

    lane_row = lax.broadcasted_iota(jnp.int32, (8, LANES), 1)

    def align_step(i, before):
        total = before
        for n in range(5):
            total = total + pow_s[n, i] * right(total, 2**n)
        w_s[i] = total
        now = sel_s[i] * total
        a_s[i] = now
        return now

    lax.fori_loop(0, length, align_step, jnp.where(lane_row == 0, 1.0, 0.0).astype(f32))

    aligned = a_s[...]
    own = jnp.where(lane_block == 0, 1.0, jax.nn.sigmoid(window - right(window, 1)))
    nxt = jax.nn.sigmoid(window - left(window, 1))
    own_s[...] = own
    nxt_s[...] = nxt
    beta = aligned * own + jnp.where(lane_block < length - 1, left(aligned, 1), 0.0) * nxt
    g_s[...] = beta

    for u in range(utts):
        at = u * length
        weights = g_s[:, u, :].astype(low)[:, :length]
        ctx_s[at : at + length] = jnp.dot(
            weights, mem_s[at : at + length].astype(low), preferred_element_type=f32
        )
    context_ref[...] = ctx_s[...].astype(low)

    squash = jnp.tanh(
        jnp.dot(dec_ref[...], mats_ref[2, :width], preferred_element_type=f32)
        + jnp.dot(context_ref[...], mats_ref[2, width:], preferred_element_type=f32)
        + vec_ref[7:8, :width]
    )
    squash_ref[...] = squash.astype(low)
    pull = contract(gl_ref[0], out_ref[0], 1, 1) + contract(gl_ref[1], out_ref[1], 1, 1)
    dz = (pull * (1.0 - squash * squash)).astype(low)
    dz_ref[...] = dz
    dvec_ref[...] = jnp.zeros_like(dvec_ref)
    dvec_ref[7:8, :width] = jnp.sum(dz.astype(f32), 0, keepdims=True)
    for h in range(2):
        logits_ref[h] = (
            jnp.dot(squash_ref[...], out_ref[h], preferred_element_type=f32) + bias_ref[h : h + 1]
        ).astype(low)
        gsum_ref[h : h + 1] = jnp.sum(gl_ref[h].astype(f32), 0, keepdims=True)
    ddec_ref[...] = contract(dz, mats_ref[2, :width], 1, 1)
    ctx_s[...] = contract(dz, mats_ref[2, width:], 1, 1).astype(low).astype(f32)

    pad = jnp.zeros((length, LANES - length), f32)
    for u in range(utts):
        at = u * length
        weights = g_s[:, u, :].astype(low)[:, :length]
        pulled = ctx_s[at : at + length].astype(low)
        beta_grad = contract(pulled, mem_s[at : at + length].astype(low), 1, 1)
        e_s[0, :, u, :] = jnp.concatenate([beta_grad, pad], -1)
        mem_s[at : at + length] = contract(weights, pulled, 0, 0)

    beta_grad = e_s[0]
    own = own_s[...]
    nxt = nxt_s[...]
    g_s[...] = beta_grad * own + jnp.where(lane_block >= 1, right(beta_grad * nxt, 1), 0.0)
    aligned = a_s[...]
    from_own = jnp.where(lane_block >= 1, beta_grad * aligned * own * (1.0 - own), 0.0)
    from_next = (
        beta_grad
        * jnp.where(lane_block < length - 1, left(aligned, 1), 0.0)
        * nxt
        * (1.0 - nxt)
    )
    d_s[1] = (from_own - left(from_own, 1) + from_next - right(from_next, 1)) * inside

    prob = prob_s[...]
    power = jnp.where(lane_block < length - 1, prob, 0.0)
    for n in range(5):
        pow_s[n] = power
        if n < 4:
            power = power * left(power, 2**n)

    def retreat_step(k, after):
        i = length - 1 - k
        grad_align = g_s[i] + after
        e_s[0, i] = grad_align
        total = sel_s[i] * grad_align
        for n in range(5):
            total = total + pow_s[n, i] * left(total, 2**n)
        e_s[1, i] = total
        return total

    lax.fori_loop(0, length, retreat_step, jnp.zeros((8, LANES), f32))
    reached = w_s[...]
    grad_select = reached * e_s[0]
    grad_prob = reached * jnp.where(lane_block < length - 1, left(e_s[1], 1), 0.0)
    chosen = sel_s[...]
    d_s[0] = grad_select * chosen * (1.0 - chosen) - grad_prob * prob * chosen

    dka_s[...] = jnp.zeros_like(dka_s)

    def energy_back(u, dvec):
        at = pl.multiple_of(u * length, 8)
        for head in range(2):
            grads = d_s[head, :, pl.ds(u, 1), :].reshape(length, LANES)
            for j in range(length):
                bc_s[head, j] = jnp.broadcast_to(grads[:, j : j + 1], (length, LANES))
        count = (frames_ref[u] + 1) // 2
        for c in range(2 * width // tile):
            columns = slice(c * tile, (c + 1) * tile)
            head = c * tile // width
            q_now = q_s[pl.ds(at, length), columns]

            def back_step(block, sums, head=head, columns=columns, q_now=q_now):
                dq, dw = sums
                for offset in range(2):
                    j = block * 2 + offset
                    squash_all = jnp.tanh(q_now + k_s[pl.ds(at + j, 1), columns])
                    grad = bc_s[head, j]
                    grad = jnp.concatenate([grad] * (tile // LANES), -1)
                    scaled = grad * squash_all
                    dw = dw + scaled
                    moved = grad - scaled * squash_all
                    dq = dq + moved
                    dka_s[pl.ds(at + j, 1), columns] = jnp.sum(moved, 0, keepdims=True)
                return (dq, dw)

            zero = jnp.zeros((length, tile), f32)
            dq, dw = lax.fori_loop(0, count, back_step, (zero, zero))
            dq = dq * vec_ref[6:7, columns]
            dqa_s[pl.ds(at, length), columns] = dq
            dvec_ref[5:6, columns] += jnp.sum(dq, 0, keepdims=True)
            dvec_ref[6:7, columns] += jnp.sum(dw, 0, keepdims=True)
        return dvec

    lax.fori_loop(0, utts, energy_back, 0)
    for h in range(2):
        columns = slice(h * width, (h + 1) * width)
        dq_ref[h] = dqa_s[:, columns].astype(low)
        dk_ref[h] = (dka_s[:, columns] * vec_ref[6:7, columns]).astype(low)
        ddec_ref[...] += jnp.dot(dq_ref[h], mats_ref[0, columns], preferred_element_type=f32)
        mem_s[...] += jnp.dot(dk_ref[h], mats_ref[1, columns], preferred_element_type=f32)
    dmem_ref[...] = mem_s[...].astype(low)


def attention(frames, decoded, memory, mats, vectors, outs, bias, gl):
    rows, width = decoded.shape
    utts = frames.shape[0]
    length = rows // utts
    lane = lax.broadcasted_iota(jnp.int32, (8, LANES), 1)
    padded = jnp.concatenate([frames, jnp.zeros((8 - utts,), frames.dtype)])
    mask = (lane < padded[:, None]).astype(jnp.float32)
    low, f32 = jnp.bfloat16, jnp.float32
    small = (length, 8, LANES)
    half_vocab = gl.shape[-1]
    return pl.pallas_call(
        attention_kernel,
        out_shape=(
            jax.ShapeDtypeStruct((rows, width), low),
            jax.ShapeDtypeStruct((rows, width), low),
            jax.ShapeDtypeStruct((rows, width), low),
            jax.ShapeDtypeStruct((2, rows, width), low),
            jax.ShapeDtypeStruct((2, rows, width), low),
            jax.ShapeDtypeStruct((rows, width), f32),
            jax.ShapeDtypeStruct((rows, width), low),
            jax.ShapeDtypeStruct((8, 2 * width), f32),
            jax.ShapeDtypeStruct((2, rows, half_vocab), low),
            jax.ShapeDtypeStruct((2, half_vocab), f32),
        ),
        in_specs=[SMEM_SPEC] + [VMEM_SPEC] * 8,
        out_specs=(VMEM_SPEC,) * 10,
        scratch_shapes=[
            pltpu.VMEM((rows, 2 * width), f32),
            pltpu.VMEM((rows, 2 * width), f32),
            pltpu.VMEM((rows, width), f32),
            pltpu.VMEM((rows, width), f32),
            pltpu.VMEM((rows, 2 * width), f32),
            pltpu.VMEM((rows, 2 * width), f32),
            pltpu.VMEM((2,) + small, f32),
            pltpu.VMEM(small, f32),
            pltpu.VMEM(small, f32),
            pltpu.VMEM((5,) + small, f32),
            pltpu.VMEM(small, f32),
            pltpu.VMEM(small, f32),
            pltpu.VMEM(small, f32),
            pltpu.VMEM(small, f32),
            pltpu.VMEM(small, f32),
            pltpu.VMEM((2,) + small, f32),
            pltpu.VMEM((2, length, length, LANES), f32),
        ],
        compiler_params=pltpu.CompilerParams(vmem_limit_bytes=VMEM_LIMIT),
    )(frames, mask, decoded, memory, mats, vectors, outs, bias, gl)


MESH_ID = pl.DeviceIdType.MESH
ANY_SPEC = pl.BlockSpec(memory_space=pl.ANY)
DP_LAYOUTS = {16: (4, 2, 1, 2), 128: (8, 4, 1, 32)}
LINE_STRIDE = 4
TURN = 256


def flipped(value, k):
    result = value
    bit = 1
    while bit <= k:
        if k & bit:
            result = result + bit - 2 * bit * lax.rem(value // bit, 2)
        bit *= 2
    return result


class Place:
    def __init__(self, n_dp):
        self.line, self.side, stride_a, stride_b = DP_LAYOUTS[n_dp]
        self.core = lax.axis_index("section")
        self.chip = lax.axis_index("dp")
        self.z = lax.rem(self.chip // LINE_STRIDE, self.line)
        at_a = lax.rem(self.chip // stride_a, self.side)
        at_b = lax.rem(self.chip // stride_b, self.side)
        self.role = lax.rem(self.z, 2)
        moves_a = [(flipped(at_a, k) - at_a) * stride_a for k in range(self.side)]
        moves_b = [(flipped(at_b, k) - at_b) * stride_b for k in range(self.side)]
        core = self.core
        self.first = [a + (b - a) * core for a, b in zip(moves_a, moves_b)]
        self.second = [b + (a - b) * core for a, b in zip(moves_a, moves_b)]
        self.along = [(flipped(self.z, k) - self.z) * LINE_STRIDE for k in range(self.line)]

    def block(self, kz, kf=0, kg=0):
        return self.chip + self.along[kz] + self.first[kf] + self.second[kg]

    def other_block(self, kz, kf=0, kg=0):
        return self.chip + self.along[kz] + self.second[kf] + self.first[kg]

    def greet(self):
        barrier = pltpu.get_barrier_semaphore()
        peers = [(1 - self.core, self.chip)]
        for k in range(1, self.line):
            peers += [(0, self.chip + self.along[k]), (1, self.chip + self.along[k])]
        for k in range(1, self.side):
            peers += [(self.core, self.chip + self.first[k]), (self.core, self.chip + self.second[k])]
        for peer in peers:
            pl.semaphore_signal(barrier, inc=1, device_id=peer, device_id_type=MESH_ID)
        pl.semaphore_wait(barrier, len(peers))


def remote(source, target, send, receive, device):
    return pltpu.make_async_remote_copy(
        src_ref=source,
        dst_ref=target,
        send_sem=send,
        recv_sem=receive,
        device_id=device,
        device_id_type=MESH_ID,
    )


class Spread:
    def __init__(self, place, here, there, sems):
        self.place, self.here, self.there, self.sems = place, here, there, sems
        self.sent = []

    def send(self, target, device, send, receive):
        copy = remote(target, target, send, receive, device)
        copy.start()
        self.sent.append(copy)

    def arrived(self, target, semaphore):
        place = self.place
        remote(target, target, semaphore, semaphore, (1 - place.core, place.chip)).wait_recv()

    def to_second(self, kz, kf):
        place = self.place
        target = self.here(place.block(kz, kf))
        for kg in range(1, place.side):
            self.send(
                target,
                (place.core, place.chip + place.second[kg]),
                self.sems["gs"].at[kg, kf, kz],
                self.sems["gr"].at[kg, kf, kz],
            )

    def to_core(self, kz, kf, kg):
        place = self.place
        self.send(
            self.here(place.block(kz, kf, kg)),
            (1 - place.core, place.chip),
            self.sems["cs"].at[kg, kf, kz],
            self.sems["cr"].at[kg, kf, kz],
        )

    def stage_one(self, *steps):
        place = self.place
        for kz in steps or range(place.line):
            self.wait_line(kz)
            target = self.here(place.block(kz))
            for kf in range(1, place.side):
                self.send(
                    target,
                    (place.core, place.chip + place.first[kf]),
                    self.sems["fs"].at[kf, kz],
                    self.sems["fr"].at[kf, kz],
                )
            self.to_second(kz, 0)
            self.to_core(kz, 0, 0)

    def stage_two(self):
        place = self.place
        for kf in range(1, place.side):
            for kz in range(place.line):
                self.arrived(self.here(place.block(kz, kf)), self.sems["fr"].at[kf, kz])
                self.to_second(kz, kf)
                self.to_core(kz, kf, 0)

    def stage_three(self):
        place = self.place
        for kg in range(1, place.side):
            for kf in range(place.side):
                for kz in range(place.line):
                    self.arrived(self.here(place.block(kz, kf, kg)), self.sems["gr"].at[kg, kf, kz])
                    self.to_core(kz, kf, kg)

    def finish(self):
        place = self.place
        for kg in range(place.side):
            for kf in range(place.side):
                for kz in range(place.line):
                    self.arrived(self.there(place.other_block(kz, kf, kg)), self.sems["cr"].at[kg, kf, kz])

    def sent_all(self):
        for copy in self.sent:
            copy.wait_send()


def spread_sems(line, side):
    dma = pltpu.SemaphoreType.DMA
    return {
        "zs": dma((line, 2)),
        "zr": dma((line,)),
        "fs": dma((side, line)),
        "fr": dma((side, line)),
        "gs": dma((side, side, line)),
        "gr": dma((side, side, line)),
        "cs": dma((side, side, line)),
        "cr": dma((side, side, line)),
    }


def spread_even(place, source, at, sems):
    own = at(place.core, place.chip)
    spread = Spread(place, lambda block: at(place.core, block), lambda block: at(1 - place.core, block), sems)
    kept = pltpu.make_async_copy(source, own, sems["zr"].at[0])
    copies = [
        remote(source, own, sems["zs"].at[k, 0], sems["zr"].at[k], (place.core, place.chip + place.along[k]))
        for k in range(1, place.line)
    ]

    def begin():
        kept.start()
        for copy in copies:
            copy.start()
        spread.sent += copies

    def wait_line(kz):
        if kz == 0:
            kept.wait()
        else:
            spread.arrived(spread.here(place.block(kz)), sems["zr"].at[kz])

    spread.begin = begin
    spread.wait_line = wait_line
    return spread


def spread_role(place, source, target, sems, rows, half):
    def columns(core):
        return pl.ds(pl.multiple_of(core * half, half), half)

    def at(block, core):
        return target.at[pl.ds(pl.multiple_of(block * rows, rows), rows), columns(core)]

    spread = Spread(
        place, lambda block: at(block, place.core), lambda block: at(block, 1 - place.core), sems
    )
    mine = place.role == place.core
    kept = pltpu.make_async_copy(source.at[:, columns(place.core)], at(place.chip, place.core), sems["zr"].at[0])
    cross = remote(
        source.at[:, columns(1 - place.core)],
        at(place.chip, 1 - place.core),
        sems["zs"].at[0, 0],
        sems["zr"].at[0],
        (1 - place.core, place.chip),
    )
    copies = [
        [
            remote(
                source.at[:, columns(core)],
                at(place.chip, core),
                sems["zs"].at[k, core],
                sems["zr"].at[k],
                (core, place.chip + place.along[k]),
            )
            for core in range(2)
        ]
        for k in range(1, place.line)
    ]

    guest = jnp.logical_not(mine)

    def each(condition, steps, action):
        @pl.when(condition)
        def _():
            for k in steps:
                for copy in copies[k - 1] if k else [cross]:
                    action(copy)

    def start(copy):
        copy.start()

    def begin():
        @pl.when(mine)
        def _():
            kept.start()

        each(mine, range(0, place.line, 2), start)
        each(guest, range(1, place.line, 2), start)

    def wait_line(kz):
        if kz == 0:

            @pl.when(mine)
            def _():
                kept.wait()

            @pl.when(jnp.logical_not(mine))
            def _():
                spread.arrived(spread.here(place.chip), sems["zr"].at[0])

        else:
            spread.arrived(spread.here(place.block(kz)), sems["zr"].at[kz])

    def finished(copy):
        copy.wait_send()

    def sent_line():
        each(mine, range(0, place.line, 2), finished)
        each(guest, range(1, place.line, 2), finished)

    spread.begin = begin
    spread.wait_line = wait_line
    spread.sent_line = sent_line
    return spread


def forward_kernel(
    n_dp,
    base_ref,
    shard_ref,
    mats_ref,
    out_ref,
    vec_ref,
    act_ref,
    cell_ref,
    h_ref,
    x_ref,
    vectors_ref,
    w_out,
    wt_out,
    mats_out,
    out_out,
    w_s,
    wt_s,
    vec_s,
    state,
    keep_sem,
    sems_w,
    sems_m,
    sems_o,
    sems_v,
):
    width = base_ref.shape[1]
    steps = base_ref.shape[0] // ROWS
    place = Place(n_dp)
    place.greet()
    matrix = spread_role(place, shard_ref, w_s, sems_w, shard_ref.shape[0], 2 * width)
    mats = spread_even(place, mats_ref, lambda core, chip: mats_out.at[:, core, chip], sems_m)
    outs = spread_even(place, out_ref, lambda core, chip: out_out.at[core, chip], sems_o)
    vecs = spread_even(place, vec_ref, lambda core, chip: vec_s.at[core, chip], sems_v)
    state[...] = jnp.zeros_like(state)
    cell_ref[:ROWS] = jnp.zeros((ROWS, width), jnp.float32)
    vecs.begin()
    matrix.begin()
    matrix.stage_one()
    vecs.stage_one()
    outs.begin()
    mats.begin()
    matrix.stage_two()
    vecs.stage_two()
    outs.stage_one(0)
    mats.stage_one(0)
    matrix.stage_three()
    vecs.stage_three()
    vecs.finish()
    piece = 2 * width // (2 * n_dp)
    per_tile = LANES // piece
    for m in range(2 * width // LANES):
        tile = jnp.zeros((8, LANES), jnp.float32)
        for k in range(per_tile):
            index = m * per_tile + k
            block = vec_s[index // n_dp, index % n_dp]
            tile = tile + (pltpu.roll(block, k * piece, 1) if k else block)
        vectors_ref[:, m * LANES : (m + 1) * LANES] = tile
    encoder = place.role == 0
    gain = jnp.where(encoder, vectors_ref[4:5, :width], 1.0)
    shift = jnp.where(encoder, vectors_ref[4:5, width:], 0.0)
    x_ref[...] = (base_ref[...] * gain + shift).astype(jnp.bfloat16)
    matrix.finish()
    keep = pltpu.make_async_copy(w_s.at[:width], w_out, keep_sem.at[0])
    keep.start()
    for q in range(4):
        columns = slice(q * width, (q + 1) * width)
        row = q // 2
        bias_columns = slice((q % 2) * width, (q % 2 + 1) * width)
        bias = jnp.where(
            encoder, vectors_ref[row : row + 1, bias_columns], vectors_ref[row + 2 : row + 3, bias_columns]
        )
        act_ref[:, columns] = (
            jnp.dot(x_ref[...], w_s[:width, columns], preferred_element_type=jnp.float32) + bias
        )

    def step(t, carry):
        rows = pl.ds(pl.multiple_of(t * ROWS, ROWS), ROWS)
        after = pl.ds(pl.multiple_of((t + 1) * ROWS, ROWS), ROWS)
        hidden = state[...]

        def gate(q):
            columns = slice(q * width, (q + 1) * width)
            return act_ref[rows, columns] + jnp.dot(
                hidden, w_s[width:, columns], preferred_element_type=jnp.float32
            )

        in_gate = jax.nn.sigmoid(gate(0))
        forget = jax.nn.sigmoid(gate(1))
        candidate = jnp.tanh(gate(2))
        cell = forget * cell_ref[rows] + in_gate * candidate
        out_gate = jax.nn.sigmoid(gate(3))
        hidden_new = (out_gate * jnp.tanh(cell)).astype(jnp.bfloat16)
        act_ref[rows, :width] = in_gate
        act_ref[rows, width : 2 * width] = forget
        act_ref[rows, 2 * width : 3 * width] = candidate
        act_ref[rows, 3 * width :] = out_gate
        cell_ref[after] = cell
        h_ref[rows] = hidden_new
        state[...] = hidden_new
        return carry

    line_rest = range(1, place.line)
    marks = [steps * n // 24 for n in (0, 4, 10, 18, 24)]
    lax.fori_loop(marks[0], marks[1], step, 0)
    outs.stage_one(*line_rest)
    mats.stage_one(*line_rest)
    lax.fori_loop(marks[1], marks[2], step, 0)
    outs.stage_two()
    mats.stage_two()
    lax.fori_loop(marks[2], marks[3], step, 0)
    outs.stage_three()
    lax.fori_loop(marks[3], marks[4], step, 0)
    for q in range(4):
        for n in range(width // TURN):
            rows = slice(width + n * TURN, width + (n + 1) * TURN)
            wt_s[q, :, n * TURN : (n + 1) * TURN] = w_s[rows, q * width : (q + 1) * width].T
    keep_turned = pltpu.make_async_copy(wt_s, wt_out, keep_sem.at[1])
    keep_turned.start()
    mats.stage_three()
    outs.finish()
    mats.finish()
    keep_turned.wait()
    keep.wait()
    matrix.sent_line()
    for spread in (matrix, vecs, outs, mats):
        spread.sent_all()


def forward(n_dp, base, shard, mats_block, out_block, vec_block):
    rows, width = base.shape
    low, f32 = jnp.bfloat16, jnp.float32
    line, side = DP_LAYOUTS[n_dp][:2]
    return pl.pallas_call(
        functools.partial(forward_kernel, n_dp),
        out_shape=(
            jax.ShapeDtypeStruct((rows, 4 * width), f32),
            jax.ShapeDtypeStruct((rows + ROWS, width), f32),
            jax.ShapeDtypeStruct((rows, width), low),
            jax.ShapeDtypeStruct((rows, width), low),
            jax.ShapeDtypeStruct((8, 2 * width), f32),
            jax.ShapeDtypeStruct((width, 4 * width), low),
            jax.ShapeDtypeStruct((4, width, width), low),
            jax.ShapeDtypeStruct((3, 2, n_dp) + mats_block.shape[1:], low),
            jax.ShapeDtypeStruct((2, n_dp) + out_block.shape, low),
        ),
        in_specs=[VMEM_SPEC, ANY_SPEC, ANY_SPEC, ANY_SPEC, VMEM_SPEC],
        out_specs=(VMEM_SPEC,) * 5 + (ANY_SPEC,) * 4,
        scratch_shapes=[
            pltpu.VMEM((2 * width, 4 * width), low),
            pltpu.VMEM((4, width, width), low),
            pltpu.VMEM((2, n_dp, 8, LANES), f32),
            pltpu.VMEM((ROWS, width), low),
            pltpu.SemaphoreType.DMA((2,)),
        ]
        + [spread_sems(line, side)] * 4,
        compiler_params=pltpu.CompilerParams(
            collective_id=1, has_side_effects=True, vmem_limit_bytes=VMEM_LIMIT
        ),
    )(base, shard, mats_block, out_block, vec_block)


class Fold:
    def __init__(self, place, part, stage, near, far, sems):
        self.place, self.part, self.stage, self.near, self.far, self.sems = place, part, stage, near, far, sems
        self.sent = []

    def send(self, source, target, device, send, receive):
        copy = remote(source, target, send, receive, device)
        copy.start()
        self.sent.append(copy)

    def arrived(self, target, semaphore):
        place = self.place
        remote(target, target, semaphore, semaphore, (1 - place.core, place.chip)).wait_recv()

    def stage_a(self, *steps):
        place = self.place
        for kz in steps or reversed(range(place.line)):
            for kg in range(1, place.side):
                for kf in reversed(range(place.side)):
                    source = self.stage.at[kg - 1, kf, kz]
                    source[...] = self.part(kz, kf, kg).astype(source.dtype)
                    self.send(
                        source,
                        self.near.at[kg - 1, kf, kz],
                        (place.core, place.chip + place.second[kg]),
                        self.sems["gs"].at[kg, kf, kz],
                        self.sems["gr"].at[kg, kf, kz],
                    )

    def stage_b(self, *steps):
        place = self.place
        for kz in steps or reversed(range(place.line)):
            for kf in reversed(range(place.side)):
                total = self.part(kz, kf, 0)
                for kg in range(1, place.side):
                    self.arrived(self.near.at[kg - 1, kf, kz], self.sems["gr"].at[kg, kf, kz])
                    total = total + self.near[kg - 1, kf, kz].astype(jnp.float32)
                source = self.near.at[0, kf, kz]
                source[...] = total.astype(source.dtype)
                if kf:
                    self.send(
                        source,
                        self.far.at[kf - 1, kz],
                        (place.core, place.chip + place.first[kf]),
                        self.sems["fs"].at[kf, kz],
                        self.sems["fr"].at[kf, kz],
                    )

    def summed(self, kz):
        place = self.place
        total = self.near[0, 0, kz].astype(jnp.float32)
        for kf in range(1, place.side):
            self.arrived(self.far.at[kf - 1, kz], self.sems["fr"].at[kf, kz])
            total = total + self.far[kf - 1, kz].astype(jnp.float32)
        return total.astype(self.far.dtype)

    def sent_all(self):
        for copy in self.sent:
            copy.wait_send()


class FoldLine:
    def __init__(self, place, parts, end, sems):
        self.place, self.parts, self.end, self.sems = place, parts, end, sems

    def begin(self, *steps):
        place = self.place
        for kz in steps or reversed(range(1, place.line)):
            self.copy(kz).start()

    def copy(self, kz):
        place = self.place
        return remote(
            self.parts.at[kz],
            self.end.at[kz - 1],
            self.sems["zs"].at[kz, 0],
            self.sems["zr"].at[kz],
            (place.core, place.chip + place.along[kz]),
        )

    def result(self):
        total = self.parts[0].astype(jnp.float32)
        for kz in range(1, self.place.line):
            self.copy(kz).wait_recv()
            total = total + self.end[kz - 1].astype(jnp.float32)
        return total

    def sent_all(self):
        for kz in range(1, self.place.line):
            self.copy(kz).wait_send()


class FoldRole(Fold):
    def __init__(self, place, part, stage, near, far, end, sems):
        super().__init__(place, part, stage, near, far, sems)
        self.end = end

    def stage_c(self, kz):
        place = self.place
        source = self.far.at[0, kz]
        source[...] = self.summed(kz)
        if kz:
            self.send(
                source,
                self.end.at[place.core, kz // 2],
                (place.role, place.chip + place.along[kz]),
                self.sems["zs"].at[kz, 0],
                self.sems["er"].at[place.core, kz // 2],
            )
        else:
            self.last = source
            self.cross = remote(
                source,
                self.end.at[place.core, 0],
                self.sems["zs"].at[0, 0],
                self.sems["er"].at[place.core, 0],
                (1 - place.core, place.chip),
            )

            @pl.when(place.core != place.role)
            def _():
                self.cross.start()

    def result(self, sum_ref):
        place = self.place
        rows, half = self.end.shape[2:]
        mine = place.core == place.role

        def columns(core):
            return pl.ds(pl.multiple_of(core * half, half), half)

        def add(parity):
            sources = [kz for kz in range(place.line) if kz % 2 == parity]
            for core in range(2):
                total = jnp.zeros((rows, half), jnp.float32)
                for kz in sources:
                    if kz:
                        self.arrived(self.end.at[core, kz // 2], self.sems["er"].at[core, kz // 2])
                        total = total + self.end[core, kz // 2].astype(jnp.float32)
                sum_ref[:, core * half : (core + 1) * half] = total

        @pl.when(mine)
        def _():
            add(0)
            own, other = columns(place.core), columns(1 - place.core)
            sum_ref[:, own] += self.last[...].astype(jnp.float32)
            self.arrived(self.end.at[1 - place.core, 0], self.sems["er"].at[1 - place.core, 0])
            sum_ref[:, other] += self.end[1 - place.core, 0].astype(jnp.float32)

        @pl.when(jnp.logical_not(mine))
        def _():
            add(1)
            self.cross.wait_send()


def fold_sems(line, side):
    dma = pltpu.SemaphoreType.DMA
    return {
        "gs": dma((side, side, line)),
        "gr": dma((side, side, line)),
        "fs": dma((side, line)),
        "fr": dma((side, line)),
        "zs": dma((line, 1)),
        "zr": dma((line,)),
        "er": dma((2, line // 2)),
    }


def fold_buffers(line, side, shape, dtype):
    return [
        pltpu.VMEM((side - 1, side, line) + shape, dtype),
        pltpu.VMEM((side - 1, side, line) + shape, dtype),
    ]


def backward_kernel(
    n_dp,
    act_ref,
    cell_ref,
    outer_ref,
    wt_ref,
    ht_ref,
    dq_ref,
    dk_ref,
    dec_ref,
    mem_ref,
    ctx_ref,
    dz_ref,
    sq_ref,
    gl_ref,
    dpre_ref,
    dpre_other,
    ht_other,
    mats_part,
    out_part,
    state,
    held,
    facts,
    facts_gl,
    g_mats,
    g_out,
    m_stage,
    m_near,
    o_stage,
    o_near,
    m_far,
    o_far,
    fact_sems,
    pre_sems,
    ht_sems,
    sems_m,
    sems_o,
):
    width = outer_ref.shape[1]
    steps = outer_ref.shape[0] // ROWS
    low, f32 = jnp.bfloat16, jnp.float32
    place = Place(n_dp)
    place.greet()
    core = place.core
    other = (1 - core, place.chip)
    sources = [dq_ref.at[1 - core], dk_ref.at[1 - core], dec_ref, mem_ref, ctx_ref, dz_ref, sq_ref]
    handed = [
        remote(source, facts.at[n], fact_sems.at[0, n], fact_sems.at[1, n], other)
        for n, source in enumerate(sources)
    ]
    handed.append(remote(gl_ref.at[1 - core], facts_gl, fact_sems.at[0, 7], fact_sems.at[1, 7], other))
    handed.append(remote(ht_ref, ht_other, ht_sems.at[0], ht_sems.at[1], other))
    for copy in handed:
        copy.start()
    state[...] = jnp.zeros_like(state)
    held[...] = jnp.zeros_like(held)

    def step(k, carry):
        t = steps - 1 - k
        rows = pl.ds(pl.multiple_of(t * ROWS, ROWS), ROWS)
        after = pl.ds(pl.multiple_of((t + 1) * ROWS, ROWS), ROWS)
        hidden_total = outer_ref[rows] + jnp.dot(
            state[:, :width], wt_ref[0], preferred_element_type=f32
        )
        for q in range(1, 4):
            hidden_total = hidden_total + jnp.dot(
                state[:, q * width : (q + 1) * width], wt_ref[q], preferred_element_type=f32
            )
        in_gate = act_ref[rows, :width]
        forget = act_ref[rows, width : 2 * width]
        candidate = act_ref[rows, 2 * width : 3 * width]
        out_gate = act_ref[rows, 3 * width :]
        squash = jnp.tanh(cell_ref[after])
        cell_total = held[...] + hidden_total * out_gate * (1.0 - squash * squash)
        held[...] = cell_total * forget
        grads = jnp.concatenate(
            [
                cell_total * candidate * in_gate * (1.0 - in_gate),
                cell_total * cell_ref[rows] * forget * (1.0 - forget),
                cell_total * in_gate * (1.0 - candidate * candidate),
                hidden_total * squash * out_gate * (1.0 - out_gate),
            ],
            -1,
        ).astype(low)
        state[...] = grads
        dpre_ref[rows] = grads
        return carry

    shares = 4
    share = steps // shares

    def hand_over(n):
        top = (steps - (n + 1) * share) * ROWS
        rows = slice(top, top + share * ROWS)
        columns = pl.ds(pl.multiple_of((1 - core) * 2 * width, 2 * width), 2 * width)
        copy = remote(
            dpre_ref.at[rows, columns], dpre_other.at[rows, :], pre_sems.at[0, n], pre_sems.at[1, n], other
        )
        copy.start()
        handed.append(copy)

    part_rows = g_mats.shape[1] // 3
    out_rows = g_out.shape[1]

    def matrices():
        for copy in handed[:8]:
            copy.wait_recv()
        joined = jnp.where(core == 0, dec_ref[...], ctx_ref[...])
        joined_other = jnp.where(core == 0, facts[2], facts[4])
        pairs = [
            (dq_ref[core], dec_ref[...], facts[0], facts[2]),
            (dk_ref[core], mem_ref[...], facts[1], facts[3]),
            (joined, dz_ref[...], joined_other, facts[5]),
        ]
        for m, (a, b, c, d) in enumerate(pairs):
            total = (contract(a, b, 0, 0) + contract(c, d, 0, 0)).astype(low)
            for block in range(n_dp):
                g_mats[block, m * part_rows : (m + 1) * part_rows] = total[
                    block * part_rows : (block + 1) * part_rows
                ]
        total = (contract(sq_ref[...], gl_ref[core], 0, 0) + contract(facts[6], facts_gl[...], 0, 0)).astype(low)
        for block in range(n_dp):
            g_out[block] = total[block * out_rows : (block + 1) * out_rows]

    mats = Fold(
        place, lambda kz, kf, kg: g_mats[place.block(kz, kf, kg)].astype(f32), m_stage, m_near, m_far, sems_m
    )
    outs = Fold(
        place, lambda kz, kf, kg: g_out[place.block(kz, kf, kg)].astype(f32), o_stage, o_near, o_far, sems_o
    )
    matrices()
    mats.stage_a()
    outs.stage_a()
    lax.fori_loop(0, share, step, 0)
    hand_over(0)
    lines = list(reversed(range(place.line)))
    for n in range(1, shares):
        for kz in lines[(n - 1) * place.line // shares : n * place.line // shares]:
            mats.stage_b(kz)
        lax.fori_loop(n * share, (n + 1) * share, step, 0)
        hand_over(n)
    for kz in lines[(shares - 1) * place.line // shares :]:
        mats.stage_b(kz)
    outs.stage_b()
    for kz in lines:
        mats_part[kz] = mats.summed(kz)
        out_part[kz] = outs.summed(kz)
    for copy in handed[8:]:
        copy.wait_recv()
    for copy in handed:
        copy.wait_send()
    mats.sent_all()
    outs.sent_all()


def backward(n_dp, act, cell, outer, weight_t, ht, facts):
    rows, width = outer.shape
    low, f32 = jnp.bfloat16, jnp.float32
    line, side = DP_LAYOUTS[n_dp][:2]
    utt_rows = facts[2].shape[0]
    half_vocab = facts[-1].shape[-1]
    mats_block = (3 * width // n_dp, width)
    out_block = (width // n_dp, half_vocab)
    dma = pltpu.SemaphoreType.DMA
    return pl.pallas_call(
        functools.partial(backward_kernel, n_dp),
        out_shape=(
            jax.ShapeDtypeStruct((rows, 4 * width), low),
            jax.ShapeDtypeStruct((rows, 2 * width), low),
            jax.ShapeDtypeStruct(ht.shape, low),
            jax.ShapeDtypeStruct((line,) + mats_block, low),
            jax.ShapeDtypeStruct((line,) + out_block, low),
        ),
        in_specs=[VMEM_SPEC] * 4 + [ANY_SPEC] + [VMEM_SPEC] * 8,
        out_specs=(VMEM_SPEC, VMEM_SPEC, ANY_SPEC, VMEM_SPEC, VMEM_SPEC),
        scratch_shapes=[
            pltpu.VMEM((ROWS, 4 * width), low),
            pltpu.VMEM((ROWS, width), f32),
            pltpu.VMEM((7, utt_rows, width), low),
            pltpu.VMEM((utt_rows, half_vocab), low),
            pltpu.VMEM((n_dp,) + mats_block, low),
            pltpu.VMEM((n_dp,) + out_block, low),
        ]
        + fold_buffers(line, side, mats_block, low)
        + fold_buffers(line, side, out_block, low)
        + [pltpu.VMEM((side - 1, line) + block, low) for block in (mats_block, out_block)]
        + [dma((2, 8)), dma((2, 4)), dma((2,))]
        + [fold_sems(line, side)] * 2,
        compiler_params=pltpu.CompilerParams(
            collective_id=2, has_side_effects=True, vmem_limit_bytes=VMEM_LIMIT
        ),
    )(act, cell, outer, weight_t, ht, *facts)


def update_kernel(
    n_dp,
    batch,
    ht_ref,
    ht_other,
    dpre_ref,
    dpre_other,
    w_ref,
    base_ref,
    spread_ref,
    outer_ref,
    vectors_ref,
    dvec_ref,
    mats_part,
    out_part,
    sum_ref,
    gin_ref,
    vec_sum,
    mats_sum,
    out_sum,
    w_s,
    gin_s,
    gin_u,
    vec_s,
    vec_other,
    vec_parts,
    l_stage,
    l_near,
    v_stage,
    v_near,
    l_far,
    l_end,
    v_far,
    v_parts,
    v_end,
    m_end,
    o_end,
    w_sem,
    gin_sems,
    vec_sems,
    sems_l,
    sems_v,
    sems_m,
    sems_o,
):
    width = base_ref.shape[1]
    steps = base_ref.shape[0] // ROWS
    low, f32 = jnp.bfloat16, jnp.float32
    place = Place(n_dp)
    load = pltpu.make_async_copy(w_ref, w_s, w_sem)
    load.start()
    place.greet()
    core = place.core
    encoder = place.role == 0
    mine = core == place.role
    block_rows = sum_ref.shape[0]
    half = pl.ds(pl.multiple_of(core * 2 * width, 2 * width), 2 * width)

    def part(kz, kf, kg):
        rows = pl.ds(pl.multiple_of(place.block(kz, kf, kg) * block_rows, block_rows), block_rows)
        return jnp.dot(ht_ref[rows], dpre_ref[:, half], preferred_element_type=f32) + jnp.dot(
            ht_other[rows], dpre_other[...], preferred_element_type=f32
        )

    matrix = FoldRole(place, part, l_stage, l_near, l_far, l_end, sems_l)
    mats = FoldLine(place, mats_part, m_end, sems_m)
    outs = FoldLine(place, out_part, o_end, sems_o)
    matrix.stage_a()
    mats.begin()
    outs.begin()

    load.wait()
    gin_s[...] = contract(dpre_ref[...], w_s[...], 1, 1)
    input_grad = gin_s[...]
    scaled = base_ref[...]
    vec_s[...] = dvec_ref[...]
    vec_s[4:5, :width] = jnp.where(encoder, jnp.sum(input_grad * scaled, 0, keepdims=True), 0.0)
    vec_s[4:5, width:] = jnp.where(encoder, jnp.sum(input_grad, 0, keepdims=True), 0.0)
    for q in range(4):
        columns = slice((q % 2) * width, (q % 2 + 1) * width)
        bias = jnp.sum(dpre_ref[:, q * width : (q + 1) * width].astype(f32), 0, keepdims=True)
        for role in range(2):
            row = 2 * role + q // 2
            vec_s[row : row + 1, columns] = jnp.where(place.role == role, bias, 0.0)

    @pl.when(encoder)
    def _():
        grads = gin_s[...] * vectors_ref[4:5, :width]
        values = base_ref[...]
        gin_s[...] = (
            spread_ref[...]
            * (
                grads
                - jnp.mean(grads, -1, keepdims=True)
                - values * jnp.mean(grads * values, -1, keepdims=True)
            )
            + outer_ref[...]
        )

    turned = gin_s[...].reshape(steps, ROWS, width)
    for u in range(batch):
        gin_u[u] = turned[:, u, :]
    kept = pltpu.make_async_copy(gin_u, gin_ref, gin_sems.at[0])
    handed = remote(gin_u, gin_ref, gin_sems.at[1], gin_sems.at[2], (1 - core, place.chip + place.along[1]))

    @pl.when(mine)
    def _():
        kept.start()

    @pl.when(jnp.logical_not(mine))
    def _():
        handed.start()

    own_half = pl.ds(pl.multiple_of(core * width, width), width)
    other_half = pl.ds(pl.multiple_of((1 - core) * width, width), width)
    trade = remote(
        vec_s.at[:, other_half], vec_other, vec_sems.at[0], vec_sems.at[1], (1 - core, place.chip)
    )
    trade.start()
    trade.wait_recv()
    total = vec_s[:, own_half] + vec_other[...]
    piece = width // n_dp
    per_tile = LANES // piece
    for block in range(n_dp):
        tile = total[:, (block // per_tile) * LANES : (block // per_tile + 1) * LANES]
        turn = (block % per_tile) * piece
        vec_parts[block] = pltpu.roll(tile, LANES - turn, 1) if turn else tile
    vecs = Fold(place, lambda kz, kf, kg: vec_parts[place.block(kz, kf, kg)], v_stage, v_near, v_far, sems_v)
    vec_line = FoldLine(place, v_parts, v_end, sems_v)
    vecs.stage_a()
    lines = list(reversed(range(place.line)))
    matrix.stage_b(lines[0])
    for n, kz in enumerate(lines[1:]):
        if n == place.line // 2 - 1:
            vecs.stage_b()
        matrix.stage_b(kz)
        matrix.stage_c(lines[n])
    for n in lines:
        v_parts[n] = vecs.summed(n)
    vec_line.begin()
    matrix.stage_c(lines[-1])
    mats_sum[...] = mats.result()
    out_sum[...] = outs.result()
    vec_sum[...] = vec_line.result()
    matrix.result(sum_ref)

    @pl.when(mine)
    def _():
        kept.wait()

    @pl.when(jnp.logical_not(mine))
    def _():
        handed.wait()

    trade.wait_send()
    for fold in (matrix, vecs, vec_line, mats, outs):
        fold.sent_all()


def update(
    n_dp, batch, ht, ht_other, dpre, dpre_other, weight, base, spread, outer, vectors, dvec, mats_part, out_part
):
    rows, width = base.shape
    steps = rows // ROWS
    low, f32 = jnp.bfloat16, jnp.float32
    line, side = DP_LAYOUTS[n_dp][:2]
    block_rows = 2 * width // n_dp
    block = (block_rows, 2 * width)
    dma = pltpu.SemaphoreType.DMA
    return pl.pallas_call(
        functools.partial(update_kernel, n_dp, batch),
        out_shape=(
            jax.ShapeDtypeStruct((block_rows, 4 * width), f32),
            jax.ShapeDtypeStruct((batch, steps, width), f32),
            jax.ShapeDtypeStruct((8, LANES), f32),
            jax.ShapeDtypeStruct(mats_part.shape[1:], f32),
            jax.ShapeDtypeStruct(out_part.shape[1:], f32),
        ),
        in_specs=[VMEM_SPEC] * 4 + [ANY_SPEC] + [VMEM_SPEC] * 7,
        out_specs=(VMEM_SPEC, ANY_SPEC, VMEM_SPEC, VMEM_SPEC, VMEM_SPEC),
        scratch_shapes=[
            pltpu.VMEM((width, 4 * width), low),
            pltpu.VMEM((rows, width), f32),
            pltpu.VMEM((batch, steps, width), f32),
            pltpu.VMEM((8, 2 * width), f32),
            pltpu.VMEM((8, width), f32),
            pltpu.VMEM((n_dp, 8, LANES), f32),
        ]
        + fold_buffers(line, side, block, low)
        + fold_buffers(line, side, (8, LANES), f32)
        + [
            pltpu.VMEM((side - 1, line) + block, low),
            pltpu.VMEM((2, line // 2) + block, low),
            pltpu.VMEM((side - 1, line, 8, LANES), f32),
            pltpu.VMEM((line, 8, LANES), f32),
            pltpu.VMEM((line - 1, 8, LANES), f32),
            pltpu.VMEM((line - 1,) + mats_part.shape[1:], low),
            pltpu.VMEM((line - 1,) + out_part.shape[1:], low),
        ]
        + [dma, dma((3,)), dma((2,))]
        + [fold_sems(line, side)] * 4,
        compiler_params=pltpu.CompilerParams(
            collective_id=3, has_side_effects=True, vmem_limit_bytes=VMEM_LIMIT
        ),
    )(ht, ht_other, dpre, dpre_other, weight, base, spread, outer, vectors, dvec, mats_part, out_part)


STEP = 5
NORM_EPS = 1e-05
BETA_ONE = 0.9
BETA_TWO = 0.999
ADAM_EPS = 1e-08
WEIGHT_DECAY = 0.01
RATE_LSTM = 0.05
RATE_MATRIX = 0.02
RATE_VECTOR = 0.3
AXES = ("section", "dp")


def swapped(block):
    return lax.ppermute(block, "section", [(0, 1), (1, 0)])


def adamw(master, first, second, grad, rate):
    first_new = BETA_ONE * first + (1.0 - BETA_ONE) * grad
    second_new = BETA_TWO * second + (1.0 - BETA_TWO) * grad * grad
    first_hat = first_new / (1.0 - BETA_ONE**STEP)
    second_hat = second_new / (1.0 - BETA_TWO**STEP)
    master_new = master - rate * (
        first_hat / (jnp.sqrt(second_hat) + ADAM_EPS) + WEIGHT_DECAY * master
    )
    return (master_new, first_new, second_new)


def slot_major(block):
    batch_size, length, width = block.shape
    padded = jnp.pad(jnp.swapaxes(block, 0, 1), ((0, 0), (0, ROWS - batch_size), (0, 0)))
    return padded.reshape(length * ROWS, width)


def utt_major(block, batch_size):
    width = block.shape[-1]
    return jnp.swapaxes(block.reshape(-1, ROWS, width)[:, :batch_size], 0, 1)


def runner(chip, section, n_dp):
    if chip // LINE_STRIDE % 2 == section:
        return section * n_dp + chip
    return (1 - section) * n_dp + (chip ^ LINE_STRIDE)


def local(
    inputs,
    counts,
    cotangent,
    lstm_master,
    lstm_copy,
    lstm_first,
    lstm_second,
    mats_master,
    mats_copy,
    mats_first,
    mats_second,
    out_master,
    out_copy,
    out_first,
    out_second,
    vec_master,
    vec_first,
    vec_second,
):
    low, f32 = jnp.bfloat16, jnp.float32
    n_dp = lax.axis_size("dp")
    section_index = lax.axis_index("section")
    role = lax.rem(lax.axis_index("dp") // LINE_STRIDE, 2)
    on_first = section_index == 0
    as_encoder = role == 0
    at_home = section_index == role
    chips = range(n_dp)
    batch_size, length, model_width = inputs.shape[1:]
    half = batch_size // 2
    vocab_half = out_copy.shape[1]
    vocab_pad = -(-vocab_half // LANES) * LANES

    homes = [(s * n_dp + c, runner(c, s, n_dp)) for s in range(2) for c in chips]
    away = [pair for pair in homes if pair[0] != pair[1]]
    straight = [(runner(c, s, n_dp), s * n_dp + c) for s in range(2) for c in chips]
    crossed = [(runner(c, s, n_dp), (1 - s) * n_dp + c) for s in range(2) for c in chips]

    def traded(block):
        kept = jnp.where(on_first, block[:half], block[half:])
        other = swapped(jnp.where(on_first, block[half:], block[:half]))
        return jnp.where(on_first, kept, other), jnp.where(on_first, other, kept)

    def to_halves(block):
        low_half, high_half = block[:half], block[half:]
        one = lax.ppermute(jnp.where(as_encoder, low_half, high_half), AXES, straight)
        two = lax.ppermute(jnp.where(as_encoder, high_half, low_half), AXES, crossed)
        return jnp.where(on_first, one, two), jnp.where(on_first, two, one)

    def from_halves(from_encoder, from_decoder):
        one = lax.ppermute(
            jnp.where(on_first, from_encoder, from_decoder), AXES, [(b, a) for a, b in straight]
        )
        two = lax.ppermute(
            jnp.where(on_first, from_decoder, from_encoder), AXES, [(b, a) for a, b in crossed]
        )
        return jnp.where(
            as_encoder, jnp.concatenate([one, two], 0), jnp.concatenate([two, one], 0)
        )

    sequence = jnp.where(at_home, inputs[0], lax.ppermute(inputs[0], AXES, away))
    frames, labels = traded(counts[0])
    label_mask = lax.broadcasted_iota(jnp.int32, (half, length), 1) < labels[:, None]
    grad_low, grad_high = traded(cotangent)
    grad_logits = jnp.stack([grad_low, grad_high]) * label_mask[None, :, :, None].astype(low)
    grad_logits = jnp.pad(grad_logits, ((0, 0),) * 3 + ((0, vocab_pad - vocab_half),))
    grad_logits = grad_logits.reshape(2, half * length, vocab_pad)

    raw_values = sequence.astype(f32)
    center = raw_values - jnp.mean(raw_values, -1, keepdims=True)
    spread = lax.rsqrt(jnp.mean(center * center, -1, keepdims=True) + NORM_EPS)
    base = slot_major(jnp.where(as_encoder, center * spread, raw_values))
    spread = slot_major(spread)

    mats_block = jnp.swapaxes(mats_copy, 1, 2)
    out_block = jnp.pad(out_copy, ((0, 0), (0, vocab_pad - vocab_half)))
    piece = vec_master.shape[1]
    vec_block = jnp.pad(vec_master.astype(low).astype(f32), ((0, 0), (0, LANES - piece)))
    act, cell, h_rows, x_rows, vectors, weight, weight_t, mats_full, out_full = forward(
        n_dp, base, lstm_copy[0], mats_block, out_block, vec_block
    )
    mats_full = mats_full.reshape(3, 2 * model_width, model_width)
    out_full = out_full.reshape(2, model_width, vocab_pad)

    states = utt_major(h_rows, batch_size).astype(f32)
    result = jnp.where(as_encoder, raw_values + states, states).astype(low)
    memory, decoded = to_halves(result)
    decoded = decoded.reshape(-1, model_width)
    memory = memory.reshape(-1, model_width)
    row = jnp.pad(vectors[7], (0, vocab_pad))
    bias = jnp.stack(
        [row[model_width + s * vocab_half : model_width + s * vocab_half + vocab_pad] for s in range(2)]
    )
    squashed, context, dz, dq, dk, ddec, dmem, vec_rows, logits, logit_sums = attention(
        frames, decoded, memory, mats_full, vectors, out_full, bias, grad_logits
    )
    logits = logits.reshape(2, half, length, vocab_pad)[..., :vocab_half]
    kept = jnp.where(on_first, logits[0], logits[1])
    other = swapped(jnp.where(on_first, logits[1], logits[0]))
    logits = jnp.concatenate([jnp.where(on_first, kept, other), jnp.where(on_first, other, kept)], 0)

    outer = from_halves(dmem, ddec.astype(low)).reshape(batch_size, length, model_width)
    outer = slot_major(outer).astype(f32)
    h_before = jnp.concatenate([jnp.zeros_like(h_rows[:ROWS]), h_rows[:-ROWS]], 0)
    ht = jnp.concatenate([x_rows.T, h_before.T], 0)
    dpre, dpre_other, ht_other, mats_part, out_part = backward(
        n_dp, act, cell, outer, weight_t, ht, (dq, dk, decoded, memory, context, dz, squashed, grad_logits)
    )
    logit_row = jnp.concatenate(
        [
            jnp.zeros((model_width,), f32),
            logit_sums[0, :vocab_half],
            logit_sums[1, :vocab_half],
            jnp.zeros((model_width - 2 * vocab_half,), f32),
        ]
    )
    vec_rows = vec_rows + jnp.pad(logit_row[None], ((7, 0), (0, 0)))
    lstm_sum, inputs_grad, vec_sum, mats_sum, out_sum = update(
        n_dp,
        batch_size,
        ht,
        ht_other,
        dpre,
        dpre_other,
        weight,
        base,
        spread,
        outer,
        vectors,
        vec_rows,
        mats_part,
        out_part,
    )
    mats_sum = jnp.swapaxes(mats_sum.reshape(3, -1, model_width), 1, 2)
    lstm_new, lstm_first_new, lstm_second_new = adamw(
        lstm_master, lstm_first, lstm_second, lstm_sum[None], RATE_LSTM
    )
    mats_new, mats_first_new, mats_second_new = adamw(
        mats_master, mats_first, mats_second, mats_sum, RATE_MATRIX
    )
    out_new, out_first_new, out_second_new = adamw(
        out_master, out_first, out_second, out_sum[:, :vocab_half], RATE_MATRIX
    )
    vec_new, vec_first_new, vec_second_new = adamw(
        vec_master, vec_first, vec_second, vec_sum[:, :piece], RATE_VECTOR
    )
    return (
        logits,
        inputs_grad[None],
        lstm_new,
        lstm_first_new,
        lstm_second_new,
        lstm_new.astype(low),
        mats_new,
        mats_first_new,
        mats_second_new,
        mats_new.astype(low),
        out_new,
        out_first_new,
        out_second_new,
        out_new.astype(low),
        vec_new,
        vec_first_new,
        vec_second_new,
    )


def solution(mesh):
    lstm = P("section", "dp", None)
    mats = P(None, None, ("section", "dp"))
    out = P("dp", "section")
    vec = P(None, ("section", "dp"))
    logits = P("dp", None, "section")
    rows = P("section", "dp", None, None)
    groups = (lstm,) * 4 + (mats,) * 4 + (out,) * 4 + (vec,) * 3
    return jax.shard_map(
        local,
        mesh=mesh,
        in_specs=(rows, P("section", "dp"), logits) + groups,
        out_specs=(logits, rows) + groups,
        check_vma=False,
    )
```

```python
import functools
import jax
import jax.numpy as jnp
from jax import lax
from jax.experimental import pallas as pl
from jax.experimental.pallas import tpu as pltpu
from jax.sharding import PartitionSpec as P

ROWS = 16
LANES = 128
UNROLL = 8
ENERGY_OFFSET = -4.0
NORM_EPS = 1e-05
VMEM_SPEC = pl.BlockSpec(memory_space=pltpu.VMEM)
SMEM_SPEC = pl.BlockSpec(memory_space=pltpu.SMEM)
VMEM_LIMIT = 60 * 1024 * 1024


def contract(left, right, left_dim, right_dim):
    return lax.dot_general(
        left, right, (((left_dim,), (right_dim,)), ((), ())), preferred_element_type=jnp.float32
    )


MESH_ID = pl.DeviceIdType.MESH
ANY_SPEC = pl.BlockSpec(memory_space=pl.ANY)
DP_LAYOUTS = {16: (4, 2, 1, 2), 128: (8, 4, 1, 32)}
LINE_STRIDE = 4
TURN = 256
CHUNKS = 2


def flipped(value, k):
    result = value
    bit = 1
    while bit <= k:
        if k & bit:
            result = result + bit - 2 * bit * lax.rem(value // bit, 2)
        bit *= 2
    return result


class Place:
    def __init__(self, n_dp):
        self.line, self.side, stride_a, stride_b = DP_LAYOUTS[n_dp]
        self.core = lax.axis_index("section")
        self.chip = lax.axis_index("dp")
        self.z = lax.rem(self.chip // LINE_STRIDE, self.line)
        at_a = lax.rem(self.chip // stride_a, self.side)
        at_b = lax.rem(self.chip // stride_b, self.side)
        self.role = lax.rem(self.z, 2)
        moves_a = [(flipped(at_a, k) - at_a) * stride_a for k in range(self.side)]
        moves_b = [(flipped(at_b, k) - at_b) * stride_b for k in range(self.side)]
        core = self.core
        self.first = [a + (b - a) * core for a, b in zip(moves_a, moves_b)]
        self.second = [b + (a - b) * core for a, b in zip(moves_a, moves_b)]
        self.along = [(flipped(self.z, k) - self.z) * LINE_STRIDE for k in range(self.line)]

    def block(self, kz, kf=0, kg=0):
        return self.chip + self.along[kz] + self.first[kf] + self.second[kg]

    def other_block(self, kz, kf=0, kg=0):
        return self.chip + self.along[kz] + self.second[kf] + self.first[kg]

    def greet(self):
        barrier = pltpu.get_barrier_semaphore()
        peers = [(1 - self.core, self.chip)]
        for k in range(1, self.line):
            peers += [(0, self.chip + self.along[k]), (1, self.chip + self.along[k])]
        for k in range(1, self.side):
            peers += [(self.core, self.chip + self.first[k]), (self.core, self.chip + self.second[k])]
        for peer in peers:
            pl.semaphore_signal(barrier, inc=1, device_id=peer, device_id_type=MESH_ID)
        pl.semaphore_wait(barrier, len(peers))


def remote(source, target, send, receive, device):
    return pltpu.make_async_remote_copy(
        src_ref=source,
        dst_ref=target,
        send_sem=send,
        recv_sem=receive,
        device_id=device,
        device_id_type=MESH_ID,
    )


class Spread:
    def __init__(self, place, here, there, sems):
        self.place, self.here, self.there, self.sems = place, here, there, sems
        self.sent = []

    def send(self, target, device, send, receive):
        copy = remote(target, target, send, receive, device)
        copy.start()
        self.sent.append(copy)

    def arrived(self, target, semaphore):
        place = self.place
        remote(target, target, semaphore, semaphore, (1 - place.core, place.chip)).wait_recv()

    def to_second(self, kz, kf):
        place = self.place
        target = self.here(place.block(kz, kf))
        for kg in range(1, place.side):
            self.send(
                target,
                (place.core, place.chip + place.second[kg]),
                self.sems["gs"].at[kg, kf, kz],
                self.sems["gr"].at[kg, kf, kz],
            )

    def to_core(self, kz, kf, kg):
        place = self.place
        self.send(
            self.here(place.block(kz, kf, kg)),
            (1 - place.core, place.chip),
            self.sems["cs"].at[kg, kf, kz],
            self.sems["cr"].at[kg, kf, kz],
        )

    def stage_one(self, *steps):
        place = self.place
        for kz in steps or range(place.line):
            self.wait_line(kz)
            target = self.here(place.block(kz))
            for kf in range(1, place.side):
                self.send(
                    target,
                    (place.core, place.chip + place.first[kf]),
                    self.sems["fs"].at[kf, kz],
                    self.sems["fr"].at[kf, kz],
                )
            self.to_second(kz, 0)
            self.to_core(kz, 0, 0)

    def stage_two(self):
        place = self.place
        for kf in range(1, place.side):
            for kz in range(place.line):
                self.arrived(self.here(place.block(kz, kf)), self.sems["fr"].at[kf, kz])
                self.to_second(kz, kf)
                self.to_core(kz, kf, 0)

    def stage_three(self):
        place = self.place
        for kg in range(1, place.side):
            for kf in range(place.side):
                for kz in range(place.line):
                    self.arrived(self.here(place.block(kz, kf, kg)), self.sems["gr"].at[kg, kf, kz])
                    self.to_core(kz, kf, kg)

    def finish(self):
        place = self.place
        for kg in range(place.side):
            for kf in range(place.side):
                for kz in range(place.line):
                    self.arrived(self.there(place.other_block(kz, kf, kg)), self.sems["cr"].at[kg, kf, kz])

    def sent_all(self):
        for copy in self.sent:
            copy.wait_send()


def spread_sems(line, side):
    dma = pltpu.SemaphoreType.DMA
    return {
        "zs": dma((line, 2)),
        "zr": dma((line,)),
        "fs": dma((side, line)),
        "fr": dma((side, line)),
        "gs": dma((side, side, line)),
        "gr": dma((side, side, line)),
        "cs": dma((side, side, line)),
        "cr": dma((side, side, line)),
    }


def spread_even(place, source, at, sems):
    own = at(place.core, place.chip)
    spread = Spread(place, lambda block: at(place.core, block), lambda block: at(1 - place.core, block), sems)
    kept = pltpu.make_async_copy(source, own, sems["zr"].at[0])
    copies = [
        remote(source, own, sems["zs"].at[k, 0], sems["zr"].at[k], (place.core, place.chip + place.along[k]))
        for k in range(1, place.line)
    ]

    def begin():
        kept.start()
        for copy in copies:
            copy.start()
        spread.sent += copies

    def wait_line(kz):
        if kz == 0:
            kept.wait()
        else:
            spread.arrived(spread.here(place.block(kz)), sems["zr"].at[kz])

    spread.begin = begin
    spread.wait_line = wait_line
    return spread


class LineGather:
    def __init__(self, place, source, target, sems):
        self.kept = pltpu.make_async_copy(source, target.at[0], sems["zr"].at[0])
        self.copies = [
            remote(source, target.at[k], sems["zs"].at[k, 0], sems["zr"].at[k], (place.core, place.chip + place.along[k]))
            for k in range(1, place.line)
        ]

    def begin(self):
        for copy in [self.kept] + self.copies:
            copy.start()

    def finish(self):
        for copy in [self.kept] + self.copies:
            copy.wait()


def spread_line(place, source, target, sems):
    spread = Spread(
        place,
        lambda block: target.at[place.core, block],
        lambda block: target.at[1 - place.core, block],
        sems,
    )
    kept = [
        pltpu.make_async_copy(source.at[kz], spread.here(place.block(kz)), sems["zr"].at[kz])
        for kz in range(place.line)
    ]

    def begin():
        for copy in kept:
            copy.start()

    spread.begin = begin
    spread.wait_line = lambda kz: kept[kz].wait()
    return spread


def spread_role(place, source, target, sems, rows, half, first, count):
    source = source.at[first : first + count]

    def columns(core):
        return pl.ds(pl.multiple_of(core * half, half), half)

    def at(block, core):
        return target.at[pl.ds(pl.multiple_of(block * rows + first, count), count), columns(core)]

    spread = Spread(
        place, lambda block: at(block, place.core), lambda block: at(block, 1 - place.core), sems
    )
    mine = place.role == place.core
    kept = pltpu.make_async_copy(source.at[:, columns(place.core)], at(place.chip, place.core), sems["zr"].at[0])
    cross = remote(
        source.at[:, columns(1 - place.core)],
        at(place.chip, 1 - place.core),
        sems["zs"].at[0, 0],
        sems["zr"].at[0],
        (1 - place.core, place.chip),
    )
    copies = [
        [
            remote(
                source.at[:, columns(core)],
                at(place.chip, core),
                sems["zs"].at[k, core],
                sems["zr"].at[k],
                (core, place.chip + place.along[k]),
            )
            for core in range(2)
        ]
        for k in range(1, place.line)
    ]

    guest = jnp.logical_not(mine)

    def each(condition, steps, action):
        @pl.when(condition)
        def _():
            for k in steps:
                for copy in copies[k - 1] if k else [cross]:
                    action(copy)

    def start(copy):
        copy.start()

    def begin():
        @pl.when(mine)
        def _():
            kept.start()

        each(mine, range(0, place.line, 2), start)
        each(guest, range(1, place.line, 2), start)

    def wait_line(kz):
        if kz == 0:

            @pl.when(mine)
            def _():
                kept.wait()

            @pl.when(jnp.logical_not(mine))
            def _():
                spread.arrived(spread.here(place.chip), sems["zr"].at[0])

        else:
            spread.arrived(spread.here(place.block(kz)), sems["zr"].at[kz])

    def finished(copy):
        copy.wait_send()

    def sent_line():
        each(mine, range(0, place.line, 2), finished)
        each(guest, range(1, place.line, 2), finished)

    spread.begin = begin
    spread.wait_line = wait_line
    spread.sent_line = sent_line
    return spread


def forward_kernel(
    n_dp,
    seq_ref,
    shard_ref,
    mats_ref,
    out_ref,
    vec_ref,
    act_ref,
    cell_ref,
    ht_ref,
    base_ref,
    spread_ref,
    vectors_ref,
    pair_ref,
    w_out,
    wt_out,
    mats_out,
    mats_line,
    out_line,
    seq_s,
    result_s,
    x_s,
    h_s,
    w_s,
    wt_s,
    vec_s,
    state,
    keep_sem,
    seq_sem,
    pair_sem,
    sems_m,
    sems_v,
    sems_n,
    sems_o,
    *sems_w,
):
    batch, steps, width = seq_ref.shape
    low, f32 = jnp.bfloat16, jnp.float32
    place = Place(n_dp)
    core, chip = place.core, place.chip
    mine = core == place.role
    guest = jnp.logical_not(mine)
    encoder = place.role == 0
    place.greet()
    rows = shard_ref.shape[0]
    count = max(ROWS, rows // CHUNKS)
    matrix = [
        spread_role(place, shard_ref, w_s, sems, rows, 2 * width, n * count, count)
        for n, sems in zip(range(rows // count), sems_w)
    ]
    mats = spread_even(place, mats_ref.at[:2], lambda core, chip: mats_out.at[:, core, chip], sems_m)
    vecs = spread_even(place, vec_ref, lambda core, chip: vec_s.at[core, chip], sems_v)
    thirds = LineGather(place, mats_ref.at[2], mats_line, sems_n)
    outs = LineGather(place, out_ref, out_line, sems_o)
    vecs.begin()
    for part in matrix:
        part.begin()
    seq_kept = pltpu.make_async_copy(seq_ref, seq_s, seq_sem.at[0])
    seq_away = remote(seq_ref, seq_s, seq_sem.at[1], seq_sem.at[2], (1 - core, chip + place.along[1]))
    pl.when(mine)(seq_kept.start)
    pl.when(guest)(seq_away.start)
    for part in matrix:
        part.stage_one(0)
    state[...] = jnp.zeros_like(state)
    cell_ref[:ROWS] = jnp.zeros((ROWS, width), f32)
    base_ref[:, batch:] = jnp.zeros((steps, ROWS - batch, width), f32)
    spread_ref[...] = jnp.zeros_like(spread_ref)
    pl.when(mine)(seq_kept.wait)
    pl.when(guest)(seq_away.wait)
    for u in range(batch):
        raw = seq_s[u].astype(f32)
        center = raw - jnp.mean(raw, -1, keepdims=True)
        spread = lax.rsqrt(jnp.mean(center * center, -1, keepdims=True) + NORM_EPS)
        base_ref[:, u, :] = jnp.where(encoder, center * spread, raw)
        spread_ref[:, u, :] = jnp.broadcast_to(spread, (steps, LANES))
    line_rest = range(1, place.line)
    for n in range(len(matrix) + 2):
        if n < len(matrix):
            matrix[n].stage_one(*line_rest)
        if n == 0:
            vecs.stage_one()
        if n == len(matrix) - 1:
            mats.begin()
            thirds.begin()
            outs.begin()
        if 1 <= n <= len(matrix):
            matrix[n - 1].stage_two()
        if n == 1:
            vecs.stage_two()
        if n >= 2:
            matrix[n - 2].stage_three()
    mats.stage_one(0)
    vecs.stage_three()
    vecs.finish()
    piece = 2 * width // (2 * n_dp)
    per_tile = LANES // piece
    for m in range(2 * width // LANES):
        tile = jnp.zeros((8, LANES), f32)
        for k in range(per_tile):
            index = m * per_tile + k
            block = vec_s[index // n_dp, index % n_dp]
            tile = tile + (pltpu.roll(block, k * piece, 1) if k else block)
        vectors_ref[:, m * LANES : (m + 1) * LANES] = tile
    gain = jnp.where(encoder, vectors_ref[4:5, :width], 1.0)
    shift = jnp.where(encoder, vectors_ref[4:5, width:], 0.0)
    x_s[...] = (base_ref[...].reshape(steps * ROWS, width) * gain + shift).astype(low)
    ht_ref[:width] = x_s[...].T
    for part in matrix:
        part.finish()
    keep = pltpu.make_async_copy(w_s.at[:width], w_out, keep_sem.at[0])
    keep.start()
    for q in range(4):
        columns = slice(q * width, (q + 1) * width)
        row = q // 2
        bias_columns = slice((q % 2) * width, (q % 2 + 1) * width)
        bias = jnp.where(
            encoder, vectors_ref[row : row + 1, bias_columns], vectors_ref[row + 2 : row + 3, bias_columns]
        )
        act_ref[:, columns] = jnp.dot(x_s[...], w_s[:width, columns], preferred_element_type=f32) + bias

    def step(t, carry):
        rows = pl.ds(pl.multiple_of(t * ROWS, ROWS), ROWS)
        after = pl.ds(pl.multiple_of((t + 1) * ROWS, ROWS), ROWS)
        hidden = state[...]

        def gate(q):
            columns = slice(q * width, (q + 1) * width)
            return act_ref[rows, columns] + jnp.dot(hidden, w_s[width:, columns], preferred_element_type=f32)

        in_gate = jax.nn.sigmoid(gate(0))
        forget = jax.nn.sigmoid(gate(1))
        candidate = jnp.tanh(gate(2))
        cell = forget * cell_ref[rows] + in_gate * candidate
        out_gate = jax.nn.sigmoid(gate(3))
        hidden_new = (out_gate * jnp.tanh(cell)).astype(low)
        act_ref[rows, :width] = in_gate
        act_ref[rows, width : 2 * width] = forget
        act_ref[rows, 2 * width : 3 * width] = candidate
        act_ref[rows, 3 * width :] = out_gate
        cell_ref[after] = cell
        h_s[after] = hidden_new
        state[...] = hidden_new
        return carry

    h_s[:ROWS] = jnp.zeros((ROWS, width), low)
    marks = [steps * n // 24 for n in (0, 4, 14, 24)]
    lax.fori_loop(marks[0], marks[1], step, 0)
    mats.stage_one(*line_rest)
    lax.fori_loop(marks[1], marks[2], step, 0)
    mats.stage_two()
    lax.fori_loop(marks[2], marks[3], step, 0)
    turned = h_s[ROWS:].astype(f32).reshape(steps, ROWS, width)
    for u in range(batch):
        value = turned[:, u, :]
        result_s[u] = jnp.where(encoder, seq_s[u].astype(f32) + value, value).astype(low)
    half = batch // 2
    for h in range(2):
        home = jnp.logical_and(mine, core == h)
        source, target = result_s.at[h * half : (h + 1) * half], pair_ref.at[place.role]
        stay = pltpu.make_async_copy(source, target, pair_sem.at[0, h])
        leave = remote(
            source,
            target,
            pair_sem.at[0, h],
            pair_sem.at[1, place.role],
            (h, jnp.where(mine, chip, chip + place.along[1])),
        )
        pl.when(home)(stay.start)
        pl.when(jnp.logical_not(home))(leave.start)
    for q in range(4):
        for n in range(width // TURN):
            rows = slice(width + n * TURN, width + (n + 1) * TURN)
            wt_s[q, :, n * TURN : (n + 1) * TURN] = w_s[rows, q * width : (q + 1) * width].T
    keep_turned = pltpu.make_async_copy(wt_s, wt_out, keep_sem.at[1])
    keep_turned.start()
    ht_ref[width:] = h_s[:-ROWS].T
    mats.stage_three()
    mats.finish()
    thirds.finish()
    outs.finish()
    for h in range(2):
        home = jnp.logical_and(mine, core == h)
        source, target = result_s.at[h * half : (h + 1) * half], pair_ref.at[place.role]
        stay = pltpu.make_async_copy(source, target, pair_sem.at[0, h])
        leave = remote(
            source,
            target,
            pair_sem.at[0, h],
            pair_sem.at[1, place.role],
            (h, jnp.where(mine, chip, chip + place.along[1])),
        )
        pl.when(home)(stay.wait)
        pl.when(jnp.logical_not(home))(leave.wait_send)

    def arrived(section):
        target = pair_ref.at[section]
        remote(target, target, pair_sem.at[0, 0], pair_sem.at[1, section], (1 - core, chip)).wait_recv()

    pl.when(guest)(lambda: arrived(place.role))
    arrived(1 - place.role)
    keep.wait()
    keep_turned.wait()
    for part in matrix:
        part.sent_line()
    for spread in (*matrix, vecs, mats):
        spread.sent_all()


def forward(n_dp, seq, shard, mats_block, out_block, vec_block):
    batch, steps, width = seq.shape
    rows = steps * ROWS
    low, f32 = jnp.bfloat16, jnp.float32
    line, side = DP_LAYOUTS[n_dp][:2]
    columns = mats_block.shape[1]
    dma = pltpu.SemaphoreType.DMA
    return pl.pallas_call(
        functools.partial(forward_kernel, n_dp),
        out_shape=(
            jax.ShapeDtypeStruct((rows, 4 * width), f32),
            jax.ShapeDtypeStruct((rows + ROWS, width), f32),
            jax.ShapeDtypeStruct((2 * width, rows), low),
            jax.ShapeDtypeStruct((steps, ROWS, width), f32),
            jax.ShapeDtypeStruct((steps, ROWS, LANES), f32),
            jax.ShapeDtypeStruct((8, 2 * width), f32),
            jax.ShapeDtypeStruct((2, batch // 2, steps, width), low),
            jax.ShapeDtypeStruct((width, 4 * width), low),
            jax.ShapeDtypeStruct((4, width, width), low),
            jax.ShapeDtypeStruct((2, 2, n_dp, columns, width), low),
            jax.ShapeDtypeStruct((line, columns, width), low),
            jax.ShapeDtypeStruct((line,) + out_block.shape, low),
        ),
        in_specs=[VMEM_SPEC, ANY_SPEC, ANY_SPEC, ANY_SPEC, VMEM_SPEC],
        out_specs=(VMEM_SPEC,) * 7 + (ANY_SPEC,) * 5,
        scratch_shapes=[
            pltpu.VMEM((batch, steps, width), low),
            pltpu.VMEM((batch, steps, width), low),
            pltpu.VMEM((rows, width), low),
            pltpu.VMEM((rows + ROWS, width), low),
            pltpu.VMEM((2 * width, 4 * width), low),
            pltpu.VMEM((4, width, width), low),
            pltpu.VMEM((2, n_dp, 8, LANES), f32),
            pltpu.VMEM((ROWS, width), low),
            dma((2,)),
            dma((3,)),
            dma((2, 2)),
        ]
        + [spread_sems(line, side)] * (4 + CHUNKS),
        compiler_params=pltpu.CompilerParams(
            collective_id=1, has_side_effects=True, vmem_limit_bytes=VMEM_LIMIT
        ),
    )(seq, shard, mats_block, out_block, vec_block)


class Fold:
    def __init__(self, place, part, stage, near, far, sems):
        self.place, self.part, self.stage, self.near, self.far, self.sems = place, part, stage, near, far, sems
        self.sent = []

    def send(self, source, target, device, send, receive):
        copy = remote(source, target, send, receive, device)
        copy.start()
        self.sent.append(copy)

    def arrived(self, target, semaphore):
        place = self.place
        remote(target, target, semaphore, semaphore, (1 - place.core, place.chip)).wait_recv()

    def stage_a(self, *steps):
        place = self.place
        for kz in steps or reversed(range(place.line)):
            for kg in range(1, place.side):
                for kf in reversed(range(place.side)):
                    source = self.stage.at[kg - 1, kf, kz]
                    source[...] = self.part(kz, kf, kg).astype(source.dtype)
                    self.send(
                        source,
                        self.near.at[kg - 1, kf, kz],
                        (place.core, place.chip + place.second[kg]),
                        self.sems["gs"].at[kg, kf, kz],
                        self.sems["gr"].at[kg, kf, kz],
                    )

    def stage_b(self, *steps):
        place = self.place
        for kz in steps or reversed(range(place.line)):
            for kf in reversed(range(place.side)):
                total = self.part(kz, kf, 0)
                for kg in range(1, place.side):
                    self.arrived(self.near.at[kg - 1, kf, kz], self.sems["gr"].at[kg, kf, kz])
                    total = total + self.near[kg - 1, kf, kz].astype(jnp.float32)
                source = self.near.at[0, kf, kz]
                source[...] = total.astype(source.dtype)
                if kf:
                    self.send(
                        source,
                        self.far.at[kf - 1, kz],
                        (place.core, place.chip + place.first[kf]),
                        self.sems["fs"].at[kf, kz],
                        self.sems["fr"].at[kf, kz],
                    )

    def summed(self, kz):
        place = self.place
        total = self.near[0, 0, kz].astype(jnp.float32)
        for kf in range(1, place.side):
            self.arrived(self.far.at[kf - 1, kz], self.sems["fr"].at[kf, kz])
            total = total + self.far[kf - 1, kz].astype(jnp.float32)
        return total.astype(self.far.dtype)

    def sent_all(self):
        for copy in self.sent:
            copy.wait_send()


class FoldLine:
    def __init__(self, place, parts, end, sems):
        self.place, self.parts, self.end, self.sems = place, parts, end, sems

    def begin(self, *steps):
        place = self.place
        for kz in steps or reversed(range(1, place.line)):
            self.copy(kz).start()

    def copy(self, kz):
        place = self.place
        return remote(
            self.parts.at[kz],
            self.end.at[kz - 1],
            self.sems["zs"].at[kz, 0],
            self.sems["zr"].at[kz],
            (place.core, place.chip + place.along[kz]),
        )

    def result(self):
        total = self.parts[0].astype(jnp.float32)
        for kz in range(1, self.place.line):
            self.copy(kz).wait_recv()
            total = total + self.end[kz - 1].astype(jnp.float32)
        return total

    def sent_all(self):
        for kz in range(1, self.place.line):
            self.copy(kz).wait_send()


class FoldRole(Fold):
    def __init__(self, place, part, stage, near, far, end, sems):
        super().__init__(place, part, stage, near, far, sems)
        self.end = end

    def stage_c(self, kz):
        place = self.place
        source = self.far.at[0, kz]
        source[...] = self.summed(kz)
        if kz:
            self.send(
                source,
                self.end.at[place.core, kz // 2],
                (place.role, place.chip + place.along[kz]),
                self.sems["zs"].at[kz, 0],
                self.sems["er"].at[place.core, kz // 2],
            )
        else:
            self.last = source
            self.cross = remote(
                source,
                self.end.at[place.core, 0],
                self.sems["zs"].at[0, 0],
                self.sems["er"].at[place.core, 0],
                (1 - place.core, place.chip),
            )

            @pl.when(place.core != place.role)
            def _():
                self.cross.start()

    def result(self, sum_ref):
        place = self.place
        rows, half = self.end.shape[2:]
        mine = place.core == place.role

        def columns(core):
            return pl.ds(pl.multiple_of(core * half, half), half)

        def add(parity):
            sources = [kz for kz in range(place.line) if kz % 2 == parity]
            for core in range(2):
                total = jnp.zeros((rows, half), jnp.float32)
                for kz in sources:
                    if kz:
                        self.arrived(self.end.at[core, kz // 2], self.sems["er"].at[core, kz // 2])
                        total = total + self.end[core, kz // 2].astype(jnp.float32)
                sum_ref[:, core * half : (core + 1) * half] = total

        @pl.when(mine)
        def _():
            add(0)
            own, other = columns(place.core), columns(1 - place.core)
            sum_ref[:, own] += self.last[...].astype(jnp.float32)
            self.arrived(self.end.at[1 - place.core, 0], self.sems["er"].at[1 - place.core, 0])
            sum_ref[:, other] += self.end[1 - place.core, 0].astype(jnp.float32)

        @pl.when(jnp.logical_not(mine))
        def _():
            add(1)
            self.cross.wait_send()


def fold_sems(line, side):
    dma = pltpu.SemaphoreType.DMA
    return {
        "gs": dma((side, side, line)),
        "gr": dma((side, side, line)),
        "fs": dma((side, line)),
        "fr": dma((side, line)),
        "zs": dma((line, 1)),
        "zr": dma((line,)),
        "er": dma((2, line // 2)),
    }


def fold_buffers(line, side, shape, dtype):
    return [
        pltpu.VMEM((side - 1, side, line) + shape, dtype),
        pltpu.VMEM((side - 1, side, line) + shape, dtype),
    ]


def attention_kernel(
    n_dp,
    frames_ref,
    labels_ref,
    mem_ref,
    dec_ref,
    cot_ref,
    vec_ref,
    pairs_any,
    third_line,
    out_line,
    dz_ref,
    dq_ref,
    dk_ref,
    dvec_ref,
    logits_ref,
    outer_ref,
    third_part,
    out_part,
    squash_ref,
    context_ref,
    ddec_ref,
    cot_s,
    gl_f,
    gl_ref,
    own_logits,
    mats_ref,
    third_s,
    out_s,
    back_s,
    facts,
    facts_gl,
    g_third,
    g_out,
    t_stage,
    t_near,
    o_stage,
    o_near,
    t_far,
    o_far,
    q_s,
    k_s,
    mem_s,
    ctx_s,
    dqa_s,
    dka_s,
    e_s,
    sel_s,
    prob_s,
    sel_d,
    prob_d,
    reach_d,
    back_d,
    w_s,
    a_s,
    own_s,
    nxt_s,
    g_s,
    d_s,
    d_rows,
    bc_s,
    load_sem,
    cot_sems,
    fact_sems,
    logit_sems,
    back_sems,
    sems_t,
    sems_o,
    sems_ft,
    sems_fo,
):
    rows, width = dec_ref.shape
    utts = frames_ref.shape[0]
    length = rows // utts
    vocab_half = cot_ref.shape[2]
    vocab_pad = gl_f.shape[2]
    low = jnp.bfloat16
    f32 = jnp.float32
    lane = lax.broadcasted_iota(jnp.int32, (length, LANES), 1)
    lane_block = lax.broadcasted_iota(jnp.int32, (length, 8, LANES), 2)

    place = Place(n_dp)
    core, chip = place.core, place.chip
    other = (1 - core, chip)
    load = pltpu.make_async_copy(pairs_any, mats_ref, load_sem)
    load.start()
    place.greet()
    third = spread_line(place, third_line, third_s, sems_t)
    outs = spread_line(place, out_line, out_s, sems_o)
    third.begin()
    outs.begin()
    cot_away = remote(
        cot_ref.at[pl.ds((1 - core) * utts, utts)], cot_s, cot_sems.at[0], cot_sems.at[1], other
    )
    cot_away.start()
    third.stage_one()
    outs.stage_one()
    load.wait()
    q_s[...] = contract(dec_ref[...], mats_ref[0], 1, 1) + vec_ref[5:6]
    k_s[...] = contract(mem_ref[...], mats_ref[1], 1, 1)
    mem_s[...] = mem_ref[...].astype(f32)
    e_s[...] = jnp.zeros_like(e_s)
    d_s[...] = jnp.zeros_like(d_s)

    tile = 256
    group = 4

    gl_f[...] = jnp.zeros_like(gl_f)
    cot_away.wait()
    slot = lax.broadcasted_iota(jnp.int32, (length, 1), 0)
    for u in range(utts):
        keep = (slot < labels_ref[u]).astype(f32)
        at = slice(u * length, (u + 1) * length)
        gl_f[core, at, :vocab_half] = cot_ref[core * utts + u].astype(f32) * keep
        gl_f[1 - core, at, :vocab_half] = cot_s[u].astype(f32) * keep
    gl_ref[...] = gl_f[...].astype(low)

    for u in range(utts):
        at = u * length
        if u == utts // 2:
            third.stage_two()
            outs.stage_two()

        def energy_step(block, sums, at=at):
            base = block * group
            for offset in range(group):
                j = base + offset
                row = k_s[pl.ds(at + j, 1), :]
                for head in range(2):
                    total = jnp.zeros((length, LANES), f32)
                    for c in range(width // LANES):
                        columns = slice(head * width + c * LANES, head * width + (c + 1) * LANES)
                        total = total + jnp.tanh(
                            q_s[at : at + length, columns] + row[:, columns]
                        ) * vec_ref[6:7, columns]
                    value = jnp.sum(total, -1, keepdims=True)
                    sums = tuple(
                        jnp.where(lane == j, value, s) if h == head else s
                        for h, s in enumerate(sums)
                    )
            return sums

        blocks = length // group
        zero = jnp.zeros((length, LANES), f32)
        mono, window = lax.fori_loop(0, blocks, energy_step, (zero, zero))
        e_s[0, :, u, :] = mono
        e_s[1, :, u, :] = window

    mask = jnp.zeros((8, LANES), f32)
    row_u = lax.broadcasted_iota(jnp.int32, (8, LANES), 0)
    lane_u = lax.broadcasted_iota(jnp.int32, (8, LANES), 1)
    for u in range(utts):
        inside_u = jnp.logical_and(row_u == u, lane_u < frames_ref[u])
        mask = jnp.where(inside_u, 1.0, mask)
    mask = mask[None]
    third.stage_three()
    outs.stage_three()
    mono = e_s[0] + ENERGY_OFFSET
    window = e_s[1]
    chosen = jax.nn.sigmoid(mono)
    inside = (lane_block < length).astype(f32)
    sel_s[...] = chosen * mask
    leave = (jnp.maximum(mono, 0.0) + jnp.log1p(jnp.exp(-jnp.abs(mono)))) * mask
    prob = jnp.exp(-leave) * inside
    prob_s[...] = prob

    def right(value, distance):
        return pltpu.roll(value, distance, value.ndim - 1)

    def left(value, distance):
        return pltpu.roll(value, LANES - distance, value.ndim - 1)

    diagonals = 2 * length - 1
    bits = [2**n for n in range(5)]

    def skewed(value):
        value = jnp.concatenate([value, jnp.zeros((diagonals - length, 8, LANES), f32)], 0)
        for bit in bits:
            moved = jnp.concatenate([jnp.zeros((bit, 8, LANES), f32), value[:-bit]], 0)
            value = jnp.where(lane_row & bit != 0, moved, value)
        return value

    def straight(value):
        for bit in bits:
            moved = jnp.concatenate([value[bit:], jnp.zeros((bit, 8, LANES), f32)], 0)
            value = jnp.where(lane_row & bit != 0, moved, value)
        return value[:length]

    lane_row = lax.broadcasted_iota(jnp.int32, (8, LANES), 1)
    sel_d[...] = skewed(sel_s[...])
    prob_d[...] = skewed(jnp.where(lane_block < length - 1, prob, 0.0))

    def align_step(d, total):
        reach_d[d] = total
        return sel_d[d] * total + right(prob_d[d] * total, 1)

    lax.fori_loop(0, diagonals, align_step, jnp.where(lane_row == 0, 1.0, 0.0).astype(f32))
    w_s[...] = straight(reach_d[...])
    a_s[...] = sel_s[...] * w_s[...]

    aligned = a_s[...]
    own = jnp.where(lane_block == 0, 1.0, jax.nn.sigmoid(window - right(window, 1)))
    nxt = jax.nn.sigmoid(window - left(window, 1))
    own_s[...] = own
    nxt_s[...] = nxt
    beta = aligned * own + jnp.where(lane_block < length - 1, left(aligned, 1), 0.0) * nxt
    g_s[...] = beta

    for u in range(utts):
        at = u * length
        weights = g_s[:, u, :].astype(low)[:, :length]
        ctx_s[at : at + length] = jnp.dot(
            weights, mem_s[at : at + length].astype(low), preferred_element_type=f32
        )
    context_ref[...] = ctx_s[...].astype(low)

    third.finish()
    outs.finish()
    third_low, third_high = (third_s[s].reshape(width, width) for s in range(2))
    squash = jnp.tanh(
        jnp.dot(dec_ref[...], third_low, preferred_element_type=f32)
        + jnp.dot(context_ref[...], third_high, preferred_element_type=f32)
        + vec_ref[7:8, :width]
    )
    squash_ref[...] = squash.astype(low)
    pull = contract(gl_ref[0], out_s[0].reshape(width, vocab_pad), 1, 1) + contract(
        gl_ref[1], out_s[1].reshape(width, vocab_pad), 1, 1
    )
    dz = (pull * (1.0 - squash * squash)).astype(low)
    dz_ref[...] = dz
    sources = [dec_ref, context_ref, dz_ref, squash_ref]
    handed = [
        remote(source, facts.at[n], fact_sems.at[0, n], fact_sems.at[1, n], other)
        for n, source in enumerate(sources)
    ]
    handed.append(remote(gl_ref.at[1 - core], facts_gl, fact_sems.at[0, 4], fact_sems.at[1, 4], other))
    for copy in handed:
        copy.start()
    dvec_ref[...] = jnp.zeros_like(dvec_ref)
    dvec_ref[7:8, :width] = jnp.sum(dz.astype(f32), 0, keepdims=True)
    for h in range(2):
        begin = width + h * vocab_half
        row = jnp.concatenate(
            [
                jnp.sum(gl_f[h], 0, keepdims=True),
                jnp.zeros((1, 2 * width - vocab_pad), f32),
            ],
            -1,
        )
        dvec_ref[7:8] += pltpu.roll(row, begin, 1)
        bias = pltpu.roll(vec_ref[7:8], 2 * width - begin, 1)[:, :vocab_pad]
        own_logits[h] = (
            jnp.dot(squash_ref[...], out_s[h].reshape(width, vocab_pad), preferred_element_type=f32) + bias
        ).astype(low)
    logits_kept = pltpu.make_async_copy(own_logits.at[core], logits_ref.at[core], logit_sems.at[0])
    logits_away = remote(
        own_logits.at[1 - core], logits_ref.at[core], logit_sems.at[1], logit_sems.at[2], other
    )
    logits_kept.start()
    logits_away.start()
    ddec_ref[...] = contract(dz, third_low, 1, 1)
    ctx_s[...] = contract(dz, third_high, 1, 1).astype(low).astype(f32)

    pad = jnp.zeros((length, LANES - length), f32)
    for u in range(utts):
        at = u * length
        weights = g_s[:, u, :].astype(low)[:, :length]
        pulled = ctx_s[at : at + length].astype(low)
        beta_grad = contract(pulled, mem_s[at : at + length].astype(low), 1, 1)
        e_s[0, :, u, :] = jnp.concatenate([beta_grad, pad], -1)
        mem_s[at : at + length] = contract(weights, pulled, 0, 0)

    for copy in handed:
        copy.wait_recv()
    joined = jnp.where(core == 0, dec_ref[...], context_ref[...])
    joined_other = jnp.where(core == 0, facts[0], facts[1])
    part_rows, out_rows = g_third.shape[1], g_out.shape[1]
    total = (contract(joined, dz_ref[...], 0, 0) + contract(joined_other, facts[2], 0, 0)).astype(low)
    for block in range(n_dp):
        g_third[block] = total[block * part_rows : (block + 1) * part_rows]
    total = (contract(squash_ref[...], gl_ref[core], 0, 0) + contract(facts[3], facts_gl[...], 0, 0)).astype(low)
    for block in range(n_dp):
        g_out[block] = total[block * out_rows : (block + 1) * out_rows]
    third_fold = Fold(
        place, lambda kz, kf, kg: g_third[place.block(kz, kf, kg)].astype(f32), t_stage, t_near, t_far, sems_ft
    )
    out_fold = Fold(
        place, lambda kz, kf, kg: g_out[place.block(kz, kf, kg)].astype(f32), o_stage, o_near, o_far, sems_fo
    )
    third_fold.stage_a()
    out_fold.stage_a()

    beta_grad = e_s[0]
    own = own_s[...]
    nxt = nxt_s[...]
    g_s[...] = beta_grad * own + jnp.where(lane_block >= 1, right(beta_grad * nxt, 1), 0.0)
    aligned = a_s[...]
    from_own = jnp.where(lane_block >= 1, beta_grad * aligned * own * (1.0 - own), 0.0)
    from_next = (
        beta_grad
        * jnp.where(lane_block < length - 1, left(aligned, 1), 0.0)
        * nxt
        * (1.0 - nxt)
    )
    d_s[1] = (from_own - left(from_own, 1) + from_next - right(from_next, 1)) * inside

    prob = prob_s[...]
    reach_d[...] = skewed(g_s[...])

    def retreat_step(k, after):
        d = diagonals - 1 - k
        grad_align = reach_d[d] + after
        total = sel_d[d] * grad_align + prob_d[d] * left(after, 1)
        reach_d[d] = grad_align
        back_d[d] = total
        return total

    lax.fori_loop(0, diagonals, retreat_step, jnp.zeros((8, LANES), f32))
    e_s[0] = straight(reach_d[...])
    e_s[1] = straight(back_d[...])
    reached = w_s[...]
    grad_select = reached * e_s[0]
    grad_prob = reached * jnp.where(lane_block < length - 1, left(e_s[1], 1), 0.0)
    chosen = sel_s[...]
    d_s[0] = grad_select * chosen * (1.0 - chosen) - grad_prob * prob * chosen

    dka_s[...] = jnp.zeros_like(dka_s)
    spots = lax.broadcasted_iota(jnp.int32, (LANES, length * LANES), 1) // LANES
    picks = (lax.broadcasted_iota(jnp.int32, (LANES, length * LANES), 0) == spots).astype(f32)
    for head in range(2):
        for u in range(utts):
            d_rows[u * length : (u + 1) * length] = d_s[head, :, u, :]
        bc_s[head] = jnp.dot(
            d_rows[...], picks, precision=lax.Precision.HIGHEST, preferred_element_type=f32
        )

    def energy_back(u, dvec):
        at = pl.multiple_of(u * length, 8)
        count = length // UNROLL
        for c in range(2 * width // tile):
            columns = slice(c * tile, (c + 1) * tile)
            head = c * tile // width
            q_now = q_s[pl.ds(at, length), columns]

            def back_step(block, sums, head=head, columns=columns, q_now=q_now):
                dq, dw = sums
                for offset in range(UNROLL):
                    j = block * UNROLL + offset
                    squash_all = jnp.tanh(q_now + k_s[pl.ds(at + j, 1), columns])
                    grad = bc_s[head, pl.ds(at, length), pl.ds(pl.multiple_of(j * LANES, LANES), LANES)]
                    grad = jnp.concatenate([grad] * (tile // LANES), -1)
                    scaled = grad * squash_all
                    dw = dw + scaled
                    moved = grad - scaled * squash_all
                    dq = dq + moved
                    dka_s[pl.ds(at + j, 1), columns] = jnp.sum(moved, 0, keepdims=True)
                return (dq, dw)

            zero = jnp.zeros((length, tile), f32)
            dq, dw = lax.fori_loop(0, count, back_step, (zero, zero))
            dq = dq * vec_ref[6:7, columns]
            dqa_s[pl.ds(at, length), columns] = dq
            dvec_ref[5:6, columns] += jnp.sum(dq, 0, keepdims=True)
            dvec_ref[6:7, columns] += jnp.sum(dw, 0, keepdims=True)
        return dvec

    lax.fori_loop(0, utts // 2, energy_back, 0)
    third_fold.stage_b()
    out_fold.stage_b()
    lax.fori_loop(utts // 2, utts, energy_back, 0)
    for h in range(2):
        columns = slice(h * width, (h + 1) * width)
        dq_ref[h] = dqa_s[:, columns].astype(low)
        dk_ref[h] = (dka_s[:, columns] * vec_ref[6:7, columns]).astype(low)
        ddec_ref[...] += jnp.dot(dq_ref[h], mats_ref[0, columns], preferred_element_type=f32)
        mem_s[...] += jnp.dot(dk_ref[h], mats_ref[1, columns], preferred_element_type=f32)
    for u in range(utts):
        at = slice(u * length, (u + 1) * length)
        back_s[0, u] = mem_s[at].astype(low)
        back_s[1, u] = ddec_ref[at].astype(low)
    role = place.role
    mine = core == role
    guest = jnp.logical_not(mine)
    stay = pltpu.make_async_copy(back_s.at[role], outer_ref.at[core], back_sems.at[0, 0])
    cross = remote(back_s.at[role], outer_ref.at[core], back_sems.at[0, 0], back_sems.at[1, core], (role, chip))
    away = remote(
        back_s.at[1 - role],
        outer_ref.at[core],
        back_sems.at[0, 1],
        back_sems.at[1, core],
        (role, chip + place.along[1]),
    )
    away.start()
    pl.when(mine)(stay.start)
    pl.when(guest)(cross.start)
    for kz in range(place.line):
        third_part[kz] = third_fold.summed(kz)
        out_part[kz] = out_fold.summed(kz)
    logits_kept.wait()
    logits_away.wait()
    for copy in handed:
        copy.wait_send()
    away.wait_send()
    pl.when(mine)(stay.wait)
    pl.when(guest)(cross.wait_send)

    def arrived(slot):
        target = outer_ref.at[slot]
        remote(target, target, back_sems.at[0, 0], back_sems.at[1, slot], other).wait_recv()

    arrived(1 - core)
    pl.when(guest)(lambda: arrived(core))
    for moved in (third, outs, third_fold, out_fold):
        moved.sent_all()


def attention(n_dp, frames, labels, memory, decoded, cotangent, vectors, pairs, third_line, out_line):
    rows, width = decoded.shape
    utts = frames.shape[0]
    length = rows // utts
    low, f32 = jnp.bfloat16, jnp.float32
    line, side = DP_LAYOUTS[n_dp][:2]
    third_block, out_block = third_line.shape[1:], out_line.shape[1:]
    vocab_half, vocab_pad = cotangent.shape[2], out_block[1]
    small = (length, 8, LANES)
    diagonal = (2 * length - 1, 8, LANES)
    dma = pltpu.SemaphoreType.DMA
    return pl.pallas_call(
        functools.partial(attention_kernel, n_dp),
        out_shape=(
            jax.ShapeDtypeStruct((rows, width), low),
            jax.ShapeDtypeStruct((2, rows, width), low),
            jax.ShapeDtypeStruct((2, rows, width), low),
            jax.ShapeDtypeStruct((8, 2 * width), f32),
            jax.ShapeDtypeStruct((2, rows, vocab_pad), low),
            jax.ShapeDtypeStruct((2, utts, length, width), low),
            jax.ShapeDtypeStruct((line,) + third_block, low),
            jax.ShapeDtypeStruct((line,) + out_block, low),
        ),
        in_specs=[SMEM_SPEC] * 2 + [VMEM_SPEC] * 4 + [ANY_SPEC] * 3,
        out_specs=(VMEM_SPEC,) * 8,
        scratch_shapes=[
            pltpu.VMEM((rows, width), low),
            pltpu.VMEM((rows, width), low),
            pltpu.VMEM((rows, width), f32),
            pltpu.VMEM((utts, length, vocab_half), low),
            pltpu.VMEM((2, rows, vocab_pad), f32),
            pltpu.VMEM((2, rows, vocab_pad), low),
            pltpu.VMEM((2, rows, vocab_pad), low),
            pltpu.VMEM((2, 2 * width, width), low),
            pltpu.VMEM((2, n_dp) + third_block, low),
            pltpu.VMEM((2, n_dp) + out_block, low),
            pltpu.VMEM((2, utts, length, width), low),
            pltpu.VMEM((4, rows, width), low),
            pltpu.VMEM((rows, vocab_pad), low),
            pltpu.VMEM((n_dp,) + third_block, low),
            pltpu.VMEM((n_dp,) + out_block, low),
        ]
        + fold_buffers(line, side, third_block, low)
        + fold_buffers(line, side, out_block, low)
        + [pltpu.VMEM((side - 1, line) + block, low) for block in (third_block, out_block)]
        + [
            pltpu.VMEM((rows, 2 * width), f32),
            pltpu.VMEM((rows, 2 * width), f32),
            pltpu.VMEM((rows, width), f32),
            pltpu.VMEM((rows, width), f32),
            pltpu.VMEM((rows, 2 * width), f32),
            pltpu.VMEM((rows, 2 * width), f32),
            pltpu.VMEM((2,) + small, f32),
            pltpu.VMEM(small, f32),
            pltpu.VMEM(small, f32),
            pltpu.VMEM(diagonal, f32),
            pltpu.VMEM(diagonal, f32),
            pltpu.VMEM(diagonal, f32),
            pltpu.VMEM(diagonal, f32),
            pltpu.VMEM(small, f32),
            pltpu.VMEM(small, f32),
            pltpu.VMEM(small, f32),
            pltpu.VMEM(small, f32),
            pltpu.VMEM(small, f32),
            pltpu.VMEM((2,) + small, f32),
            pltpu.VMEM((rows, LANES), f32),
            pltpu.VMEM((2, rows, length * LANES), f32),
            dma,
            dma((2,)),
            dma((2, 5)),
            dma((3,)),
            dma((2, 2)),
        ]
        + [spread_sems(line, side)] * 2
        + [fold_sems(line, side)] * 2,
        compiler_params=pltpu.CompilerParams(
            collective_id=2, has_side_effects=True, vmem_limit_bytes=VMEM_LIMIT
        ),
    )(frames, labels, memory, decoded, cotangent, vectors, pairs, third_line, out_line)


def backward_kernel(
    n_dp,
    act_ref,
    cell_ref,
    outer_ref,
    dq_ref,
    dk_ref,
    dec_ref,
    mem_ref,
    wt_any,
    ht_ref,
    dpre_ref,
    dpre_other,
    ht_other,
    mats_part,
    wt_ref,
    outer_s,
    state,
    held,
    facts,
    g_mats,
    m_stage,
    m_near,
    m_far,
    load_sem,
    fact_sems,
    pre_sems,
    ht_sems,
    sems_m,
):
    halves, half, steps, width = outer_ref.shape
    low, f32 = jnp.bfloat16, jnp.float32
    place = Place(n_dp)
    load = pltpu.make_async_copy(wt_any, wt_ref, load_sem)
    load.start()
    place.greet()
    core = place.core
    other = (1 - core, place.chip)
    sources = [dq_ref.at[1 - core], dk_ref.at[1 - core], dec_ref, mem_ref]
    handed = [
        remote(source, facts.at[n], fact_sems.at[0, n], fact_sems.at[1, n], other)
        for n, source in enumerate(sources)
    ]
    handed.append(remote(ht_ref, ht_other, ht_sems.at[0], ht_sems.at[1], other))
    for copy in handed:
        copy.start()
    state[...] = jnp.zeros_like(state)
    held[...] = jnp.zeros_like(held)
    outer_s[:, halves * half :] = jnp.zeros((steps, ROWS - halves * half, width), f32)
    for u in range(halves * half):
        outer_s[:, u, :] = outer_ref[u // half, u % half].astype(f32)

    def step(k, carry):
        t = steps - 1 - k
        rows = pl.ds(pl.multiple_of(t * ROWS, ROWS), ROWS)
        after = pl.ds(pl.multiple_of((t + 1) * ROWS, ROWS), ROWS)
        hidden_total = outer_s[t]
        for q in range(4):
            hidden_total = hidden_total + jnp.dot(
                state[:, q * width : (q + 1) * width], wt_ref[q], preferred_element_type=f32
            )
        in_gate = act_ref[rows, :width]
        forget = act_ref[rows, width : 2 * width]
        candidate = act_ref[rows, 2 * width : 3 * width]
        out_gate = act_ref[rows, 3 * width :]
        squash = jnp.tanh(cell_ref[after])
        cell_total = held[...] + hidden_total * out_gate * (1.0 - squash * squash)
        held[...] = cell_total * forget
        grads = jnp.concatenate(
            [
                cell_total * candidate * in_gate * (1.0 - in_gate),
                cell_total * cell_ref[rows] * forget * (1.0 - forget),
                cell_total * in_gate * (1.0 - candidate * candidate),
                hidden_total * squash * out_gate * (1.0 - out_gate),
            ],
            -1,
        ).astype(low)
        state[...] = grads
        dpre_ref[rows] = grads
        return carry

    shares = 4
    share = steps // shares

    def hand_over(n):
        top = (steps - (n + 1) * share) * ROWS
        rows = slice(top, top + share * ROWS)
        columns = pl.ds(pl.multiple_of((1 - core) * 2 * width, 2 * width), 2 * width)
        copy = remote(
            dpre_ref.at[rows, columns], dpre_other.at[rows, :], pre_sems.at[0, n], pre_sems.at[1, n], other
        )
        copy.start()
        handed.append(copy)

    part_rows = g_mats.shape[1] // 2

    def matrices():
        for copy in handed[:4]:
            copy.wait_recv()
        pairs = [
            (dq_ref[core], dec_ref[...], facts[0], facts[2]),
            (dk_ref[core], mem_ref[...], facts[1], facts[3]),
        ]
        for m, (a, b, c, d) in enumerate(pairs):
            total = (contract(a, b, 0, 0) + contract(c, d, 0, 0)).astype(low)
            for block in range(n_dp):
                g_mats[block, m * part_rows : (m + 1) * part_rows] = total[
                    block * part_rows : (block + 1) * part_rows
                ]

    mats = Fold(
        place, lambda kz, kf, kg: g_mats[place.block(kz, kf, kg)].astype(f32), m_stage, m_near, m_far, sems_m
    )
    matrices()
    mats.stage_a()
    load.wait()
    lines = list(reversed(range(place.line)))
    lax.fori_loop(0, share, step, 0)
    hand_over(0)
    lax.fori_loop(share, 2 * share, step, 0)
    hand_over(1)
    mats.stage_b(*lines[: place.line // 2])
    lax.fori_loop(2 * share, 3 * share, step, 0)
    hand_over(2)
    mats.stage_b(*lines[place.line // 2 :])
    lax.fori_loop(3 * share, steps, step, 0)
    hand_over(3)
    for kz in lines:
        mats_part[kz] = mats.summed(kz)
    for copy in handed[4:]:
        copy.wait_recv()
    for copy in handed:
        copy.wait_send()
    mats.sent_all()


def backward(n_dp, act, cell, outer, dq, dk, decoded, memory, weight_t, ht):
    rows = act.shape[0]
    steps, width = outer.shape[2:]
    low, f32 = jnp.bfloat16, jnp.float32
    line, side = DP_LAYOUTS[n_dp][:2]
    utt_rows = decoded.shape[0]
    mats_block = (2 * width // n_dp, width)
    dma = pltpu.SemaphoreType.DMA
    return pl.pallas_call(
        functools.partial(backward_kernel, n_dp),
        out_shape=(
            jax.ShapeDtypeStruct((rows, 4 * width), low),
            jax.ShapeDtypeStruct((rows, 2 * width), low),
            jax.ShapeDtypeStruct(ht.shape, low),
            jax.ShapeDtypeStruct((line,) + mats_block, low),
        ),
        in_specs=[VMEM_SPEC] * 7 + [ANY_SPEC] * 2,
        out_specs=(VMEM_SPEC, VMEM_SPEC, ANY_SPEC, VMEM_SPEC),
        scratch_shapes=[
            pltpu.VMEM((4, width, width), low),
            pltpu.VMEM((steps, ROWS, width), f32),
            pltpu.VMEM((ROWS, 4 * width), low),
            pltpu.VMEM((ROWS, width), f32),
            pltpu.VMEM((4, utt_rows, width), low),
            pltpu.VMEM((n_dp,) + mats_block, low),
        ]
        + fold_buffers(line, side, mats_block, low)
        + [pltpu.VMEM((side - 1, line) + mats_block, low)]
        + [dma, dma((2, 4)), dma((2, 4)), dma((2,))]
        + [fold_sems(line, side)],
        compiler_params=pltpu.CompilerParams(
            collective_id=3, has_side_effects=True, vmem_limit_bytes=VMEM_LIMIT
        ),
    )(act, cell, outer, dq, dk, decoded, memory, weight_t, ht)


def update_kernel(
    n_dp,
    batch,
    ht_ref,
    ht_other,
    dpre_ref,
    dpre_other,
    w_ref,
    base_ref,
    spread_ref,
    outer_ref,
    vectors_ref,
    dvec_ref,
    mats_part,
    third_part,
    out_part,
    sum_ref,
    gin_ref,
    vec_sum,
    mats_sum,
    third_sum,
    out_sum,
    w_s,
    gin_s,
    gin_u,
    vec_s,
    vec_other,
    vec_parts,
    l_stage,
    l_near,
    v_stage,
    v_near,
    l_far,
    l_end,
    v_far,
    v_parts,
    v_end,
    m_end,
    t_end,
    o_end,
    w_sem,
    gin_sems,
    vec_sems,
    sems_l,
    sems_v,
    sems_m,
    sems_t,
    sems_o,
):
    width = base_ref.shape[1]
    steps = base_ref.shape[0] // ROWS
    low, f32 = jnp.bfloat16, jnp.float32
    place = Place(n_dp)
    load = pltpu.make_async_copy(w_ref, w_s, w_sem)
    load.start()
    place.greet()
    core = place.core
    encoder = place.role == 0
    mine = core == place.role
    block_rows = sum_ref.shape[0]
    half = pl.ds(pl.multiple_of(core * 2 * width, 2 * width), 2 * width)

    def part(kz, kf, kg):
        rows = pl.ds(pl.multiple_of(place.block(kz, kf, kg) * block_rows, block_rows), block_rows)
        return jnp.dot(ht_ref[rows], dpre_ref[:, half], preferred_element_type=f32) + jnp.dot(
            ht_other[rows], dpre_other[...], preferred_element_type=f32
        )

    matrix = FoldRole(place, part, l_stage, l_near, l_far, l_end, sems_l)
    mats = FoldLine(place, mats_part, m_end, sems_m)
    third = FoldLine(place, third_part, t_end, sems_t)
    outs = FoldLine(place, out_part, o_end, sems_o)
    matrix.stage_a()
    mats.begin()
    third.begin()
    outs.begin()

    load.wait()
    gin_s[...] = contract(dpre_ref[...], w_s[...], 1, 1)
    input_grad = gin_s[...]
    scaled = base_ref[...]
    vec_s[...] = dvec_ref[...]
    vec_s[4:5, :width] = jnp.where(encoder, jnp.sum(input_grad * scaled, 0, keepdims=True), 0.0)
    vec_s[4:5, width:] = jnp.where(encoder, jnp.sum(input_grad, 0, keepdims=True), 0.0)
    for q in range(4):
        columns = slice((q % 2) * width, (q % 2 + 1) * width)
        bias = jnp.sum(dpre_ref[:, q * width : (q + 1) * width].astype(f32), 0, keepdims=True)
        for role in range(2):
            row = 2 * role + q // 2
            vec_s[row : row + 1, columns] = jnp.where(place.role == role, bias, 0.0)

    @pl.when(encoder)
    def _():
        grads = gin_s[...] * vectors_ref[4:5, :width]
        values = base_ref[...]
        gin_s[...] = (
            spread_ref[:, :1]
            * (
                grads
                - jnp.mean(grads, -1, keepdims=True)
                - values * jnp.mean(grads * values, -1, keepdims=True)
            )
        )

    turned = gin_s[...].reshape(steps, ROWS, width)
    half_batch = batch // 2
    for u in range(batch):
        straight = outer_ref[u // half_batch, u % half_batch].astype(f32)
        gin_u[u] = turned[:, u, :] + jnp.where(encoder, straight, 0.0)
    kept = pltpu.make_async_copy(gin_u, gin_ref, gin_sems.at[0])
    handed = remote(gin_u, gin_ref, gin_sems.at[1], gin_sems.at[2], (1 - core, place.chip + place.along[1]))

    @pl.when(mine)
    def _():
        kept.start()

    @pl.when(jnp.logical_not(mine))
    def _():
        handed.start()

    own_half = pl.ds(pl.multiple_of(core * width, width), width)
    other_half = pl.ds(pl.multiple_of((1 - core) * width, width), width)
    trade = remote(
        vec_s.at[:, other_half], vec_other, vec_sems.at[0], vec_sems.at[1], (1 - core, place.chip)
    )
    trade.start()
    trade.wait_recv()
    total = vec_s[:, own_half] + vec_other[...]
    piece = width // n_dp
    per_tile = LANES // piece
    for block in range(n_dp):
        tile = total[:, (block // per_tile) * LANES : (block // per_tile + 1) * LANES]
        turn = (block % per_tile) * piece
        vec_parts[block] = pltpu.roll(tile, LANES - turn, 1) if turn else tile
    vecs = Fold(place, lambda kz, kf, kg: vec_parts[place.block(kz, kf, kg)], v_stage, v_near, v_far, sems_v)
    vec_line = FoldLine(place, v_parts, v_end, sems_v)
    vecs.stage_a()
    lines = list(reversed(range(place.line)))
    matrix.stage_b(lines[0])
    for n, kz in enumerate(lines[1:]):
        if n == place.line // 2 - 1:
            vecs.stage_b()
        matrix.stage_b(kz)
        matrix.stage_c(lines[n])
    for n in lines:
        v_parts[n] = vecs.summed(n)
    vec_line.begin()
    matrix.stage_c(lines[-1])
    mats_sum[...] = mats.result()
    third_sum[...] = third.result()
    out_sum[...] = outs.result()
    vec_sum[...] = vec_line.result()
    matrix.result(sum_ref)

    @pl.when(mine)
    def _():
        kept.wait()

    @pl.when(jnp.logical_not(mine))
    def _():
        handed.wait()

    trade.wait_send()
    for fold in (matrix, vecs, vec_line, mats, third, outs):
        fold.sent_all()


def update(n_dp, batch, ht, ht_other, dpre, dpre_other, weight, base, spread, outer, vectors, dvec, *parts):
    rows, width = base.shape
    steps = rows // ROWS
    low, f32 = jnp.bfloat16, jnp.float32
    line, side = DP_LAYOUTS[n_dp][:2]
    block_rows = 2 * width // n_dp
    block = (block_rows, 2 * width)
    dma = pltpu.SemaphoreType.DMA
    return pl.pallas_call(
        functools.partial(update_kernel, n_dp, batch),
        out_shape=(
            jax.ShapeDtypeStruct((block_rows, 4 * width), f32),
            jax.ShapeDtypeStruct((batch, steps, width), f32),
            jax.ShapeDtypeStruct((8, LANES), f32),
        )
        + tuple(jax.ShapeDtypeStruct(part.shape[1:], f32) for part in parts),
        in_specs=[VMEM_SPEC] * 4 + [ANY_SPEC] + [VMEM_SPEC] * 8,
        out_specs=(VMEM_SPEC, ANY_SPEC) + (VMEM_SPEC,) * 4,
        scratch_shapes=[
            pltpu.VMEM((width, 4 * width), low),
            pltpu.VMEM((rows, width), f32),
            pltpu.VMEM((batch, steps, width), f32),
            pltpu.VMEM((8, 2 * width), f32),
            pltpu.VMEM((8, width), f32),
            pltpu.VMEM((n_dp, 8, LANES), f32),
        ]
        + fold_buffers(line, side, block, low)
        + fold_buffers(line, side, (8, LANES), f32)
        + [
            pltpu.VMEM((side - 1, line) + block, low),
            pltpu.VMEM((2, line // 2) + block, low),
            pltpu.VMEM((side - 1, line, 8, LANES), f32),
            pltpu.VMEM((line, 8, LANES), f32),
            pltpu.VMEM((line - 1, 8, LANES), f32),
        ]
        + [pltpu.VMEM((line - 1,) + part.shape[1:], low) for part in parts]
        + [dma, dma((3,)), dma((2,))]
        + [fold_sems(line, side)] * 5,
        compiler_params=pltpu.CompilerParams(
            collective_id=4, has_side_effects=True, vmem_limit_bytes=VMEM_LIMIT
        ),
    )(ht, ht_other, dpre, dpre_other, weight, base, spread, outer, vectors, dvec, *parts)


STEP = 5
BETA_ONE = 0.9
BETA_TWO = 0.999
ADAM_EPS = 1e-08
WEIGHT_DECAY = 0.01
RATE_LSTM = 0.05
RATE_MATRIX = 0.02
RATE_VECTOR = 0.3


def adamw(master, first, second, grad, rate):
    first_new = BETA_ONE * first + (1.0 - BETA_ONE) * grad
    second_new = BETA_TWO * second + (1.0 - BETA_TWO) * grad * grad
    first_hat = first_new / (1.0 - BETA_ONE**STEP)
    second_hat = second_new / (1.0 - BETA_TWO**STEP)
    master_new = master - rate * (
        first_hat / (jnp.sqrt(second_hat) + ADAM_EPS) + WEIGHT_DECAY * master
    )
    return (master_new, first_new, second_new)


def local(
    inputs,
    counts,
    cotangent,
    lstm_master,
    lstm_copy,
    lstm_first,
    lstm_second,
    mats_master,
    mats_copy,
    mats_first,
    mats_second,
    out_master,
    out_copy,
    out_first,
    out_second,
    vec_master,
    vec_first,
    vec_second,
):
    low, f32 = jnp.bfloat16, jnp.float32
    n_dp = lax.axis_size("dp")
    on_first = lax.axis_index("section") == 0
    batch_size, length, model_width = inputs.shape[1:]
    half = batch_size // 2
    vocab_half = out_copy.shape[1]
    vocab_pad = -(-vocab_half // LANES) * LANES
    piece = vec_master.shape[1]

    kept = jnp.where(on_first, counts[0, :half], counts[0, half:])
    other = jnp.where(on_first, counts[0, half:], counts[0, :half])
    other = lax.ppermute(other, "section", [(0, 1), (1, 0)])
    frames, labels = jnp.where(on_first, kept, other), jnp.where(on_first, other, kept)

    mats_block = jnp.swapaxes(mats_copy, 1, 2)
    out_block = jnp.pad(out_copy, ((0, 0), (0, vocab_pad - vocab_half)))
    vec_block = jnp.pad(vec_master.astype(low).astype(f32), ((0, 0), (0, LANES - piece)))
    act, cell, ht, base, spread, vectors, pair, weight, weight_t, pairs, third_line, out_line = forward(
        n_dp, inputs[0], lstm_copy[0], mats_block, out_block, vec_block
    )
    memory, decoded = pair.reshape(2, half * length, model_width)
    pairs = pairs.reshape(2, 2 * model_width, model_width)
    dz, dq, dk, vec_rows, logits, outer, third_part, out_part = attention(
        n_dp, frames, labels, memory, decoded, cotangent, vectors, pairs, third_line, out_line
    )
    logits = logits.reshape(batch_size, length, vocab_pad)[..., :vocab_half]
    dpre, dpre_other, ht_other, mats_part = backward(
        n_dp, act, cell, outer, dq, dk, decoded, memory, weight_t, ht
    )
    lstm_sum, inputs_grad, vec_sum, mats_sum, third_sum, out_sum = update(
        n_dp,
        batch_size,
        ht,
        ht_other,
        dpre,
        dpre_other,
        weight,
        base.reshape(-1, model_width),
        spread.reshape(-1, LANES),
        outer,
        vectors,
        vec_rows,
        mats_part,
        third_part,
        out_part,
    )
    mats_sum = jnp.concatenate([mats_sum.reshape(2, -1, model_width), third_sum[None]], 0)
    mats_sum = jnp.swapaxes(mats_sum, 1, 2)
    lstm_new, lstm_first_new, lstm_second_new = adamw(
        lstm_master, lstm_first, lstm_second, lstm_sum[None], RATE_LSTM
    )
    mats_new, mats_first_new, mats_second_new = adamw(
        mats_master, mats_first, mats_second, mats_sum, RATE_MATRIX
    )
    out_new, out_first_new, out_second_new = adamw(
        out_master, out_first, out_second, out_sum[:, :vocab_half], RATE_MATRIX
    )
    vec_new, vec_first_new, vec_second_new = adamw(
        vec_master, vec_first, vec_second, vec_sum[:, :piece], RATE_VECTOR
    )
    return (
        logits,
        inputs_grad[None],
        lstm_new,
        lstm_first_new,
        lstm_second_new,
        lstm_new.astype(low),
        mats_new,
        mats_first_new,
        mats_second_new,
        mats_new.astype(low),
        out_new,
        out_first_new,
        out_second_new,
        out_new.astype(low),
        vec_new,
        vec_first_new,
        vec_second_new,
    )


def solution(mesh):
    lstm = P("section", "dp", None)
    mats = P(None, None, ("section", "dp"))
    out = P("dp", "section")
    vec = P(None, ("section", "dp"))
    logits = P("dp", None, "section")
    rows = P("section", "dp", None, None)
    groups = (lstm,) * 4 + (mats,) * 4 + (out,) * 4 + (vec,) * 3
    return jax.shard_map(
        local,
        mesh=mesh,
        in_specs=(rows, P("section", "dp"), logits) + groups,
        out_specs=(logits, rows) + groups,
        check_vma=False,
    )
```

```python
import functools
import jax
import jax.numpy as jnp
from jax import lax
from jax.experimental import pallas as pl
from jax.experimental.pallas import tpu as pltpu
from jax.sharding import PartitionSpec as P

ROWS = 16
LANES = 128
UNROLL = 8
FOLDS = 4
LAG = 2
LAST_LAG = 3
ENERGY_OFFSET = -4.0
NORM_EPS = 1e-05
VMEM_SPEC = pl.BlockSpec(memory_space=pltpu.VMEM)
SMEM_SPEC = pl.BlockSpec(memory_space=pltpu.SMEM)
VMEM_LIMIT = 60 * 1024 * 1024


def contract(left, right, left_dim, right_dim):
    return lax.dot_general(
        left, right, (((left_dim,), (right_dim,)), ((), ())), preferred_element_type=jnp.float32
    )


MESH_ID = pl.DeviceIdType.MESH
ANY_SPEC = pl.BlockSpec(memory_space=pl.ANY)
DP_LAYOUTS = {16: (4, 2, 1, 2), 128: (8, 4, 1, 32)}
LINE_STRIDE = 4
TURN = 256
CHUNKS = 2


def flipped(value, k):
    result = value
    bit = 1
    while bit <= k:
        if k & bit:
            result = result + bit - 2 * bit * lax.rem(value // bit, 2)
        bit *= 2
    return result


class Place:
    def __init__(self, n_dp):
        self.line, self.side, stride_a, stride_b = DP_LAYOUTS[n_dp]
        self.core = lax.axis_index("section")
        self.chip = lax.axis_index("dp")
        self.z = lax.rem(self.chip // LINE_STRIDE, self.line)
        at_a = lax.rem(self.chip // stride_a, self.side)
        at_b = lax.rem(self.chip // stride_b, self.side)
        self.role = lax.rem(self.z, 2)
        moves_a = [(flipped(at_a, k) - at_a) * stride_a for k in range(self.side)]
        moves_b = [(flipped(at_b, k) - at_b) * stride_b for k in range(self.side)]
        core = self.core
        self.first = [a + (b - a) * core for a, b in zip(moves_a, moves_b)]
        self.second = [b + (a - b) * core for a, b in zip(moves_a, moves_b)]
        self.along = [(flipped(self.z, k) - self.z) * LINE_STRIDE for k in range(self.line)]

    def block(self, kz, kf=0, kg=0):
        return self.chip + self.along[kz] + self.first[kf] + self.second[kg]

    def other_block(self, kz, kf=0, kg=0):
        return self.chip + self.along[kz] + self.second[kf] + self.first[kg]

    def greet(self):
        barrier = pltpu.get_barrier_semaphore()
        peers = [(1 - self.core, self.chip)]
        for k in range(1, self.line):
            peers += [(0, self.chip + self.along[k]), (1, self.chip + self.along[k])]
        for k in range(1, self.side):
            peers += [(self.core, self.chip + self.first[k]), (self.core, self.chip + self.second[k])]
        for peer in peers:
            pl.semaphore_signal(barrier, inc=1, device_id=peer, device_id_type=MESH_ID)
        pl.semaphore_wait(barrier, len(peers))


def remote(source, target, send, receive, device):
    return pltpu.make_async_remote_copy(
        src_ref=source,
        dst_ref=target,
        send_sem=send,
        recv_sem=receive,
        device_id=device,
        device_id_type=MESH_ID,
    )


class Spread:
    def __init__(self, place, here, there, sems):
        self.place, self.here, self.there, self.sems = place, here, there, sems
        self.sent = []

    def send(self, target, device, send, receive):
        copy = remote(target, target, send, receive, device)
        copy.start()
        self.sent.append(copy)

    def arrived(self, target, semaphore):
        place = self.place
        remote(target, target, semaphore, semaphore, (1 - place.core, place.chip)).wait_recv()

    def to_second(self, kz, kf):
        place = self.place
        target = self.here(place.block(kz, kf))
        for kg in range(1, place.side):
            self.send(
                target,
                (place.core, place.chip + place.second[kg]),
                self.sems["gs"].at[kg, kf, kz],
                self.sems["gr"].at[kg, kf, kz],
            )

    def to_core(self, kz, kf, kg):
        place = self.place
        self.send(
            self.here(place.block(kz, kf, kg)),
            (1 - place.core, place.chip),
            self.sems["cs"].at[kg, kf, kz],
            self.sems["cr"].at[kg, kf, kz],
        )

    def stage_one(self, *steps):
        place = self.place
        for kz in steps or range(place.line):
            self.wait_line(kz)
            target = self.here(place.block(kz))
            for kf in range(1, place.side):
                self.send(
                    target,
                    (place.core, place.chip + place.first[kf]),
                    self.sems["fs"].at[kf, kz],
                    self.sems["fr"].at[kf, kz],
                )
            self.to_second(kz, 0)
            self.to_core(kz, 0, 0)

    def stage_two(self):
        place = self.place
        for kf in range(1, place.side):
            for kz in range(place.line):
                self.arrived(self.here(place.block(kz, kf)), self.sems["fr"].at[kf, kz])
                self.to_second(kz, kf)
                self.to_core(kz, kf, 0)

    def stage_three(self):
        place = self.place
        for kg in range(1, place.side):
            for kf in range(place.side):
                for kz in range(place.line):
                    self.arrived(self.here(place.block(kz, kf, kg)), self.sems["gr"].at[kg, kf, kz])
                    self.to_core(kz, kf, kg)

    def finish(self):
        place = self.place
        for kg in range(place.side):
            for kf in range(place.side):
                for kz in range(place.line):
                    self.arrived(self.there(place.other_block(kz, kf, kg)), self.sems["cr"].at[kg, kf, kz])

    def sent_all(self):
        for copy in self.sent:
            copy.wait_send()


def spread_sems(line, side, last=False):
    dma = pltpu.SemaphoreType.DMA
    ends = {"ls": dma((side, side, line)), "lr": dma((side, side, line))}
    return (ends if last else {}) | {
        "zs": dma((line, 2)),
        "zr": dma((line,)),
        "fs": dma((side, line)),
        "fr": dma((side, line)),
        "gs": dma((side, side, line)),
        "gr": dma((side, side, line)),
        "cs": dma((side, side, line)),
        "cr": dma((side, side, line)),
    }


def spread_even(place, source, at, sems):
    own = at(place.core, place.chip)
    spread = Spread(place, lambda block: at(place.core, block), lambda block: at(1 - place.core, block), sems)
    kept = pltpu.make_async_copy(source, own, sems["zr"].at[0])
    copies = [
        remote(source, own, sems["zs"].at[k, 0], sems["zr"].at[k], (place.core, place.chip + place.along[k]))
        for k in range(1, place.line)
    ]

    def begin():
        kept.start()
        for copy in copies:
            copy.start()
        spread.sent += copies

    def wait_line(kz):
        if kz == 0:
            kept.wait()
        else:
            spread.arrived(spread.here(place.block(kz)), sems["zr"].at[kz])

    spread.begin = begin
    spread.wait_line = wait_line
    return spread


class SpreadLast(Spread):
    def __init__(self, place, source, at, sems):
        super().__init__(place, lambda block: at(place.core, block), lambda block: at(1 - place.core, block), sems)
        self.source = source
        self.kept = pltpu.make_async_copy(source, self.here(place.chip), sems["zr"].at[0])

    def begin(self):
        place = self.place
        self.kept.start()
        own = self.here(place.chip)
        for k in range(1, place.side):
            for moves, send, receive in (
                (place.first, self.sems["fs"].at[k, 0], self.sems["fr"].at[k, 0]),
                (place.second, self.sems["gs"].at[k, 0, 0], self.sems["gr"].at[k, 0, 0]),
            ):
                copy = remote(self.source, own, send, receive, (place.core, place.chip + moves[k]))
                copy.start()
                self.sent.append(copy)

    def stage_plane(self):
        for kf in range(1, self.place.side):
            self.arrived(self.here(self.place.block(0, kf)), self.sems["fr"].at[kf, 0])
            self.to_second(0, kf)

    def stage_line(self):
        place = self.place
        self.kept.wait()
        for kg in range(place.side):
            for kf in range(place.side):
                target = self.here(place.block(0, kf, kg))
                if kg:
                    self.arrived(target, self.sems["gr"].at[kg, kf, 0])
                for kz in reversed(range(1, place.line)):
                    self.send(
                        target,
                        (place.core, place.chip + place.along[kz]),
                        self.sems["ls"].at[kg, kf, kz],
                        self.sems["lr"].at[kg, kf, kz],
                    )
                self.to_core(0, kf, kg)

    def stage_core(self):
        place = self.place
        for kg in range(place.side):
            for kf in range(place.side):
                for kz in range(1, place.line):
                    self.arrived(self.here(place.block(kz, kf, kg)), self.sems["lr"].at[kg, kf, kz])
                    self.to_core(kz, kf, kg)


def spread_role(place, source, target, sems, rows, half, first, count):
    source = source.at[first : first + count]

    def columns(core):
        return pl.ds(pl.multiple_of(core * half, half), half)

    def at(block, core):
        return target.at[pl.ds(pl.multiple_of(block * rows + first, count), count), columns(core)]

    spread = Spread(
        place, lambda block: at(block, place.core), lambda block: at(block, 1 - place.core), sems
    )
    mine = place.role == place.core
    kept = pltpu.make_async_copy(source.at[:, columns(place.core)], at(place.chip, place.core), sems["zr"].at[0])
    cross = remote(
        source.at[:, columns(1 - place.core)],
        at(place.chip, 1 - place.core),
        sems["zs"].at[0, 0],
        sems["zr"].at[0],
        (1 - place.core, place.chip),
    )
    copies = [
        [
            remote(
                source.at[:, columns(core)],
                at(place.chip, core),
                sems["zs"].at[k, core],
                sems["zr"].at[k],
                (core, place.chip + place.along[k]),
            )
            for core in range(2)
        ]
        for k in range(1, place.line)
    ]

    guest = jnp.logical_not(mine)

    def each(condition, steps, action):
        @pl.when(condition)
        def _():
            for k in steps:
                for copy in copies[k - 1] if k else [cross]:
                    action(copy)

    def start(copy):
        copy.start()

    def begin():
        @pl.when(mine)
        def _():
            kept.start()

        each(mine, range(0, place.line, 2), start)
        each(guest, range(1, place.line, 2), start)

    def wait_line(kz):
        if kz == 0:

            @pl.when(mine)
            def _():
                kept.wait()

            @pl.when(jnp.logical_not(mine))
            def _():
                spread.arrived(spread.here(place.chip), sems["zr"].at[0])

        else:
            spread.arrived(spread.here(place.block(kz)), sems["zr"].at[kz])

    def finished(copy):
        copy.wait_send()

    def sent_line():
        each(mine, range(0, place.line, 2), finished)
        each(guest, range(1, place.line, 2), finished)

    spread.begin = begin
    spread.wait_line = wait_line
    spread.sent_line = sent_line
    return spread


def forward_kernel(
    n_dp,
    seq_ref,
    shard_ref,
    mats_ref,
    out_ref,
    vec_ref,
    act_out,
    cell_ref,
    ht_ref,
    base_ref,
    spread_ref,
    vectors_ref,
    pair_ref,
    w_out,
    wt_out,
    mats_out,
    third_out,
    out_out,
    act_ref,
    seq_s,
    result_s,
    x_s,
    h_s,
    w_s,
    wt_s,
    vec_s,
    state,
    keep_sem,
    seq_sem,
    pair_sem,
    sems_m,
    sems_v,
    sems_n,
    sems_o,
    *sems_w,
):
    batch, steps, width = seq_ref.shape
    low, f32 = jnp.bfloat16, jnp.float32
    place = Place(n_dp)
    core, chip = place.core, place.chip
    mine = core == place.role
    guest = jnp.logical_not(mine)
    encoder = place.role == 0
    place.greet()
    rows = shard_ref.shape[0]
    count = max(ROWS, rows // CHUNKS)
    matrix = [
        spread_role(place, shard_ref, w_s, sems, rows, 2 * width, n * count, count)
        for n, sems in zip(range(rows // count), sems_w)
    ]
    mats = spread_even(place, mats_ref.at[:2], lambda core, chip: mats_out.at[:, core, chip], sems_m)
    vecs = spread_even(place, vec_ref, lambda core, chip: vec_s.at[core, chip], sems_v)
    thirds = SpreadLast(place, mats_ref.at[2], lambda core, chip: third_out.at[core, chip], sems_n)
    outs = spread_even(place, out_ref, lambda core, chip: out_out.at[core, chip], sems_o)
    vecs.begin()
    for part in matrix:
        part.begin()
    seq_kept = pltpu.make_async_copy(seq_ref, seq_s, seq_sem.at[0])
    seq_away = remote(seq_ref, seq_s, seq_sem.at[1], seq_sem.at[2], (1 - core, chip + place.along[1]))
    pl.when(mine)(seq_kept.start)
    pl.when(guest)(seq_away.start)
    thirds.begin()
    for part in matrix:
        part.stage_one(0)
    state[...] = jnp.zeros_like(state)
    cell_ref[:ROWS] = jnp.zeros((ROWS, width), f32)
    base_ref[:, batch:] = jnp.zeros((steps, ROWS - batch, width), f32)
    spread_ref[...] = jnp.zeros_like(spread_ref)
    line_rest = range(1, place.line)
    thirds.stage_plane()
    for n in range(len(matrix) + 2):
        if n < len(matrix):
            matrix[n].stage_one(*line_rest)
        if n == 0:
            vecs.stage_one()
        if n == len(matrix) - 1:
            mats.begin()
            outs.begin()
        if 1 <= n <= len(matrix):
            matrix[n - 1].stage_two()
        if n == 1:
            vecs.stage_two()
        if n >= 2:
            matrix[n - 2].stage_three()
    mats.stage_one(0)
    thirds.stage_line()
    pl.when(mine)(seq_kept.wait)
    pl.when(guest)(seq_away.wait)
    for u in range(batch):
        raw = seq_s[u].astype(f32)
        center = raw - jnp.mean(raw, -1, keepdims=True)
        spread = lax.rsqrt(jnp.mean(center * center, -1, keepdims=True) + NORM_EPS)
        base_ref[:, u, :] = jnp.where(encoder, center * spread, raw)
        spread_ref[:, u, :] = jnp.broadcast_to(spread, (steps, LANES))
    vecs.stage_three()
    vecs.finish()
    piece = 2 * width // (2 * n_dp)
    per_tile = LANES // piece
    for m in range(2 * width // LANES):
        tile = jnp.zeros((8, LANES), f32)
        for k in range(per_tile):
            index = m * per_tile + k
            block = vec_s[index // n_dp, index % n_dp]
            tile = tile + (pltpu.roll(block, k * piece, 1) if k else block)
        vectors_ref[:, m * LANES : (m + 1) * LANES] = tile
    gain = jnp.where(encoder, vectors_ref[4:5, :width], 1.0)
    shift = jnp.where(encoder, vectors_ref[4:5, width:], 0.0)
    x_s[...] = (base_ref[...].reshape(steps * ROWS, width) * gain + shift).astype(low)
    ht_ref[:width] = x_s[...].T
    for part in matrix:
        part.finish()
    keep = pltpu.make_async_copy(w_s.at[:width], w_out, keep_sem.at[0])
    keep.start()
    for q in range(4):
        columns = slice(q * width, (q + 1) * width)
        row = q // 2
        bias_columns = slice((q % 2) * width, (q % 2 + 1) * width)
        bias = jnp.where(
            encoder, vectors_ref[row : row + 1, bias_columns], vectors_ref[row + 2 : row + 3, bias_columns]
        )
        act_ref[:, columns] = jnp.dot(x_s[...], w_s[:width, columns], preferred_element_type=f32) + bias

    def step(t, carry):
        rows = pl.ds(pl.multiple_of(t * ROWS, ROWS), ROWS)
        after = pl.ds(pl.multiple_of((t + 1) * ROWS, ROWS), ROWS)
        hidden = state[...]

        def gate(q):
            columns = slice(q * width, (q + 1) * width)
            return act_ref[rows, columns] + jnp.dot(hidden, w_s[width:, columns], preferred_element_type=f32)

        in_gate = jax.nn.sigmoid(gate(0))
        forget = jax.nn.sigmoid(gate(1))
        candidate = jnp.tanh(gate(2))
        cell = forget * cell_ref[rows] + in_gate * candidate
        out_gate = jax.nn.sigmoid(gate(3))
        hidden_new = (out_gate * jnp.tanh(cell)).astype(low)
        act_ref[rows, :width] = in_gate
        act_ref[rows, width : 2 * width] = forget
        act_ref[rows, 2 * width : 3 * width] = candidate
        act_ref[rows, 3 * width :] = out_gate
        cell_ref[after] = cell
        h_s[after] = hidden_new
        state[...] = hidden_new
        return carry

    h_s[:ROWS] = jnp.zeros((ROWS, width), low)
    marks = [steps * n // 24 for n in (0, 8, 12, 18, 24)]
    gates_out = []

    def run(n):
        lax.fori_loop(marks[n], marks[n + 1], step, 0)
        rows = slice(marks[n] * ROWS, marks[n + 1] * ROWS)
        gates_out.append(pltpu.make_async_copy(act_ref.at[rows], act_out.at[rows], keep_sem.at[2 + n]))
        gates_out[-1].start()

    mats.stage_one(*line_rest)
    run(0)
    mats.stage_two()
    outs.stage_one()
    run(1)
    outs.stage_two()
    run(2)
    mats.stage_three()
    run(3)
    turned = h_s[ROWS:].astype(f32).reshape(steps, ROWS, width)
    for u in range(batch):
        value = turned[:, u, :]
        result_s[u] = jnp.where(encoder, seq_s[u].astype(f32) + value, value).astype(low)
    half = batch // 2
    for h in range(2):
        home = jnp.logical_and(mine, core == h)
        source, target = result_s.at[h * half : (h + 1) * half], pair_ref.at[place.role]
        stay = pltpu.make_async_copy(source, target, pair_sem.at[0, h])
        leave = remote(
            source,
            target,
            pair_sem.at[0, h],
            pair_sem.at[1, place.role],
            (h, jnp.where(mine, chip, chip + place.along[1])),
        )
        pl.when(home)(stay.start)
        pl.when(jnp.logical_not(home))(leave.start)
    for q in range(4):
        for n in range(width // TURN):
            rows = slice(width + n * TURN, width + (n + 1) * TURN)
            wt_s[q, :, n * TURN : (n + 1) * TURN] = w_s[rows, q * width : (q + 1) * width].T
    keep_turned = pltpu.make_async_copy(wt_s, wt_out, keep_sem.at[1])
    keep_turned.start()
    ht_ref[width:] = h_s[:-ROWS].T
    outs.stage_three()
    thirds.stage_core()
    mats.finish()
    outs.finish()
    thirds.finish()
    for h in range(2):
        home = jnp.logical_and(mine, core == h)
        source, target = result_s.at[h * half : (h + 1) * half], pair_ref.at[place.role]
        stay = pltpu.make_async_copy(source, target, pair_sem.at[0, h])
        leave = remote(
            source,
            target,
            pair_sem.at[0, h],
            pair_sem.at[1, place.role],
            (h, jnp.where(mine, chip, chip + place.along[1])),
        )
        pl.when(home)(stay.wait)
        pl.when(jnp.logical_not(home))(leave.wait_send)

    def arrived(section):
        target = pair_ref.at[section]
        remote(target, target, pair_sem.at[0, 0], pair_sem.at[1, section], (1 - core, chip)).wait_recv()

    pl.when(guest)(lambda: arrived(place.role))
    arrived(1 - place.role)
    keep.wait()
    keep_turned.wait()
    for copy in gates_out:
        copy.wait()
    for part in matrix:
        part.sent_line()
    for spread in (*matrix, vecs, mats, thirds, outs):
        spread.sent_all()


def forward(n_dp, seq, shard, mats_block, out_block, vec_block):
    batch, steps, width = seq.shape
    rows = steps * ROWS
    low, f32 = jnp.bfloat16, jnp.float32
    line, side = DP_LAYOUTS[n_dp][:2]
    columns = mats_block.shape[1]
    dma = pltpu.SemaphoreType.DMA
    return pl.pallas_call(
        functools.partial(forward_kernel, n_dp),
        out_shape=(
            jax.ShapeDtypeStruct((rows, 4 * width), f32),
            jax.ShapeDtypeStruct((rows + ROWS, width), f32),
            jax.ShapeDtypeStruct((2 * width, rows), low),
            jax.ShapeDtypeStruct((steps, ROWS, width), f32),
            jax.ShapeDtypeStruct((steps, ROWS, LANES), f32),
            jax.ShapeDtypeStruct((8, 2 * width), f32),
            jax.ShapeDtypeStruct((2, batch // 2, steps, width), low),
            jax.ShapeDtypeStruct((width, 4 * width), low),
            jax.ShapeDtypeStruct((4, width, width), low),
            jax.ShapeDtypeStruct((2, 2, n_dp, columns, width), low),
            jax.ShapeDtypeStruct((2, n_dp, columns, width), low),
            jax.ShapeDtypeStruct((2, n_dp) + out_block.shape, low),
        ),
        in_specs=[VMEM_SPEC, ANY_SPEC, ANY_SPEC, ANY_SPEC, VMEM_SPEC],
        out_specs=(ANY_SPEC,) + (VMEM_SPEC,) * 6 + (ANY_SPEC,) * 5,
        scratch_shapes=[
            pltpu.VMEM((rows, 4 * width), f32),
            pltpu.VMEM((batch, steps, width), low),
            pltpu.VMEM((batch, steps, width), low),
            pltpu.VMEM((rows, width), low),
            pltpu.VMEM((rows + ROWS, width), low),
            pltpu.VMEM((2 * width, 4 * width), low),
            pltpu.VMEM((4, width, width), low),
            pltpu.VMEM((2, n_dp, 8, LANES), f32),
            pltpu.VMEM((ROWS, width), low),
            dma((6,)),
            dma((3,)),
            dma((2, 2)),
        ]
        + [spread_sems(line, side)] * 2
        + [spread_sems(line, side, last=True)]
        + [spread_sems(line, side)] * (1 + shard.shape[0] // max(ROWS, shard.shape[0] // CHUNKS)),
        compiler_params=pltpu.CompilerParams(
            collective_id=1, has_side_effects=True, vmem_limit_bytes=VMEM_LIMIT
        ),
    )(seq, shard, mats_block, out_block, vec_block)


class Fold:
    def __init__(self, place, part, stage, near, far, sems):
        self.place, self.part, self.stage, self.near, self.far, self.sems = place, part, stage, near, far, sems
        self.sent = []

    def send(self, source, target, device, send, receive):
        copy = remote(source, target, send, receive, device)
        copy.start()
        self.sent.append(copy)

    def arrived(self, target, semaphore):
        place = self.place
        remote(target, target, semaphore, semaphore, (1 - place.core, place.chip)).wait_recv()

    def stage_a(self, *steps):
        place = self.place
        for kz in steps or reversed(range(place.line)):
            for kg in range(1, place.side):
                for kf in reversed(range(place.side)):
                    source = self.stage.at[kg - 1, kf, kz]
                    source[...] = self.part(kz, kf, kg).astype(source.dtype)
                    self.send(
                        source,
                        self.near.at[kg - 1, kf, kz],
                        (place.core, place.chip + place.second[kg]),
                        self.sems["gs"].at[kg, kf, kz],
                        self.sems["gr"].at[kg, kf, kz],
                    )

    def stage_b(self, *steps):
        place = self.place
        for kz in steps or reversed(range(place.line)):
            for kf in reversed(range(place.side)):
                total = self.part(kz, kf, 0)
                for kg in range(1, place.side):
                    self.arrived(self.near.at[kg - 1, kf, kz], self.sems["gr"].at[kg, kf, kz])
                    total = total + self.near[kg - 1, kf, kz].astype(jnp.float32)
                source = self.near.at[0, kf, kz]
                source[...] = total.astype(source.dtype)
                if kf:
                    self.send(
                        source,
                        self.far.at[kf - 1, kz],
                        (place.core, place.chip + place.first[kf]),
                        self.sems["fs"].at[kf, kz],
                        self.sems["fr"].at[kf, kz],
                    )

    def stage_half(self, half_ref):
        place = self.place
        for kz in range(place.line):
            for kf in range(place.side):
                total = self.part(kz, kf, 0)
                for kg in range(1, place.side):
                    self.arrived(self.near.at[kg - 1, kf, kz], self.sems["gr"].at[kg, kf, kz])
                    total = total + self.near[kg - 1, kf, kz].astype(jnp.float32)
                half_ref[kf, kz] = total.astype(half_ref.dtype)

    def summed(self, kz):
        place = self.place
        total = self.near[0, 0, kz].astype(jnp.float32)
        for kf in range(1, place.side):
            self.arrived(self.far.at[kf - 1, kz], self.sems["fr"].at[kf, kz])
            total = total + self.far[kf - 1, kz].astype(jnp.float32)
        return total.astype(self.far.dtype)

    def sent_all(self):
        for copy in self.sent:
            copy.wait_send()


class FoldRest(Fold):
    def __init__(self, place, half_ref, far, sems):
        super().__init__(place, None, None, None, far, sems)
        self.half_ref = half_ref

    def begin(self):
        place = self.place
        for kz in range(place.line):
            for kf in range(1, place.side):
                self.send(
                    self.half_ref.at[kf, kz],
                    self.far.at[kf - 1, kz],
                    (place.core, place.chip + place.first[kf]),
                    self.sems["fs"].at[kf, kz],
                    self.sems["fr"].at[kf, kz],
                )

    def summed(self, kz):
        total = self.half_ref[0, kz].astype(jnp.float32)
        for kf in range(1, self.place.side):
            self.arrived(self.far.at[kf - 1, kz], self.sems["fr"].at[kf, kz])
            total = total + self.far[kf - 1, kz].astype(jnp.float32)
        return total.astype(self.far.dtype)


class FoldLine:
    def __init__(self, place, parts, end, sems):
        self.place, self.parts, self.end, self.sems = place, parts, end, sems

    def begin(self, *steps):
        place = self.place
        for kz in steps or reversed(range(1, place.line)):
            self.copy(kz).start()

    def copy(self, kz):
        place = self.place
        return remote(
            self.parts.at[kz],
            self.end.at[kz - 1],
            self.sems["zs"].at[kz, 0],
            self.sems["zr"].at[kz],
            (place.core, place.chip + place.along[kz]),
        )

    def result(self):
        total = self.parts[0].astype(jnp.float32)
        for kz in range(1, self.place.line):
            self.copy(kz).wait_recv()
            total = total + self.end[kz - 1].astype(jnp.float32)
        return total

    def sent_all(self):
        for kz in range(1, self.place.line):
            self.copy(kz).wait_send()


class FoldRole(Fold):
    def __init__(self, place, part, stage, near, far, end, sems):
        super().__init__(place, part, stage, near, far, sems)
        self.end = end

    def stage_c(self, kz):
        place = self.place
        source = self.far.at[0, kz]
        source[...] = self.summed(kz)
        if kz:
            self.send(
                source,
                self.end.at[place.core, kz // 2],
                (place.role, place.chip + place.along[kz]),
                self.sems["zs"].at[kz, 0],
                self.sems["er"].at[place.core, kz // 2],
            )
        else:
            self.last = source
            self.cross = remote(
                source,
                self.end.at[place.core, 0],
                self.sems["zs"].at[0, 0],
                self.sems["er"].at[place.core, 0],
                (1 - place.core, place.chip),
            )

            @pl.when(place.core != place.role)
            def _():
                self.cross.start()

    def result(self, sum_ref):
        place = self.place
        rows, half = self.end.shape[2:]
        mine = place.core == place.role

        def columns(core):
            return pl.ds(pl.multiple_of(core * half, half), half)

        def add(parity):
            sources = [kz for kz in range(place.line) if kz % 2 == parity]
            for core in range(2):
                total = jnp.zeros((rows, half), jnp.float32)
                for kz in sources:
                    if kz:
                        self.arrived(self.end.at[core, kz // 2], self.sems["er"].at[core, kz // 2])
                        total = total + self.end[core, kz // 2].astype(jnp.float32)
                sum_ref[:, core * half : (core + 1) * half] = total

        @pl.when(mine)
        def _():
            add(0)
            own, other = columns(place.core), columns(1 - place.core)
            sum_ref[:, own] += self.last[...].astype(jnp.float32)
            self.arrived(self.end.at[1 - place.core, 0], self.sems["er"].at[1 - place.core, 0])
            sum_ref[:, other] += self.end[1 - place.core, 0].astype(jnp.float32)

        @pl.when(jnp.logical_not(mine))
        def _():
            add(1)
            self.cross.wait_send()


def fold_sems(line, side):
    dma = pltpu.SemaphoreType.DMA
    return {
        "gs": dma((side, side, line)),
        "gr": dma((side, side, line)),
        "fs": dma((side, line)),
        "fr": dma((side, line)),
        "zs": dma((line, 1)),
        "zr": dma((line,)),
        "er": dma((2, line // 2)),
    }


def fold_buffers(line, side, shape, dtype):
    return [
        pltpu.VMEM((side - 1, side, line) + shape, dtype),
        pltpu.VMEM((side - 1, side, line) + shape, dtype),
    ]


def attention_kernel(
    n_dp,
    frames_ref,
    labels_ref,
    mem_ref,
    dec_ref,
    cot_ref,
    vec_ref,
    pairs_any,
    third_any,
    out_any,
    dz_ref,
    dq_ref,
    dk_ref,
    dvec_ref,
    logits_ref,
    outer_ref,
    third_half,
    out_half,
    squash_ref,
    context_ref,
    ddec_ref,
    cot_s,
    gl_f,
    gl_ref,
    own_logits,
    mats_ref,
    third_s,
    out_s,
    back_s,
    facts,
    facts_gl,
    g_third,
    g_out,
    t_stage,
    t_near,
    o_stage,
    o_near,
    q_s,
    k_s,
    mem_s,
    ctx_s,
    dqa_s,
    dka_s,
    e_s,
    sel_s,
    prob_s,
    sel_d,
    prob_d,
    reach_d,
    back_d,
    w_s,
    a_s,
    own_s,
    nxt_s,
    g_s,
    d_s,
    d_rows,
    bc_s,
    load_sem,
    cot_sems,
    fact_sems,
    logit_sems,
    back_sems,
    sems_ft,
    sems_fo,
):
    rows, width = dec_ref.shape
    utts = frames_ref.shape[0]
    length = rows // utts
    vocab_half = cot_ref.shape[2]
    vocab_pad = gl_f.shape[2]
    low = jnp.bfloat16
    f32 = jnp.float32
    lane = lax.broadcasted_iota(jnp.int32, (length, LANES), 1)
    lane_block = lax.broadcasted_iota(jnp.int32, (length, 8, LANES), 2)

    place = Place(n_dp)
    core, chip = place.core, place.chip
    other = (1 - core, chip)
    loads = [
        pltpu.make_async_copy(pairs_any.at[0], mats_ref.at[0], load_sem.at[0]),
        pltpu.make_async_copy(pairs_any.at[1], mats_ref.at[1], load_sem.at[1]),
        pltpu.make_async_copy(third_any, third_s, load_sem.at[2]),
        pltpu.make_async_copy(out_any, out_s, load_sem.at[3]),
    ]
    for load in loads:
        load.start()
    place.greet()
    cot_away = remote(
        cot_ref.at[pl.ds((1 - core) * utts, utts)], cot_s, cot_sems.at[0], cot_sems.at[1], other
    )
    cot_away.start()
    loads[0].wait()
    q_s[...] = contract(dec_ref[...], mats_ref[0], 1, 1) + vec_ref[5:6]
    loads[1].wait()
    k_s[...] = contract(mem_ref[...], mats_ref[1], 1, 1)
    mem_s[...] = mem_ref[...].astype(f32)
    e_s[...] = jnp.zeros_like(e_s)
    d_s[...] = jnp.zeros_like(d_s)

    tile = 256
    group = 4

    gl_f[...] = jnp.zeros_like(gl_f)
    cot_away.wait()
    slot = lax.broadcasted_iota(jnp.int32, (length, 1), 0)
    for u in range(utts):
        keep = (slot < labels_ref[u]).astype(f32)
        at = slice(u * length, (u + 1) * length)
        gl_f[core, at, :vocab_half] = cot_ref[core * utts + u].astype(f32) * keep
        gl_f[1 - core, at, :vocab_half] = cot_s[u].astype(f32) * keep
    gl_ref[...] = gl_f[...].astype(low)

    for u in range(utts):
        at = u * length

        def energy_step(block, sums, at=at):
            base = block * group
            for offset in range(group):
                j = base + offset
                row = k_s[pl.ds(at + j, 1), :]
                for head in range(2):
                    total = jnp.zeros((length, LANES), f32)
                    for c in range(width // LANES):
                        columns = slice(head * width + c * LANES, head * width + (c + 1) * LANES)
                        total = total + jnp.tanh(
                            q_s[at : at + length, columns] + row[:, columns]
                        ) * vec_ref[6:7, columns]
                    value = jnp.sum(total, -1, keepdims=True)
                    sums = tuple(
                        jnp.where(lane == j, value, s) if h == head else s
                        for h, s in enumerate(sums)
                    )
            return sums

        blocks = length // group
        zero = jnp.zeros((length, LANES), f32)
        mono, window = lax.fori_loop(0, blocks, energy_step, (zero, zero))
        e_s[0, :, u, :] = mono
        e_s[1, :, u, :] = window

    mask = jnp.zeros((8, LANES), f32)
    row_u = lax.broadcasted_iota(jnp.int32, (8, LANES), 0)
    lane_u = lax.broadcasted_iota(jnp.int32, (8, LANES), 1)
    for u in range(utts):
        inside_u = jnp.logical_and(row_u == u, lane_u < frames_ref[u])
        mask = jnp.where(inside_u, 1.0, mask)
    mask = mask[None]
    mono = e_s[0] + ENERGY_OFFSET
    window = e_s[1]
    chosen = jax.nn.sigmoid(mono)
    inside = (lane_block < length).astype(f32)
    sel_s[...] = chosen * mask
    leave = (jnp.maximum(mono, 0.0) + jnp.log1p(jnp.exp(-jnp.abs(mono)))) * mask
    prob = jnp.exp(-leave) * inside
    prob_s[...] = prob

    def right(value, distance):
        return pltpu.roll(value, distance, value.ndim - 1)

    def left(value, distance):
        return pltpu.roll(value, LANES - distance, value.ndim - 1)

    diagonals = 2 * length - 1
    bits = [2**n for n in range(5)]

    def skewed(value):
        value = jnp.concatenate([value, jnp.zeros((diagonals - length, 8, LANES), f32)], 0)
        for bit in bits:
            moved = jnp.concatenate([jnp.zeros((bit, 8, LANES), f32), value[:-bit]], 0)
            value = jnp.where(lane_row & bit != 0, moved, value)
        return value

    def straight(value):
        for bit in bits:
            moved = jnp.concatenate([value[bit:], jnp.zeros((bit, 8, LANES), f32)], 0)
            value = jnp.where(lane_row & bit != 0, moved, value)
        return value[:length]

    lane_row = lax.broadcasted_iota(jnp.int32, (8, LANES), 1)
    sel_d[...] = skewed(sel_s[...])
    prob_d[...] = skewed(jnp.where(lane_block < length - 1, prob, 0.0))

    def align_step(d, total):
        reach_d[d] = total
        return sel_d[d] * total + right(prob_d[d] * total, 1)

    lax.fori_loop(0, diagonals, align_step, jnp.where(lane_row == 0, 1.0, 0.0).astype(f32))
    w_s[...] = straight(reach_d[...])
    a_s[...] = sel_s[...] * w_s[...]

    aligned = a_s[...]
    own = jnp.where(lane_block == 0, 1.0, jax.nn.sigmoid(window - right(window, 1)))
    nxt = jax.nn.sigmoid(window - left(window, 1))
    own_s[...] = own
    nxt_s[...] = nxt
    beta = aligned * own + jnp.where(lane_block < length - 1, left(aligned, 1), 0.0) * nxt
    g_s[...] = beta

    for u in range(utts):
        at = u * length
        weights = g_s[:, u, :].astype(low)[:, :length]
        ctx_s[at : at + length] = jnp.dot(
            weights, mem_s[at : at + length].astype(low), preferred_element_type=f32
        )
    context_ref[...] = ctx_s[...].astype(low)

    loads[2].wait()
    loads[3].wait()
    third_low, third_high = third_s[0], third_s[1]
    squash = jnp.tanh(
        jnp.dot(dec_ref[...], third_low, preferred_element_type=f32)
        + jnp.dot(context_ref[...], third_high, preferred_element_type=f32)
        + vec_ref[7:8, :width]
    )
    squash_ref[...] = squash.astype(low)
    pull = contract(gl_ref[0], out_s[0], 1, 1) + contract(
        gl_ref[1], out_s[1], 1, 1
    )
    dz = (pull * (1.0 - squash * squash)).astype(low)
    dz_ref[...] = dz
    sources = [dec_ref, context_ref, dz_ref, squash_ref]
    handed = [
        remote(source, facts.at[n], fact_sems.at[0, n], fact_sems.at[1, n], other)
        for n, source in enumerate(sources)
    ]
    handed.append(remote(gl_ref.at[1 - core], facts_gl, fact_sems.at[0, 4], fact_sems.at[1, 4], other))
    for copy in handed:
        copy.start()
    dvec_ref[...] = jnp.zeros_like(dvec_ref)
    dvec_ref[7:8, :width] = jnp.sum(dz.astype(f32), 0, keepdims=True)
    for h in range(2):
        begin = width + h * vocab_half
        row = jnp.concatenate(
            [
                jnp.sum(gl_f[h], 0, keepdims=True),
                jnp.zeros((1, 2 * width - vocab_pad), f32),
            ],
            -1,
        )
        dvec_ref[7:8] += pltpu.roll(row, begin, 1)
        bias = pltpu.roll(vec_ref[7:8], 2 * width - begin, 1)[:, :vocab_pad]
        own_logits[h] = (
            jnp.dot(squash_ref[...], out_s[h], preferred_element_type=f32) + bias
        ).astype(low)
    logits_kept = pltpu.make_async_copy(own_logits.at[core], logits_ref.at[core], logit_sems.at[0])
    logits_away = remote(
        own_logits.at[1 - core], logits_ref.at[core], logit_sems.at[1], logit_sems.at[2], other
    )
    logits_kept.start()
    logits_away.start()
    ddec_ref[...] = contract(dz, third_low, 1, 1)
    ctx_s[...] = contract(dz, third_high, 1, 1).astype(low).astype(f32)

    pad = jnp.zeros((length, LANES - length), f32)
    for u in range(utts):
        at = u * length
        weights = g_s[:, u, :].astype(low)[:, :length]
        pulled = ctx_s[at : at + length].astype(low)
        beta_grad = contract(pulled, mem_s[at : at + length].astype(low), 1, 1)
        e_s[0, :, u, :] = jnp.concatenate([beta_grad, pad], -1)
        mem_s[at : at + length] = contract(weights, pulled, 0, 0)

    for copy in handed:
        copy.wait_recv()
    joined = jnp.where(core == 0, dec_ref[...], context_ref[...])
    joined_other = jnp.where(core == 0, facts[0], facts[1])
    part_rows, out_rows = g_third.shape[1], g_out.shape[1]
    total = (contract(joined, dz_ref[...], 0, 0) + contract(joined_other, facts[2], 0, 0)).astype(low)
    for block in range(n_dp):
        g_third[block] = total[block * part_rows : (block + 1) * part_rows]
    total = (contract(squash_ref[...], gl_ref[core], 0, 0) + contract(facts[3], facts_gl[...], 0, 0)).astype(low)
    for block in range(n_dp):
        g_out[block] = total[block * out_rows : (block + 1) * out_rows]
    third_fold = Fold(
        place, lambda kz, kf, kg: g_third[place.block(kz, kf, kg)].astype(f32), t_stage, t_near, None, sems_ft
    )
    out_fold = Fold(
        place, lambda kz, kf, kg: g_out[place.block(kz, kf, kg)].astype(f32), o_stage, o_near, None, sems_fo
    )
    third_fold.stage_a()
    out_fold.stage_a()

    beta_grad = e_s[0]
    own = own_s[...]
    nxt = nxt_s[...]
    g_s[...] = beta_grad * own + jnp.where(lane_block >= 1, right(beta_grad * nxt, 1), 0.0)
    aligned = a_s[...]
    from_own = jnp.where(lane_block >= 1, beta_grad * aligned * own * (1.0 - own), 0.0)
    from_next = (
        beta_grad
        * jnp.where(lane_block < length - 1, left(aligned, 1), 0.0)
        * nxt
        * (1.0 - nxt)
    )
    d_s[1] = (from_own - left(from_own, 1) + from_next - right(from_next, 1)) * inside

    prob = prob_s[...]
    reach_d[...] = skewed(g_s[...])

    def retreat_step(k, after):
        d = diagonals - 1 - k
        grad_align = reach_d[d] + after
        total = sel_d[d] * grad_align + prob_d[d] * left(after, 1)
        reach_d[d] = grad_align
        back_d[d] = total
        return total

    lax.fori_loop(0, diagonals, retreat_step, jnp.zeros((8, LANES), f32))
    e_s[0] = straight(reach_d[...])
    e_s[1] = straight(back_d[...])
    reached = w_s[...]
    grad_select = reached * e_s[0]
    grad_prob = reached * jnp.where(lane_block < length - 1, left(e_s[1], 1), 0.0)
    chosen = sel_s[...]
    d_s[0] = grad_select * chosen * (1.0 - chosen) - grad_prob * prob * chosen

    dka_s[...] = jnp.zeros_like(dka_s)
    spots = lax.broadcasted_iota(jnp.int32, (LANES, length * LANES), 1) // LANES
    picks = (lax.broadcasted_iota(jnp.int32, (LANES, length * LANES), 0) == spots).astype(f32)
    for head in range(2):
        for u in range(utts):
            d_rows[u * length : (u + 1) * length] = d_s[head, :, u, :]
        bc_s[head] = jnp.dot(
            d_rows[...], picks, precision=lax.Precision.HIGHEST, preferred_element_type=f32
        )

    def energy_back(u, dvec):
        at = pl.multiple_of(u * length, 8)
        count = length // UNROLL
        for c in range(2 * width // tile):
            columns = slice(c * tile, (c + 1) * tile)
            head = c * tile // width
            q_now = q_s[pl.ds(at, length), columns]

            def back_step(block, sums, head=head, columns=columns, q_now=q_now):
                dq, dw = sums
                for offset in range(UNROLL):
                    j = block * UNROLL + offset
                    squash_all = jnp.tanh(q_now + k_s[pl.ds(at + j, 1), columns])
                    grad = bc_s[head, pl.ds(at, length), pl.ds(pl.multiple_of(j * LANES, LANES), LANES)]
                    grad = jnp.concatenate([grad] * (tile // LANES), -1)
                    scaled = grad * squash_all
                    dw = dw + scaled
                    moved = grad - scaled * squash_all
                    dq = dq + moved
                    dka_s[pl.ds(at + j, 1), columns] = jnp.sum(moved, 0, keepdims=True)
                return (dq, dw)

            zero = jnp.zeros((length, tile), f32)
            dq, dw = lax.fori_loop(0, count, back_step, (zero, zero))
            dq = dq * vec_ref[6:7, columns]
            dqa_s[pl.ds(at, length), columns] = dq
            dvec_ref[5:6, columns] += jnp.sum(dq, 0, keepdims=True)
            dvec_ref[6:7, columns] += jnp.sum(dw, 0, keepdims=True)
        return dvec

    lax.fori_loop(0, utts, energy_back, 0)
    for h in range(2):
        columns = slice(h * width, (h + 1) * width)
        dq_ref[h] = dqa_s[:, columns].astype(low)
        dk_ref[h] = (dka_s[:, columns] * vec_ref[6:7, columns]).astype(low)
        ddec_ref[...] += jnp.dot(dq_ref[h], mats_ref[0, columns], preferred_element_type=f32)
        mem_s[...] += jnp.dot(dk_ref[h], mats_ref[1, columns], preferred_element_type=f32)
    for u in range(utts):
        at = slice(u * length, (u + 1) * length)
        back_s[0, u] = mem_s[at].astype(low)
        back_s[1, u] = ddec_ref[at].astype(low)
    role = place.role
    mine = core == role
    guest = jnp.logical_not(mine)
    stay = pltpu.make_async_copy(back_s.at[role], outer_ref.at[core], back_sems.at[0, 0])
    cross = remote(back_s.at[role], outer_ref.at[core], back_sems.at[0, 0], back_sems.at[1, core], (role, chip))
    away = remote(
        back_s.at[1 - role],
        outer_ref.at[core],
        back_sems.at[0, 1],
        back_sems.at[1, core],
        (role, chip + place.along[1]),
    )
    away.start()
    pl.when(mine)(stay.start)
    pl.when(guest)(cross.start)
    third_fold.stage_half(third_half)
    out_fold.stage_half(out_half)
    logits_kept.wait()
    logits_away.wait()
    for copy in handed:
        copy.wait_send()
    away.wait_send()
    pl.when(mine)(stay.wait)
    pl.when(guest)(cross.wait_send)

    def arrived(slot):
        target = outer_ref.at[slot]
        remote(target, target, back_sems.at[0, 0], back_sems.at[1, slot], other).wait_recv()

    arrived(1 - core)
    pl.when(guest)(lambda: arrived(core))
    for moved in (third_fold, out_fold):
        moved.sent_all()


def attention(n_dp, frames, labels, memory, decoded, cotangent, vectors, pairs, third, outs):
    rows, width = decoded.shape
    utts = frames.shape[0]
    length = rows // utts
    low, f32 = jnp.bfloat16, jnp.float32
    line, side = DP_LAYOUTS[n_dp][:2]
    vocab_pad = outs.shape[2]
    third_block, out_block = (width // n_dp, width), (width // n_dp, vocab_pad)
    vocab_half = cotangent.shape[2]
    small = (length, 8, LANES)
    diagonal = (2 * length - 1, 8, LANES)
    dma = pltpu.SemaphoreType.DMA
    return pl.pallas_call(
        functools.partial(attention_kernel, n_dp),
        out_shape=(
            jax.ShapeDtypeStruct((rows, width), low),
            jax.ShapeDtypeStruct((2, rows, width), low),
            jax.ShapeDtypeStruct((2, rows, width), low),
            jax.ShapeDtypeStruct((8, 2 * width), f32),
            jax.ShapeDtypeStruct((2, rows, vocab_pad), low),
            jax.ShapeDtypeStruct((2, utts, length, width), low),
            jax.ShapeDtypeStruct((side, line) + third_block, low),
            jax.ShapeDtypeStruct((side, line) + out_block, low),
        ),
        in_specs=[SMEM_SPEC] * 2 + [VMEM_SPEC] * 4 + [ANY_SPEC] * 3,
        out_specs=(VMEM_SPEC,) * 8,
        scratch_shapes=[
            pltpu.VMEM((rows, width), low),
            pltpu.VMEM((rows, width), low),
            pltpu.VMEM((rows, width), f32),
            pltpu.VMEM((utts, length, vocab_half), low),
            pltpu.VMEM((2, rows, vocab_pad), f32),
            pltpu.VMEM((2, rows, vocab_pad), low),
            pltpu.VMEM((2, rows, vocab_pad), low),
            pltpu.VMEM((2, 2 * width, width), low),
            pltpu.VMEM((2, width, width), low),
            pltpu.VMEM((2, width, vocab_pad), low),
            pltpu.VMEM((2, utts, length, width), low),
            pltpu.VMEM((4, rows, width), low),
            pltpu.VMEM((rows, vocab_pad), low),
            pltpu.VMEM((n_dp,) + third_block, low),
            pltpu.VMEM((n_dp,) + out_block, low),
        ]
        + fold_buffers(line, side, third_block, low)
        + fold_buffers(line, side, out_block, low)
        + [
            pltpu.VMEM((rows, 2 * width), f32),
            pltpu.VMEM((rows, 2 * width), f32),
            pltpu.VMEM((rows, width), f32),
            pltpu.VMEM((rows, width), f32),
            pltpu.VMEM((rows, 2 * width), f32),
            pltpu.VMEM((rows, 2 * width), f32),
            pltpu.VMEM((2,) + small, f32),
            pltpu.VMEM(small, f32),
            pltpu.VMEM(small, f32),
            pltpu.VMEM(diagonal, f32),
            pltpu.VMEM(diagonal, f32),
            pltpu.VMEM(diagonal, f32),
            pltpu.VMEM(diagonal, f32),
            pltpu.VMEM(small, f32),
            pltpu.VMEM(small, f32),
            pltpu.VMEM(small, f32),
            pltpu.VMEM(small, f32),
            pltpu.VMEM(small, f32),
            pltpu.VMEM((2,) + small, f32),
            pltpu.VMEM((rows, LANES), f32),
            pltpu.VMEM((2, rows, length * LANES), f32),
            dma((4,)),
            dma((2,)),
            dma((2, 5)),
            dma((3,)),
            dma((2, 2)),
        ]
        + [fold_sems(line, side)] * 2,
        compiler_params=pltpu.CompilerParams(
            collective_id=2, has_side_effects=True, vmem_limit_bytes=VMEM_LIMIT
        ),
    )(frames, labels, memory, decoded, cotangent, vectors, pairs, third, outs)


def backward_kernel(
    n_dp,
    cell_ref,
    outer_ref,
    dq_ref,
    dk_ref,
    dec_ref,
    mem_ref,
    third_half,
    out_half,
    act_any,
    wt_any,
    ht_ref,
    dpre_ref,
    dpre_other,
    ht_other,
    mats_part,
    third_sum,
    out_sum,
    act_ref,
    wt_ref,
    outer_s,
    state,
    held,
    facts,
    g_mats,
    m_stage,
    m_near,
    m_far,
    t_far,
    t_parts,
    t_end,
    o_far,
    o_parts,
    o_end,
    load_sem,
    fact_sems,
    pre_sems,
    ht_sems,
    sems_m,
    sems_t,
    sems_o,
):
    halves, half, steps, width = outer_ref.shape
    low, f32 = jnp.bfloat16, jnp.float32
    place = Place(n_dp)
    loads = [
        pltpu.make_async_copy(act_any, act_ref, load_sem.at[0]),
        pltpu.make_async_copy(wt_any, wt_ref, load_sem.at[1]),
    ]
    for load in loads:
        load.start()
    place.greet()
    core = place.core
    third, outs = FoldRest(place, third_half, t_far, sems_t), FoldRest(place, out_half, o_far, sems_o)
    third_line, out_line = FoldLine(place, t_parts, t_end, sems_t), FoldLine(place, o_parts, o_end, sems_o)
    third.begin()
    outs.begin()
    other = (1 - core, place.chip)
    sources = [dq_ref.at[1 - core], dk_ref.at[1 - core], dec_ref, mem_ref]
    handed = [
        remote(source, facts.at[n], fact_sems.at[0, n], fact_sems.at[1, n], other)
        for n, source in enumerate(sources)
    ]
    handed.append(remote(ht_ref, ht_other, ht_sems.at[0], ht_sems.at[1], other))
    for copy in handed:
        copy.start()
    state[...] = jnp.zeros_like(state)
    held[...] = jnp.zeros_like(held)
    outer_s[:, halves * half :] = jnp.zeros((steps, ROWS - halves * half, width), f32)
    for u in range(halves * half):
        outer_s[:, u, :] = outer_ref[u // half, u % half].astype(f32)

    def step(k, carry):
        t = steps - 1 - k
        rows = pl.ds(pl.multiple_of(t * ROWS, ROWS), ROWS)
        after = pl.ds(pl.multiple_of((t + 1) * ROWS, ROWS), ROWS)
        hidden_total = outer_s[t]
        for q in range(4):
            hidden_total = hidden_total + jnp.dot(
                state[:, q * width : (q + 1) * width], wt_ref[q], preferred_element_type=f32
            )
        in_gate = act_ref[rows, :width]
        forget = act_ref[rows, width : 2 * width]
        candidate = act_ref[rows, 2 * width : 3 * width]
        out_gate = act_ref[rows, 3 * width :]
        squash = jnp.tanh(cell_ref[after])
        cell_total = held[...] + hidden_total * out_gate * (1.0 - squash * squash)
        held[...] = cell_total * forget
        grads = jnp.concatenate(
            [
                cell_total * candidate * in_gate * (1.0 - in_gate),
                cell_total * cell_ref[rows] * forget * (1.0 - forget),
                cell_total * in_gate * (1.0 - candidate * candidate),
                hidden_total * squash * out_gate * (1.0 - out_gate),
            ],
            -1,
        ).astype(low)
        state[...] = grads
        dpre_ref[rows] = grads
        return carry

    shares = 4
    share = steps // shares

    def hand_over(n):
        top = (steps - (n + 1) * share) * ROWS
        rows = slice(top, top + share * ROWS)
        columns = pl.ds(pl.multiple_of((1 - core) * 2 * width, 2 * width), 2 * width)
        copy = remote(
            dpre_ref.at[rows, columns], dpre_other.at[rows, :], pre_sems.at[0, n], pre_sems.at[1, n], other
        )
        copy.start()
        handed.append(copy)

    part_rows = g_mats.shape[1] // 2

    def matrices():
        for copy in handed[:4]:
            copy.wait_recv()
        pairs = [
            (dq_ref[core], dec_ref[...], facts[0], facts[2]),
            (dk_ref[core], mem_ref[...], facts[1], facts[3]),
        ]
        for m, (a, b, c, d) in enumerate(pairs):
            total = (contract(a, b, 0, 0) + contract(c, d, 0, 0)).astype(low)
            for block in range(n_dp):
                g_mats[block, m * part_rows : (m + 1) * part_rows] = total[
                    block * part_rows : (block + 1) * part_rows
                ]

    mats = Fold(
        place, lambda kz, kf, kg: g_mats[place.block(kz, kf, kg)].astype(f32), m_stage, m_near, m_far, sems_m
    )
    matrices()
    mats.stage_a()
    for load in loads:
        load.wait()
    lines = list(reversed(range(place.line)))
    lax.fori_loop(0, share, step, 0)
    hand_over(0)
    for kz in lines:
        t_parts[kz] = third.summed(kz)
        o_parts[kz] = outs.summed(kz)
    third_line.begin()
    out_line.begin()
    lax.fori_loop(share, 2 * share, step, 0)
    hand_over(1)
    mats.stage_b(*lines[: place.line // 2])
    lax.fori_loop(2 * share, 3 * share, step, 0)
    hand_over(2)
    mats.stage_b(*lines[place.line // 2 :])
    lax.fori_loop(3 * share, steps, step, 0)
    hand_over(3)
    for kz in lines:
        mats_part[kz] = mats.summed(kz)
    third_sum[...] = third_line.result()
    out_sum[...] = out_line.result()
    for copy in handed[4:]:
        copy.wait_recv()
    for copy in handed:
        copy.wait_send()
    for fold in (mats, third, outs, third_line, out_line):
        fold.sent_all()


def backward(n_dp, act, cell, outer, dq, dk, decoded, memory, third_half, out_half, weight_t, ht):
    rows = act.shape[0]
    steps, width = outer.shape[2:]
    low, f32 = jnp.bfloat16, jnp.float32
    line, side = DP_LAYOUTS[n_dp][:2]
    utt_rows = decoded.shape[0]
    mats_block = (2 * width // n_dp, width)
    dma = pltpu.SemaphoreType.DMA
    return pl.pallas_call(
        functools.partial(backward_kernel, n_dp),
        out_shape=(
            jax.ShapeDtypeStruct((rows, 4 * width), low),
            jax.ShapeDtypeStruct((rows, 2 * width), low),
            jax.ShapeDtypeStruct(ht.shape, low),
            jax.ShapeDtypeStruct((line,) + mats_block, low),
            jax.ShapeDtypeStruct(third_half.shape[2:], f32),
            jax.ShapeDtypeStruct(out_half.shape[2:], f32),
        ),
        in_specs=[VMEM_SPEC] * 8 + [ANY_SPEC] * 3,
        out_specs=(VMEM_SPEC, VMEM_SPEC, ANY_SPEC) + (VMEM_SPEC,) * 3,
        scratch_shapes=[
            pltpu.VMEM((rows, 4 * width), f32),
            pltpu.VMEM((4, width, width), low),
            pltpu.VMEM((steps, ROWS, width), f32),
            pltpu.VMEM((ROWS, 4 * width), low),
            pltpu.VMEM((ROWS, width), f32),
            pltpu.VMEM((4, utt_rows, width), low),
            pltpu.VMEM((n_dp,) + mats_block, low),
        ]
        + fold_buffers(line, side, mats_block, low)
        + [pltpu.VMEM((side - 1, line) + mats_block, low)]
        + [
            pltpu.VMEM(count + block, low)
            for block in (third_half.shape[2:], out_half.shape[2:])
            for count in ((side - 1, line), (line,), (line - 1,))
        ]
        + [dma((2,)), dma((2, 4)), dma((2, 4)), dma((2,))]
        + [fold_sems(line, side)] * 3,
        compiler_params=pltpu.CompilerParams(
            collective_id=3, has_side_effects=True, vmem_limit_bytes=VMEM_LIMIT
        ),
    )(cell, outer, dq, dk, decoded, memory, third_half, out_half, act, weight_t, ht)


def update_kernel(
    n_dp,
    batch,
    ht_ref,
    ht_other,
    dpre_ref,
    dpre_other,
    w_ref,
    base_ref,
    spread_ref,
    outer_ref,
    vectors_ref,
    dvec_ref,
    mats_part,
    sum_ref,
    gin_ref,
    vec_sum,
    mats_sum,
    w_s,
    gin_s,
    gin_u,
    vec_s,
    vec_other,
    vec_parts,
    v_stage,
    v_near,
    v_far,
    v_parts,
    v_end,
    m_end,
    w_sem,
    gin_sems,
    vec_sems,
    sems_v,
    sems_m,
    *role,
):
    width = base_ref.shape[1]
    steps = base_ref.shape[0] // ROWS
    low, f32 = jnp.bfloat16, jnp.float32
    place = Place(n_dp)
    load = pltpu.make_async_copy(w_ref, w_s, w_sem)
    load.start()
    place.greet()
    core = place.core
    encoder = place.role == 0
    mine = core == place.role
    block_rows = sum_ref.shape[0]
    half = pl.ds(pl.multiple_of(core * 2 * width, 2 * width), 2 * width)

    count = max(ROWS, block_rows // FOLDS)

    def part(first):
        def at(kz, kf, kg):
            rows = pl.ds(pl.multiple_of(place.block(kz, kf, kg) * block_rows + first, count), count)
            return jnp.dot(ht_ref[rows], dpre_ref[:, half], preferred_element_type=f32) + jnp.dot(
                ht_other[rows], dpre_other[...], preferred_element_type=f32
            )

        return at

    folds = [
        FoldRole(place, part(n * count), stage, near, far, end, sems)
        for n, (stage, near, far, end, sems) in enumerate(zip(*(role[k::5] for k in range(5))))
    ]
    lines = list(reversed(range(place.line)))
    items = [(fold, kz) for kz in lines for fold in folds]
    mats = FoldLine(place, mats_part, m_end, sems_m)
    done = 0

    def advance(until):
        for n in range(done, until):
            if n < len(items):
                items[n][0].stage_a(items[n][1])
            if 0 <= n - LAG < len(items):
                items[n - LAG][0].stage_b(items[n - LAG][1])
            if 0 <= n - LAST_LAG < len(items):
                items[n - LAST_LAG][0].stage_c(items[n - LAST_LAG][1])
        return max(done, until)

    done = advance(LAG + 1)
    mats.begin()

    load.wait()
    gin_s[...] = contract(dpre_ref[...], w_s[...], 1, 1)
    done = advance(LAG + 2)
    input_grad = gin_s[...]
    scaled = base_ref[...]
    vec_s[...] = dvec_ref[...]
    vec_s[4:5, :width] = jnp.where(encoder, jnp.sum(input_grad * scaled, 0, keepdims=True), 0.0)
    vec_s[4:5, width:] = jnp.where(encoder, jnp.sum(input_grad, 0, keepdims=True), 0.0)
    for q in range(4):
        columns = slice((q % 2) * width, (q % 2 + 1) * width)
        bias = jnp.sum(dpre_ref[:, q * width : (q + 1) * width].astype(f32), 0, keepdims=True)
        for role in range(2):
            row = 2 * role + q // 2
            vec_s[row : row + 1, columns] = jnp.where(place.role == role, bias, 0.0)

    @pl.when(encoder)
    def _():
        grads = gin_s[...] * vectors_ref[4:5, :width]
        values = base_ref[...]
        gin_s[...] = (
            spread_ref[:, :1]
            * (
                grads
                - jnp.mean(grads, -1, keepdims=True)
                - values * jnp.mean(grads * values, -1, keepdims=True)
            )
        )

    half_batch = batch // 2
    done = advance(LAG + 3)
    for u in range(batch):
        straight = outer_ref[u // half_batch, u % half_batch].astype(f32)
        gin_u[u] = gin_s[...].reshape(steps, ROWS, width)[:, u, :] + jnp.where(encoder, straight, 0.0)
    kept = pltpu.make_async_copy(gin_u, gin_ref, gin_sems.at[0])
    handed = remote(gin_u, gin_ref, gin_sems.at[1], gin_sems.at[2], (1 - core, place.chip + place.along[1]))

    @pl.when(mine)
    def _():
        kept.start()

    @pl.when(jnp.logical_not(mine))
    def _():
        handed.start()

    own_half = pl.ds(pl.multiple_of(core * width, width), width)
    other_half = pl.ds(pl.multiple_of((1 - core) * width, width), width)
    trade = remote(
        vec_s.at[:, other_half], vec_other, vec_sems.at[0], vec_sems.at[1], (1 - core, place.chip)
    )
    trade.start()
    trade.wait_recv()
    total = vec_s[:, own_half] + vec_other[...]
    piece = width // n_dp
    per_tile = LANES // piece
    for block in range(n_dp):
        tile = total[:, (block // per_tile) * LANES : (block // per_tile + 1) * LANES]
        turn = (block % per_tile) * piece
        vec_parts[block] = pltpu.roll(tile, LANES - turn, 1) if turn else tile
    vecs = Fold(place, lambda kz, kf, kg: vec_parts[place.block(kz, kf, kg)], v_stage, v_near, v_far, sems_v)
    vec_line = FoldLine(place, v_parts, v_end, sems_v)
    vecs.stage_a()
    done = advance(len(items) - 2)
    vecs.stage_b()
    done = advance(len(items) + LAG)
    for n in lines:
        v_parts[n] = vecs.summed(n)
    vec_line.begin()
    done = advance(len(items) + LAST_LAG)
    mats_sum[...] = mats.result()
    vec_sum[...] = vec_line.result()
    for n, fold in enumerate(folds):
        fold.result(sum_ref.at[n * count : (n + 1) * count])

    @pl.when(mine)
    def _():
        kept.wait()

    @pl.when(jnp.logical_not(mine))
    def _():
        handed.wait()

    trade.wait_send()
    for fold in (*folds, vecs, vec_line, mats):
        fold.sent_all()


def update(n_dp, batch, ht, ht_other, dpre, dpre_other, weight, base, spread, outer, vectors, dvec, mats_part):
    rows, width = base.shape
    steps = rows // ROWS
    low, f32 = jnp.bfloat16, jnp.float32
    line, side = DP_LAYOUTS[n_dp][:2]
    block_rows = 2 * width // n_dp
    block = (max(ROWS, block_rows // FOLDS), 2 * width)
    dma = pltpu.SemaphoreType.DMA
    return pl.pallas_call(
        functools.partial(update_kernel, n_dp, batch),
        out_shape=(
            jax.ShapeDtypeStruct((block_rows, 4 * width), f32),
            jax.ShapeDtypeStruct((batch, steps, width), f32),
            jax.ShapeDtypeStruct((8, LANES), f32),
            jax.ShapeDtypeStruct(mats_part.shape[1:], f32),
        ),
        in_specs=[VMEM_SPEC] * 4 + [ANY_SPEC] + [VMEM_SPEC] * 6,
        out_specs=(VMEM_SPEC, ANY_SPEC) + (VMEM_SPEC,) * 2,
        scratch_shapes=[
            pltpu.VMEM((width, 4 * width), low),
            pltpu.VMEM((rows, width), f32),
            pltpu.VMEM((batch, steps, width), f32),
            pltpu.VMEM((8, 2 * width), f32),
            pltpu.VMEM((8, width), f32),
            pltpu.VMEM((n_dp, 8, LANES), f32),
        ]
        + fold_buffers(line, side, (8, LANES), f32)
        + [
            pltpu.VMEM((side - 1, line, 8, LANES), f32),
            pltpu.VMEM((line, 8, LANES), f32),
            pltpu.VMEM((line - 1, 8, LANES), f32),
            pltpu.VMEM((line - 1,) + mats_part.shape[1:], low),
        ]
        + [dma, dma((3,)), dma((2,))]
        + [fold_sems(line, side)] * 2
        + (
            fold_buffers(line, side, block, low)
            + [
                pltpu.VMEM((side - 1, line) + block, low),
                pltpu.VMEM((2, line // 2) + block, low),
                fold_sems(line, side),
            ]
        )
        * (block_rows // block[0]),
        compiler_params=pltpu.CompilerParams(
            collective_id=4, has_side_effects=True, vmem_limit_bytes=VMEM_LIMIT
        ),
    )(ht, ht_other, dpre, dpre_other, weight, base, spread, outer, vectors, dvec, mats_part)


STEP = 5
BETA_ONE = 0.9
BETA_TWO = 0.999
ADAM_EPS = 1e-08
WEIGHT_DECAY = 0.01
RATE_LSTM = 0.05
RATE_MATRIX = 0.02
RATE_VECTOR = 0.3


def adamw(master, first, second, grad, rate):
    first_new = BETA_ONE * first + (1.0 - BETA_ONE) * grad
    second_new = BETA_TWO * second + (1.0 - BETA_TWO) * grad * grad
    first_hat = first_new / (1.0 - BETA_ONE**STEP)
    second_hat = second_new / (1.0 - BETA_TWO**STEP)
    master_new = master - rate * (
        first_hat / (jnp.sqrt(second_hat) + ADAM_EPS) + WEIGHT_DECAY * master
    )
    return (master_new, first_new, second_new)


def local(
    inputs,
    counts,
    cotangent,
    lstm_master,
    lstm_copy,
    lstm_first,
    lstm_second,
    mats_master,
    mats_copy,
    mats_first,
    mats_second,
    out_master,
    out_copy,
    out_first,
    out_second,
    vec_master,
    vec_first,
    vec_second,
):
    low, f32 = jnp.bfloat16, jnp.float32
    n_dp = lax.axis_size("dp")
    on_first = lax.axis_index("section") == 0
    batch_size, length, model_width = inputs.shape[1:]
    half = batch_size // 2
    vocab_half = out_copy.shape[1]
    vocab_pad = -(-vocab_half // LANES) * LANES
    piece = vec_master.shape[1]

    kept = jnp.where(on_first, counts[0, :half], counts[0, half:])
    other = jnp.where(on_first, counts[0, half:], counts[0, :half])
    other = lax.ppermute(other, "section", [(0, 1), (1, 0)])
    frames, labels = jnp.where(on_first, kept, other), jnp.where(on_first, other, kept)

    mats_block = jnp.swapaxes(mats_copy, 1, 2)
    out_block = jnp.pad(out_copy, ((0, 0), (0, vocab_pad - vocab_half)))
    vec_block = jnp.pad(vec_master.astype(low).astype(f32), ((0, 0), (0, LANES - piece)))
    act, cell, ht, base, spread, vectors, pair, weight, weight_t, pairs, third, outs = forward(
        n_dp, inputs[0], lstm_copy[0], mats_block, out_block, vec_block
    )
    memory, decoded = pair.reshape(2, half * length, model_width)
    pairs = pairs.reshape(2, 2 * model_width, model_width)
    third = third.reshape(2, model_width, model_width)
    outs = outs.reshape(2, model_width, vocab_pad)
    dz, dq, dk, vec_rows, logits, outer, third_half, out_half = attention(
        n_dp, frames, labels, memory, decoded, cotangent, vectors, pairs, third, outs
    )
    logits = logits.reshape(batch_size, length, vocab_pad)[..., :vocab_half]
    dpre, dpre_other, ht_other, mats_part, third_sum, out_sum = backward(
        n_dp, act, cell, outer, dq, dk, decoded, memory, third_half, out_half, weight_t, ht
    )
    lstm_sum, inputs_grad, vec_sum, mats_sum = update(
        n_dp,
        batch_size,
        ht,
        ht_other,
        dpre,
        dpre_other,
        weight,
        base.reshape(-1, model_width),
        spread.reshape(-1, LANES),
        outer,
        vectors,
        vec_rows,
        mats_part,
    )
    mats_sum = jnp.concatenate([mats_sum.reshape(2, -1, model_width), third_sum[None]], 0)
    mats_sum = jnp.swapaxes(mats_sum, 1, 2)
    lstm_new, lstm_first_new, lstm_second_new = adamw(
        lstm_master, lstm_first, lstm_second, lstm_sum[None], RATE_LSTM
    )
    mats_new, mats_first_new, mats_second_new = adamw(
        mats_master, mats_first, mats_second, mats_sum, RATE_MATRIX
    )
    out_new, out_first_new, out_second_new = adamw(
        out_master, out_first, out_second, out_sum[:, :vocab_half], RATE_MATRIX
    )
    vec_new, vec_first_new, vec_second_new = adamw(
        vec_master, vec_first, vec_second, vec_sum[:, :piece], RATE_VECTOR
    )
    return (
        logits,
        inputs_grad[None],
        lstm_new,
        lstm_first_new,
        lstm_second_new,
        lstm_new.astype(low),
        mats_new,
        mats_first_new,
        mats_second_new,
        mats_new.astype(low),
        out_new,
        out_first_new,
        out_second_new,
        out_new.astype(low),
        vec_new,
        vec_first_new,
        vec_second_new,
    )


def solution(mesh):
    lstm = P("section", "dp", None)
    mats = P(None, None, ("section", "dp"))
    out = P("dp", "section")
    vec = P(None, ("section", "dp"))
    logits = P("dp", None, "section")
    rows = P("section", "dp", None, None)
    groups = (lstm,) * 4 + (mats,) * 4 + (out,) * 4 + (vec,) * 3
    return jax.shard_map(
        local,
        mesh=mesh,
        in_specs=(rows, P("section", "dp"), logits) + groups,
        out_specs=(logits, rows) + groups,
        check_vma=False,
    )
```

```python
import functools
import jax
import jax.numpy as jnp
from jax import lax
from jax.experimental import pallas as pl
from jax.experimental.pallas import tpu as pltpu
from jax.sharding import PartitionSpec as P

ROWS = 16
LANES = 128
UNROLL = 8
FOLDS = 4
LAG = 2
LAST_LAG = 3
ENERGY_OFFSET = -4.0
NORM_EPS = 1e-05
VMEM_SPEC = pl.BlockSpec(memory_space=pltpu.VMEM)
SMEM_SPEC = pl.BlockSpec(memory_space=pltpu.SMEM)
VMEM_LIMIT = 60 * 1024 * 1024


def contract(left, right, left_dim, right_dim):
    return lax.dot_general(
        left, right, (((left_dim,), (right_dim,)), ((), ())), preferred_element_type=jnp.float32
    )


MESH_ID = pl.DeviceIdType.MESH
ANY_SPEC = pl.BlockSpec(memory_space=pl.ANY)
DP_LAYOUTS = {16: (4, 2, 1, 2), 128: (8, 4, 1, 32)}
LINE_STRIDE = 4
TURN = 256
CHUNKS = 2


def flipped(value, k):
    result = value
    bit = 1
    while bit <= k:
        if k & bit:
            result = result + bit - 2 * bit * lax.rem(value // bit, 2)
        bit *= 2
    return result


class Place:
    def __init__(self, n_dp):
        self.line, self.side, stride_a, stride_b = DP_LAYOUTS[n_dp]
        self.core = lax.axis_index("section")
        self.chip = lax.axis_index("dp")
        self.z = lax.rem(self.chip // LINE_STRIDE, self.line)
        at_a = lax.rem(self.chip // stride_a, self.side)
        at_b = lax.rem(self.chip // stride_b, self.side)
        self.role = lax.rem(self.z, 2)
        moves_a = [(flipped(at_a, k) - at_a) * stride_a for k in range(self.side)]
        moves_b = [(flipped(at_b, k) - at_b) * stride_b for k in range(self.side)]
        core = self.core
        self.first = [a + (b - a) * core for a, b in zip(moves_a, moves_b)]
        self.second = [b + (a - b) * core for a, b in zip(moves_a, moves_b)]
        self.along = [(flipped(self.z, k) - self.z) * LINE_STRIDE for k in range(self.line)]

    def block(self, kz, kf=0, kg=0):
        return self.chip + self.along[kz] + self.first[kf] + self.second[kg]

    def other_block(self, kz, kf=0, kg=0):
        return self.chip + self.along[kz] + self.second[kf] + self.first[kg]

    def greet(self):
        barrier = pltpu.get_barrier_semaphore()
        peers = [(1 - self.core, self.chip)]
        for k in range(1, self.line):
            peers += [(0, self.chip + self.along[k]), (1, self.chip + self.along[k])]
        for k in range(1, self.side):
            peers += [(self.core, self.chip + self.first[k]), (self.core, self.chip + self.second[k])]
        for peer in peers:
            pl.semaphore_signal(barrier, inc=1, device_id=peer, device_id_type=MESH_ID)
        pl.semaphore_wait(barrier, len(peers))


def remote(source, target, send, receive, device):
    return pltpu.make_async_remote_copy(
        src_ref=source,
        dst_ref=target,
        send_sem=send,
        recv_sem=receive,
        device_id=device,
        device_id_type=MESH_ID,
    )


class Spread:
    def __init__(self, place, here, there, sems):
        self.place, self.here, self.there, self.sems = place, here, there, sems
        self.sent = []

    def send(self, target, device, send, receive):
        copy = remote(target, target, send, receive, device)
        copy.start()
        self.sent.append(copy)

    def arrived(self, target, semaphore):
        place = self.place
        remote(target, target, semaphore, semaphore, (1 - place.core, place.chip)).wait_recv()

    def to_second(self, kz, kf):
        place = self.place
        target = self.here(place.block(kz, kf))
        for kg in range(1, place.side):
            self.send(
                target,
                (place.core, place.chip + place.second[kg]),
                self.sems["gs"].at[kg, kf, kz],
                self.sems["gr"].at[kg, kf, kz],
            )

    def to_core(self, kz, kf, kg):
        place = self.place
        self.send(
            self.here(place.block(kz, kf, kg)),
            (1 - place.core, place.chip),
            self.sems["cs"].at[kg, kf, kz],
            self.sems["cr"].at[kg, kf, kz],
        )

    def stage_one(self, *steps):
        place = self.place
        for kz in steps or range(place.line):
            self.wait_line(kz)
            target = self.here(place.block(kz))
            for kf in range(1, place.side):
                self.send(
                    target,
                    (place.core, place.chip + place.first[kf]),
                    self.sems["fs"].at[kf, kz],
                    self.sems["fr"].at[kf, kz],
                )
            self.to_second(kz, 0)
            self.to_core(kz, 0, 0)

    def stage_two(self):
        place = self.place
        for kf in range(1, place.side):
            for kz in range(place.line):
                self.arrived(self.here(place.block(kz, kf)), self.sems["fr"].at[kf, kz])
                self.to_second(kz, kf)
                self.to_core(kz, kf, 0)

    def stage_three(self):
        place = self.place
        for kg in range(1, place.side):
            for kf in range(place.side):
                for kz in range(place.line):
                    self.arrived(self.here(place.block(kz, kf, kg)), self.sems["gr"].at[kg, kf, kz])
                    self.to_core(kz, kf, kg)

    def finish(self):
        place = self.place
        for kg in range(place.side):
            for kf in range(place.side):
                for kz in range(place.line):
                    self.arrived(self.there(place.other_block(kz, kf, kg)), self.sems["cr"].at[kg, kf, kz])

    def sent_all(self):
        for copy in self.sent:
            copy.wait_send()


def spread_sems(line, side, last=False):
    dma = pltpu.SemaphoreType.DMA
    ends = {"ls": dma((side, side, line)), "lr": dma((side, side, line))}
    return (ends if last else {}) | {
        "zs": dma((line, 2)),
        "zr": dma((line,)),
        "fs": dma((side, line)),
        "fr": dma((side, line)),
        "gs": dma((side, side, line)),
        "gr": dma((side, side, line)),
        "cs": dma((side, side, line)),
        "cr": dma((side, side, line)),
    }


def spread_even(place, source, at, sems):
    own = at(place.core, place.chip)
    spread = Spread(place, lambda block: at(place.core, block), lambda block: at(1 - place.core, block), sems)
    kept = pltpu.make_async_copy(source, own, sems["zr"].at[0])
    copies = [
        remote(source, own, sems["zs"].at[k, 0], sems["zr"].at[k], (place.core, place.chip + place.along[k]))
        for k in range(1, place.line)
    ]

    def begin():
        kept.start()
        for copy in copies:
            copy.start()
        spread.sent += copies

    def wait_line(kz):
        if kz == 0:
            kept.wait()
        else:
            spread.arrived(spread.here(place.block(kz)), sems["zr"].at[kz])

    spread.begin = begin
    spread.wait_line = wait_line
    return spread


class SpreadLast(Spread):
    def __init__(self, place, source, at, sems):
        super().__init__(place, lambda block: at(place.core, block), lambda block: at(1 - place.core, block), sems)
        self.source = source
        self.kept = pltpu.make_async_copy(source, self.here(place.chip), sems["zr"].at[0])

    def begin(self):
        place = self.place
        self.kept.start()
        own = self.here(place.chip)
        for k in range(1, place.side):
            for moves, send, receive in (
                (place.first, self.sems["fs"].at[k, 0], self.sems["fr"].at[k, 0]),
                (place.second, self.sems["gs"].at[k, 0, 0], self.sems["gr"].at[k, 0, 0]),
            ):
                copy = remote(self.source, own, send, receive, (place.core, place.chip + moves[k]))
                copy.start()
                self.sent.append(copy)

    def stage_plane(self):
        for kf in range(1, self.place.side):
            self.arrived(self.here(self.place.block(0, kf)), self.sems["fr"].at[kf, 0])
            self.to_second(0, kf)

    def stage_line(self):
        place = self.place
        self.kept.wait()
        for kg in range(place.side):
            for kf in range(place.side):
                target = self.here(place.block(0, kf, kg))
                if kg:
                    self.arrived(target, self.sems["gr"].at[kg, kf, 0])
                for kz in reversed(range(1, place.line)):
                    self.send(
                        target,
                        (place.core, place.chip + place.along[kz]),
                        self.sems["ls"].at[kg, kf, kz],
                        self.sems["lr"].at[kg, kf, kz],
                    )
                self.to_core(0, kf, kg)

    def stage_core(self):
        place = self.place
        for kg in range(place.side):
            for kf in range(place.side):
                for kz in range(1, place.line):
                    self.arrived(self.here(place.block(kz, kf, kg)), self.sems["lr"].at[kg, kf, kz])
                    self.to_core(kz, kf, kg)


def spread_role(place, source, target, sems, rows, half, first, count):
    source = source.at[first : first + count]

    def columns(core):
        return pl.ds(pl.multiple_of(core * half, half), half)

    def at(block, core):
        return target.at[pl.ds(pl.multiple_of(block * rows + first, count), count), columns(core)]

    spread = Spread(
        place, lambda block: at(block, place.core), lambda block: at(block, 1 - place.core), sems
    )
    mine = place.role == place.core
    kept = pltpu.make_async_copy(source.at[:, columns(place.core)], at(place.chip, place.core), sems["zr"].at[0])
    cross = remote(
        source.at[:, columns(1 - place.core)],
        at(place.chip, 1 - place.core),
        sems["zs"].at[0, 0],
        sems["zr"].at[0],
        (1 - place.core, place.chip),
    )
    copies = [
        [
            remote(
                source.at[:, columns(core)],
                at(place.chip, core),
                sems["zs"].at[k, core],
                sems["zr"].at[k],
                (core, place.chip + place.along[k]),
            )
            for core in range(2)
        ]
        for k in range(1, place.line)
    ]

    guest = jnp.logical_not(mine)

    def each(condition, steps, action):
        @pl.when(condition)
        def _():
            for k in steps:
                for copy in copies[k - 1] if k else [cross]:
                    action(copy)

    def start(copy):
        copy.start()

    def begin():
        @pl.when(mine)
        def _():
            kept.start()

        each(mine, range(0, place.line, 2), start)
        each(guest, range(1, place.line, 2), start)

    def wait_line(kz):
        if kz == 0:

            @pl.when(mine)
            def _():
                kept.wait()

            @pl.when(jnp.logical_not(mine))
            def _():
                spread.arrived(spread.here(place.chip), sems["zr"].at[0])

        else:
            spread.arrived(spread.here(place.block(kz)), sems["zr"].at[kz])

    def finished(copy):
        copy.wait_send()

    def sent_line():
        each(mine, range(0, place.line, 2), finished)
        each(guest, range(1, place.line, 2), finished)

    spread.begin = begin
    spread.wait_line = wait_line
    spread.sent_line = sent_line
    return spread


def forward_kernel(
    n_dp,
    seq_ref,
    shard_ref,
    mats_ref,
    out_part,
    vec_part,
    act_out,
    cell_ref,
    ht_ref,
    base_ref,
    spread_ref,
    vectors_ref,
    pair_ref,
    w_out,
    wt_out,
    mats_out,
    third_out,
    out_out,
    out_ref,
    vec_ref,
    act_ref,
    seq_s,
    result_s,
    x_s,
    h_s,
    w_s,
    wt_s,
    vec_s,
    state,
    keep_sem,
    seq_sem,
    pair_sem,
    sems_m,
    sems_v,
    sems_n,
    sems_o,
    *sems_w,
):
    batch, steps, width = seq_ref.shape
    low, f32 = jnp.bfloat16, jnp.float32
    place = Place(n_dp)
    core, chip = place.core, place.chip
    mine = core == place.role
    guest = jnp.logical_not(mine)
    encoder = place.role == 0
    piece = vec_part.shape[1]
    vec_ref[...] = jnp.zeros_like(vec_ref)
    vec_ref[:, :piece] = vec_part[...].astype(low).astype(f32)
    out_ref[...] = jnp.zeros_like(out_ref)
    out_ref[:, : out_part.shape[1]] = out_part[...]
    place.greet()
    rows = shard_ref.shape[0]
    count = max(ROWS, rows // CHUNKS)
    matrix = [
        spread_role(place, shard_ref, w_s, sems, rows, 2 * width, n * count, count)
        for n, sems in zip(range(rows // count), sems_w)
    ]
    mats = spread_even(place, mats_ref.at[:2], lambda core, chip: mats_out.at[:, core, chip], sems_m)
    vecs = spread_even(place, vec_ref, lambda core, chip: vec_s.at[core, chip], sems_v)
    thirds = SpreadLast(place, mats_ref.at[2], lambda core, chip: third_out.at[core, chip], sems_n)
    outs = spread_even(place, out_ref, lambda core, chip: out_out.at[core, chip], sems_o)
    vecs.begin()
    for part in matrix:
        part.begin()
    seq_kept = pltpu.make_async_copy(seq_ref, seq_s, seq_sem.at[0])
    seq_away = remote(seq_ref, seq_s, seq_sem.at[1], seq_sem.at[2], (1 - core, chip + place.along[1]))
    pl.when(mine)(seq_kept.start)
    pl.when(guest)(seq_away.start)
    thirds.begin()
    for part in matrix:
        part.stage_one(0)
    state[...] = jnp.zeros_like(state)
    cell_ref[:ROWS] = jnp.zeros((ROWS, width), f32)
    base_ref[:, batch:] = jnp.zeros((steps, ROWS - batch, width), f32)
    spread_ref[...] = jnp.zeros_like(spread_ref)
    line_rest = range(1, place.line)
    thirds.stage_plane()
    for n in range(len(matrix) + 2):
        if n < len(matrix):
            matrix[n].stage_one(*line_rest)
        if n == 0:
            vecs.stage_one()
        if n == len(matrix) - 1:
            mats.begin()
            outs.begin()
        if 1 <= n <= len(matrix):
            matrix[n - 1].stage_two()
        if n == 1:
            vecs.stage_two()
        if n >= 2:
            matrix[n - 2].stage_three()
    mats.stage_one(0)
    thirds.stage_line()
    pl.when(mine)(seq_kept.wait)
    pl.when(guest)(seq_away.wait)
    for u in range(batch):
        raw = seq_s[u].astype(f32)
        center = raw - jnp.mean(raw, -1, keepdims=True)
        spread = lax.rsqrt(jnp.mean(center * center, -1, keepdims=True) + NORM_EPS)
        base_ref[:, u, :] = jnp.where(encoder, center * spread, raw)
        spread_ref[:, u, :] = jnp.broadcast_to(spread, (steps, LANES))
    vecs.stage_three()
    vecs.finish()
    per_tile = LANES // piece
    for m in range(2 * width // LANES):
        tile = jnp.zeros((8, LANES), f32)
        for k in range(per_tile):
            index = m * per_tile + k
            block = vec_s[index // n_dp, index % n_dp]
            tile = tile + (pltpu.roll(block, k * piece, 1) if k else block)
        vectors_ref[:, m * LANES : (m + 1) * LANES] = tile
    gain = jnp.where(encoder, vectors_ref[4:5, :width], 1.0)
    shift = jnp.where(encoder, vectors_ref[4:5, width:], 0.0)
    x_s[...] = (base_ref[...].reshape(steps * ROWS, width) * gain + shift).astype(low)
    ht_ref[:width] = x_s[...].T
    for part in matrix:
        part.finish()
    keep = pltpu.make_async_copy(w_s.at[:width], w_out, keep_sem.at[0])
    keep.start()
    for q in range(4):
        columns = slice(q * width, (q + 1) * width)
        row = q // 2
        bias_columns = slice((q % 2) * width, (q % 2 + 1) * width)
        bias = jnp.where(
            encoder, vectors_ref[row : row + 1, bias_columns], vectors_ref[row + 2 : row + 3, bias_columns]
        )
        act_ref[:, columns] = jnp.dot(x_s[...], w_s[:width, columns], preferred_element_type=f32) + bias

    def step(t, carry):
        rows = pl.ds(pl.multiple_of(t * ROWS, ROWS), ROWS)
        after = pl.ds(pl.multiple_of((t + 1) * ROWS, ROWS), ROWS)
        hidden = state[...]

        def gate(q):
            columns = slice(q * width, (q + 1) * width)
            return act_ref[rows, columns] + jnp.dot(hidden, w_s[width:, columns], preferred_element_type=f32)

        in_gate = jax.nn.sigmoid(gate(0))
        forget = jax.nn.sigmoid(gate(1))
        candidate = jnp.tanh(gate(2))
        cell = forget * cell_ref[rows] + in_gate * candidate
        out_gate = jax.nn.sigmoid(gate(3))
        hidden_new = (out_gate * jnp.tanh(cell)).astype(low)
        act_ref[rows, :width] = in_gate
        act_ref[rows, width : 2 * width] = forget
        act_ref[rows, 2 * width : 3 * width] = candidate
        act_ref[rows, 3 * width :] = out_gate
        cell_ref[after] = cell
        h_s[after] = hidden_new
        state[...] = hidden_new
        return carry

    h_s[:ROWS] = jnp.zeros((ROWS, width), low)
    marks = [steps * n // 24 for n in (0, 8, 12, 18, 24)]
    gates_out = []

    def run(n):
        lax.fori_loop(marks[n], marks[n + 1], step, 0)
        rows = slice(marks[n] * ROWS, marks[n + 1] * ROWS)
        gates_out.append(pltpu.make_async_copy(act_ref.at[rows], act_out.at[rows], keep_sem.at[2 + n]))
        gates_out[-1].start()

    mats.stage_one(*line_rest)
    run(0)
    mats.stage_two()
    outs.stage_one()
    run(1)
    outs.stage_two()
    run(2)
    mats.stage_three()
    run(3)
    turned = h_s[ROWS:].astype(f32).reshape(steps, ROWS, width)
    for u in range(batch):
        value = turned[:, u, :]
        result_s[u] = jnp.where(encoder, seq_s[u].astype(f32) + value, value).astype(low)
    half = batch // 2
    for h in range(2):
        home = jnp.logical_and(mine, core == h)
        source, target = result_s.at[h * half : (h + 1) * half], pair_ref.at[place.role]
        stay = pltpu.make_async_copy(source, target, pair_sem.at[0, h])
        leave = remote(
            source,
            target,
            pair_sem.at[0, h],
            pair_sem.at[1, place.role],
            (h, jnp.where(mine, chip, chip + place.along[1])),
        )
        pl.when(home)(stay.start)
        pl.when(jnp.logical_not(home))(leave.start)
    for q in range(4):
        for n in range(width // TURN):
            rows = slice(width + n * TURN, width + (n + 1) * TURN)
            wt_s[q, :, n * TURN : (n + 1) * TURN] = w_s[rows, q * width : (q + 1) * width].T
    keep_turned = pltpu.make_async_copy(wt_s, wt_out, keep_sem.at[1])
    keep_turned.start()
    ht_ref[width:] = h_s[:-ROWS].T
    outs.stage_three()
    thirds.stage_core()
    mats.finish()
    outs.finish()
    thirds.finish()
    for h in range(2):
        home = jnp.logical_and(mine, core == h)
        source, target = result_s.at[h * half : (h + 1) * half], pair_ref.at[place.role]
        stay = pltpu.make_async_copy(source, target, pair_sem.at[0, h])
        leave = remote(
            source,
            target,
            pair_sem.at[0, h],
            pair_sem.at[1, place.role],
            (h, jnp.where(mine, chip, chip + place.along[1])),
        )
        pl.when(home)(stay.wait)
        pl.when(jnp.logical_not(home))(leave.wait_send)

    def arrived(section):
        target = pair_ref.at[section]
        remote(target, target, pair_sem.at[0, 0], pair_sem.at[1, section], (1 - core, chip)).wait_recv()

    pl.when(guest)(lambda: arrived(place.role))
    arrived(1 - place.role)
    keep.wait()
    keep_turned.wait()
    for copy in gates_out:
        copy.wait()
    for part in matrix:
        part.sent_line()
    for spread in (*matrix, vecs, mats, thirds, outs):
        spread.sent_all()


def forward(n_dp, seq, shard, mats_block, out_block, vec_block):
    batch, steps, width = seq.shape
    rows = steps * ROWS
    low, f32 = jnp.bfloat16, jnp.float32
    line, side = DP_LAYOUTS[n_dp][:2]
    columns = mats_block.shape[1]
    out_shape = (out_block.shape[0], -(-out_block.shape[1] // LANES) * LANES)
    dma = pltpu.SemaphoreType.DMA
    return pl.pallas_call(
        functools.partial(forward_kernel, n_dp),
        out_shape=(
            jax.ShapeDtypeStruct((rows, 4 * width), f32),
            jax.ShapeDtypeStruct((rows + ROWS, width), f32),
            jax.ShapeDtypeStruct((2 * width, rows), low),
            jax.ShapeDtypeStruct((steps, ROWS, width), f32),
            jax.ShapeDtypeStruct((steps, ROWS, LANES), f32),
            jax.ShapeDtypeStruct((8, 2 * width), f32),
            jax.ShapeDtypeStruct((2, batch // 2, steps, width), low),
            jax.ShapeDtypeStruct((width, 4 * width), low),
            jax.ShapeDtypeStruct((4, width, width), low),
            jax.ShapeDtypeStruct((2, 2, n_dp, columns, width), low),
            jax.ShapeDtypeStruct((2, n_dp, columns, width), low),
            jax.ShapeDtypeStruct((2, n_dp) + out_shape, low),
        ),
        in_specs=[VMEM_SPEC, ANY_SPEC, ANY_SPEC, VMEM_SPEC, VMEM_SPEC],
        out_specs=(ANY_SPEC,) + (VMEM_SPEC,) * 6 + (ANY_SPEC,) * 5,
        scratch_shapes=[
            pltpu.VMEM(out_shape, low),
            pltpu.VMEM((8, LANES), f32),
            pltpu.VMEM((rows, 4 * width), f32),
            pltpu.VMEM((batch, steps, width), low),
            pltpu.VMEM((batch, steps, width), low),
            pltpu.VMEM((rows, width), low),
            pltpu.VMEM((rows + ROWS, width), low),
            pltpu.VMEM((2 * width, 4 * width), low),
            pltpu.VMEM((4, width, width), low),
            pltpu.VMEM((2, n_dp, 8, LANES), f32),
            pltpu.VMEM((ROWS, width), low),
            dma((6,)),
            dma((3,)),
            dma((2, 2)),
        ]
        + [spread_sems(line, side)] * 2
        + [spread_sems(line, side, last=True)]
        + [spread_sems(line, side)] * (1 + shard.shape[0] // max(ROWS, shard.shape[0] // CHUNKS)),
        compiler_params=pltpu.CompilerParams(
            collective_id=1, has_side_effects=True, vmem_limit_bytes=VMEM_LIMIT
        ),
    )(seq, shard, mats_block, out_block, vec_block)


class Fold:
    def __init__(self, place, part, stage, near, far, sems):
        self.place, self.part, self.stage, self.near, self.far, self.sems = place, part, stage, near, far, sems
        self.sent = []

    def send(self, source, target, device, send, receive):
        copy = remote(source, target, send, receive, device)
        copy.start()
        self.sent.append(copy)

    def arrived(self, target, semaphore):
        place = self.place
        remote(target, target, semaphore, semaphore, (1 - place.core, place.chip)).wait_recv()

    def stage_a(self, *steps):
        place = self.place
        for kz in steps or reversed(range(place.line)):
            for kg in range(1, place.side):
                for kf in reversed(range(place.side)):
                    if callable(self.stage):
                        source = self.stage(kz, kf, kg)
                    else:
                        source = self.stage.at[kg - 1, kf, kz]
                        source[...] = self.part(kz, kf, kg).astype(source.dtype)
                    self.send(
                        source,
                        self.near.at[kg - 1, kf, kz],
                        (place.core, place.chip + place.second[kg]),
                        self.sems["gs"].at[kg, kf, kz],
                        self.sems["gr"].at[kg, kf, kz],
                    )

    def stage_b(self, *steps):
        place = self.place
        for kz in steps or reversed(range(place.line)):
            for kf in reversed(range(place.side)):
                total = self.part(kz, kf, 0)
                for kg in range(1, place.side):
                    self.arrived(self.near.at[kg - 1, kf, kz], self.sems["gr"].at[kg, kf, kz])
                    total = total + self.near[kg - 1, kf, kz].astype(jnp.float32)
                source = self.near.at[0, kf, kz]
                source[...] = total.astype(source.dtype)
                if kf:
                    self.send(
                        source,
                        self.far.at[kf - 1, kz],
                        (place.core, place.chip + place.first[kf]),
                        self.sems["fs"].at[kf, kz],
                        self.sems["fr"].at[kf, kz],
                    )

    def stage_half(self, half_ref):
        place = self.place
        for kz in range(place.line):
            for kf in range(place.side):
                total = self.part(kz, kf, 0)
                for kg in range(1, place.side):
                    self.arrived(self.near.at[kg - 1, kf, kz], self.sems["gr"].at[kg, kf, kz])
                    total = total + self.near[kg - 1, kf, kz].astype(jnp.float32)
                half_ref[kf, kz] = total.astype(half_ref.dtype)

    def summed(self, kz):
        place = self.place
        total = self.near[0, 0, kz].astype(jnp.float32)
        for kf in range(1, place.side):
            self.arrived(self.far.at[kf - 1, kz], self.sems["fr"].at[kf, kz])
            total = total + self.far[kf - 1, kz].astype(jnp.float32)
        return total.astype(self.far.dtype)

    def sent_all(self):
        for copy in self.sent:
            copy.wait_send()


class FoldRest(Fold):
    def __init__(self, place, half_ref, far, sems):
        super().__init__(place, None, None, None, far, sems)
        self.half_ref = half_ref

    def begin(self):
        place = self.place
        for kz in range(place.line):
            for kf in range(1, place.side):
                self.send(
                    self.half_ref.at[kf, kz],
                    self.far.at[kf - 1, kz],
                    (place.core, place.chip + place.first[kf]),
                    self.sems["fs"].at[kf, kz],
                    self.sems["fr"].at[kf, kz],
                )

    def summed(self, kz):
        total = self.half_ref[0, kz].astype(jnp.float32)
        for kf in range(1, self.place.side):
            self.arrived(self.far.at[kf - 1, kz], self.sems["fr"].at[kf, kz])
            total = total + self.far[kf - 1, kz].astype(jnp.float32)
        return total.astype(self.far.dtype)


class FoldLine:
    def __init__(self, place, parts, end, sems):
        self.place, self.parts, self.end, self.sems = place, parts, end, sems

    def begin(self, *steps):
        place = self.place
        for kz in steps or reversed(range(1, place.line)):
            self.copy(kz).start()

    def copy(self, kz):
        place = self.place
        return remote(
            self.parts.at[kz],
            self.end.at[kz - 1],
            self.sems["zs"].at[kz, 0],
            self.sems["zr"].at[kz],
            (place.core, place.chip + place.along[kz]),
        )

    def result(self):
        total = self.parts[0].astype(jnp.float32)
        for kz in range(1, self.place.line):
            self.copy(kz).wait_recv()
            total = total + self.end[kz - 1].astype(jnp.float32)
        return total

    def sent_all(self):
        for kz in range(1, self.place.line):
            self.copy(kz).wait_send()


class FoldFirst(Fold):
    def __init__(self, place, term, ends, near, far, sems):
        super().__init__(place, None, term, near, far, sems)
        self.ends = ends

    def begin(self):
        place = self.place
        for kz in reversed(range(1, place.line)):
            for kg in reversed(range(place.side)):
                for kf in reversed(range(place.side)):
                    self.send(
                        self.stage(kz, kf, kg),
                        self.ends.at[kz - 1, kg, kf],
                        (place.core, place.chip + place.along[kz]),
                        self.sems["ls"].at[kg, kf, kz],
                        self.sems["lr"].at[kg, kf, kz],
                    )

    def stage_line(self):
        place = self.place
        for kg in reversed(range(place.side)):
            for kf in reversed(range(place.side)):
                total = self.stage(0, kf, kg)[...].astype(jnp.float32)
                for kz in range(1, place.line):
                    self.arrived(self.ends.at[kz - 1, kg, kf], self.sems["lr"].at[kg, kf, kz])
                    total = total + self.ends[kz - 1, kg, kf].astype(jnp.float32)
                source = self.ends.at[0, kg, kf]
                source[...] = total.astype(source.dtype)
                if kg:
                    self.send(
                        source,
                        self.near.at[kg - 1, kf],
                        (place.core, place.chip + place.second[kg]),
                        self.sems["gs"].at[kg, kf, 0],
                        self.sems["gr"].at[kg, kf, 0],
                    )

    def stage_second(self):
        place = self.place
        for kf in reversed(range(place.side)):
            total = self.ends[0, 0, kf].astype(jnp.float32)
            for kg in range(1, place.side):
                self.arrived(self.near.at[kg - 1, kf], self.sems["gr"].at[kg, kf, 0])
                total = total + self.near[kg - 1, kf].astype(jnp.float32)
            source = self.near.at[0, kf]
            source[...] = total.astype(source.dtype)
            if kf:
                self.send(
                    source,
                    self.far.at[kf - 1],
                    (place.core, place.chip + place.first[kf]),
                    self.sems["fs"].at[kf, 0],
                    self.sems["fr"].at[kf, 0],
                )

    def result(self):
        total = self.near[0, 0].astype(jnp.float32)
        for kf in range(1, self.place.side):
            self.arrived(self.far.at[kf - 1], self.sems["fr"].at[kf, 0])
            total = total + self.far[kf - 1].astype(jnp.float32)
        return total


class FoldRole(Fold):
    def __init__(self, place, part, stage, near, far, end, sems):
        super().__init__(place, part, stage, near, far, sems)
        self.end = end

    def stage_c(self, kz):
        place = self.place
        source = self.far.at[0, kz]
        source[...] = self.summed(kz)
        if kz:
            self.send(
                source,
                self.end.at[place.core, kz // 2],
                (place.role, place.chip + place.along[kz]),
                self.sems["zs"].at[kz, 0],
                self.sems["er"].at[place.core, kz // 2],
            )
        else:
            self.last = source
            self.cross = remote(
                source,
                self.end.at[place.core, 0],
                self.sems["zs"].at[0, 0],
                self.sems["er"].at[place.core, 0],
                (1 - place.core, place.chip),
            )

            @pl.when(place.core != place.role)
            def _():
                self.cross.start()

    def result(self, sum_ref):
        place = self.place
        rows, half = self.end.shape[2:]
        mine = place.core == place.role

        def columns(core):
            return pl.ds(pl.multiple_of(core * half, half), half)

        def add(parity):
            sources = [kz for kz in range(place.line) if kz % 2 == parity]
            for core in range(2):
                total = jnp.zeros((rows, half), jnp.float32)
                for kz in sources:
                    if kz:
                        self.arrived(self.end.at[core, kz // 2], self.sems["er"].at[core, kz // 2])
                        total = total + self.end[core, kz // 2].astype(jnp.float32)
                sum_ref[:, core * half : (core + 1) * half] = total

        @pl.when(mine)
        def _():
            add(0)
            own, other = columns(place.core), columns(1 - place.core)
            sum_ref[:, own] += self.last[...].astype(jnp.float32)
            self.arrived(self.end.at[1 - place.core, 0], self.sems["er"].at[1 - place.core, 0])
            sum_ref[:, other] += self.end[1 - place.core, 0].astype(jnp.float32)

        @pl.when(jnp.logical_not(mine))
        def _():
            add(1)
            self.cross.wait_send()


def fold_sems(line, side, first=False):
    dma = pltpu.SemaphoreType.DMA
    ends = {"ls": dma((side, side, line)), "lr": dma((side, side, line))}
    return (ends if first else {}) | {
        "gs": dma((side, side, line)),
        "gr": dma((side, side, line)),
        "fs": dma((side, line)),
        "fr": dma((side, line)),
        "zs": dma((line, 1)),
        "zr": dma((line,)),
        "er": dma((2, line // 2)),
    }


def fold_buffers(line, side, shape, dtype):
    return [
        pltpu.VMEM((side - 1, side, line) + shape, dtype),
        pltpu.VMEM((side - 1, side, line) + shape, dtype),
    ]


def attention_kernel(
    n_dp,
    frames_ref,
    labels_ref,
    pair_ref,
    cot_ref,
    vec_ref,
    pairs_any,
    third_any,
    out_any,
    dz_ref,
    dq_ref,
    dk_ref,
    dvec_ref,
    logits_ref,
    outer_ref,
    third_half,
    out_half,
    squash_ref,
    context_ref,
    ddec_ref,
    cot_s,
    gl_f,
    gl_ref,
    own_logits,
    mats_ref,
    third_s,
    out_s,
    back_s,
    facts,
    facts_gl,
    g_third,
    g_out,
    t_stage,
    t_near,
    o_stage,
    o_near,
    q_s,
    k_s,
    mem_s,
    ctx_s,
    dqa_s,
    dka_s,
    e_s,
    sel_s,
    prob_s,
    sel_d,
    prob_d,
    reach_d,
    back_d,
    w_s,
    a_s,
    own_s,
    nxt_s,
    g_s,
    d_s,
    d_rows,
    bc_s,
    load_sem,
    cot_sems,
    fact_sems,
    logit_sems,
    back_sems,
    sems_ft,
    sems_fo,
):
    mem_ref, dec_ref = pair_ref.at[0], pair_ref.at[1]
    rows, width = dec_ref.shape
    utts = frames_ref.shape[0]
    length = rows // utts
    vocab_half = cot_ref.shape[2]
    vocab_pad = gl_f.shape[2]
    low = jnp.bfloat16
    f32 = jnp.float32
    lane = lax.broadcasted_iota(jnp.int32, (length, LANES), 1)
    lane_block = lax.broadcasted_iota(jnp.int32, (length, 8, LANES), 2)

    place = Place(n_dp)
    core, chip = place.core, place.chip
    other = (1 - core, chip)
    loads = [
        pltpu.make_async_copy(pairs_any.at[0], mats_ref.at[0], load_sem.at[0]),
        pltpu.make_async_copy(pairs_any.at[1], mats_ref.at[1], load_sem.at[1]),
        pltpu.make_async_copy(third_any, third_s, load_sem.at[2]),
        pltpu.make_async_copy(out_any, out_s, load_sem.at[3]),
    ]
    for load in loads:
        load.start()
    place.greet()
    cot_away = remote(
        cot_ref.at[pl.ds((1 - core) * utts, utts)], cot_s, cot_sems.at[0], cot_sems.at[1], other
    )
    cot_away.start()
    loads[0].wait()
    q_s[...] = contract(dec_ref[...], mats_ref[0], 1, 1) + vec_ref[5:6]
    loads[1].wait()
    k_s[...] = contract(mem_ref[...], mats_ref[1], 1, 1)
    mem_s[...] = mem_ref[...].astype(f32)
    e_s[...] = jnp.zeros_like(e_s)
    d_s[...] = jnp.zeros_like(d_s)

    tile = 256
    group = 4

    gl_f[...] = jnp.zeros_like(gl_f)
    cot_away.wait()
    slot = lax.broadcasted_iota(jnp.int32, (length, 1), 0)
    for u in range(utts):
        keep = (slot < labels_ref[u]).astype(f32)
        at = slice(u * length, (u + 1) * length)
        gl_f[core, at, :vocab_half] = cot_ref[core * utts + u].astype(f32) * keep
        gl_f[1 - core, at, :vocab_half] = cot_s[u].astype(f32) * keep
    gl_ref[...] = gl_f[...].astype(low)

    for u in range(utts):
        at = u * length

        def energy_step(block, sums, at=at):
            base = block * group
            for offset in range(group):
                j = base + offset
                row = k_s[pl.ds(at + j, 1), :]
                for head in range(2):
                    total = jnp.zeros((length, LANES), f32)
                    for c in range(width // LANES):
                        columns = slice(head * width + c * LANES, head * width + (c + 1) * LANES)
                        total = total + jnp.tanh(
                            q_s[at : at + length, columns] + row[:, columns]
                        ) * vec_ref[6:7, columns]
                    value = jnp.sum(total, -1, keepdims=True)
                    sums = tuple(
                        jnp.where(lane == j, value, s) if h == head else s
                        for h, s in enumerate(sums)
                    )
            return sums

        blocks = length // group
        zero = jnp.zeros((length, LANES), f32)
        mono, window = lax.fori_loop(0, blocks, energy_step, (zero, zero))
        e_s[0, :, u, :] = mono
        e_s[1, :, u, :] = window

    mask = jnp.zeros((8, LANES), f32)
    row_u = lax.broadcasted_iota(jnp.int32, (8, LANES), 0)
    lane_u = lax.broadcasted_iota(jnp.int32, (8, LANES), 1)
    for u in range(utts):
        inside_u = jnp.logical_and(row_u == u, lane_u < frames_ref[u])
        mask = jnp.where(inside_u, 1.0, mask)
    mask = mask[None]
    mono = e_s[0] + ENERGY_OFFSET
    window = e_s[1]
    chosen = jax.nn.sigmoid(mono)
    inside = (lane_block < length).astype(f32)
    sel_s[...] = chosen * mask
    leave = (jnp.maximum(mono, 0.0) + jnp.log1p(jnp.exp(-jnp.abs(mono)))) * mask
    prob = jnp.exp(-leave) * inside
    prob_s[...] = prob

    def right(value, distance):
        return pltpu.roll(value, distance, value.ndim - 1)

    def left(value, distance):
        return pltpu.roll(value, LANES - distance, value.ndim - 1)

    diagonals = 2 * length - 1
    bits = [2**n for n in range(5)]

    def skewed(value):
        value = jnp.concatenate([value, jnp.zeros((diagonals - length, 8, LANES), f32)], 0)
        for bit in bits:
            moved = jnp.concatenate([jnp.zeros((bit, 8, LANES), f32), value[:-bit]], 0)
            value = jnp.where(lane_row & bit != 0, moved, value)
        return value

    def straight(value):
        for bit in bits:
            moved = jnp.concatenate([value[bit:], jnp.zeros((bit, 8, LANES), f32)], 0)
            value = jnp.where(lane_row & bit != 0, moved, value)
        return value[:length]

    lane_row = lax.broadcasted_iota(jnp.int32, (8, LANES), 1)
    sel_d[...] = skewed(sel_s[...])
    prob_d[...] = skewed(jnp.where(lane_block < length - 1, prob, 0.0))

    def align_step(d, total):
        reach_d[d] = total
        return sel_d[d] * total + right(prob_d[d] * total, 1)

    lax.fori_loop(0, diagonals, align_step, jnp.where(lane_row == 0, 1.0, 0.0).astype(f32))
    w_s[...] = straight(reach_d[...])
    a_s[...] = sel_s[...] * w_s[...]

    aligned = a_s[...]
    own = jnp.where(lane_block == 0, 1.0, jax.nn.sigmoid(window - right(window, 1)))
    nxt = jax.nn.sigmoid(window - left(window, 1))
    own_s[...] = own
    nxt_s[...] = nxt
    beta = aligned * own + jnp.where(lane_block < length - 1, left(aligned, 1), 0.0) * nxt
    g_s[...] = beta

    for u in range(utts):
        at = u * length
        weights = g_s[:, u, :].astype(low)[:, :length]
        ctx_s[at : at + length] = jnp.dot(
            weights, mem_s[at : at + length].astype(low), preferred_element_type=f32
        )
    context_ref[...] = ctx_s[...].astype(low)

    loads[2].wait()
    loads[3].wait()
    third_low, third_high = third_s[0], third_s[1]
    squash = jnp.tanh(
        jnp.dot(dec_ref[...], third_low, preferred_element_type=f32)
        + jnp.dot(context_ref[...], third_high, preferred_element_type=f32)
        + vec_ref[7:8, :width]
    )
    squash_ref[...] = squash.astype(low)
    pull = contract(gl_ref[0], out_s[0], 1, 1) + contract(
        gl_ref[1], out_s[1], 1, 1
    )
    dz = (pull * (1.0 - squash * squash)).astype(low)
    dz_ref[...] = dz
    sources = [dec_ref, context_ref, dz_ref, squash_ref]
    handed = [
        remote(source, facts.at[n], fact_sems.at[0, n], fact_sems.at[1, n], other)
        for n, source in enumerate(sources)
    ]
    handed.append(remote(gl_ref.at[1 - core], facts_gl, fact_sems.at[0, 4], fact_sems.at[1, 4], other))
    for copy in handed:
        copy.start()
    dvec_ref[...] = jnp.zeros_like(dvec_ref)
    dvec_ref[7:8, :width] = jnp.sum(dz.astype(f32), 0, keepdims=True)
    for h in range(2):
        begin = width + h * vocab_half
        row = jnp.concatenate(
            [
                jnp.sum(gl_f[h], 0, keepdims=True),
                jnp.zeros((1, 2 * width - vocab_pad), f32),
            ],
            -1,
        )
        dvec_ref[7:8] += pltpu.roll(row, begin, 1)
        bias = pltpu.roll(vec_ref[7:8], 2 * width - begin, 1)[:, :vocab_pad]
        own_logits[h] = (
            jnp.dot(squash_ref[...], out_s[h], preferred_element_type=f32) + bias
        ).astype(low)
    logits_kept = pltpu.make_async_copy(own_logits.at[core], logits_ref.at[core], logit_sems.at[0])
    logits_away = remote(
        own_logits.at[1 - core], logits_ref.at[core], logit_sems.at[1], logit_sems.at[2], other
    )
    logits_kept.start()
    logits_away.start()
    ddec_ref[...] = contract(dz, third_low, 1, 1)
    ctx_s[...] = contract(dz, third_high, 1, 1).astype(low).astype(f32)

    pad = jnp.zeros((length, LANES - length), f32)
    for u in range(utts):
        at = u * length
        weights = g_s[:, u, :].astype(low)[:, :length]
        pulled = ctx_s[at : at + length].astype(low)
        beta_grad = contract(pulled, mem_s[at : at + length].astype(low), 1, 1)
        e_s[0, :, u, :] = jnp.concatenate([beta_grad, pad], -1)
        mem_s[at : at + length] = contract(weights, pulled, 0, 0)

    for copy in handed:
        copy.wait_recv()
    joined = jnp.where(core == 0, dec_ref[...], context_ref[...])
    joined_other = jnp.where(core == 0, facts[0], facts[1])
    part_rows, out_rows = g_third.shape[1], g_out.shape[1]
    total = (contract(joined, dz_ref[...], 0, 0) + contract(joined_other, facts[2], 0, 0)).astype(low)
    for block in range(n_dp):
        g_third[block] = total[block * part_rows : (block + 1) * part_rows]
    total = (contract(squash_ref[...], gl_ref[core], 0, 0) + contract(facts[3], facts_gl[...], 0, 0)).astype(low)
    for block in range(n_dp):
        g_out[block] = total[block * out_rows : (block + 1) * out_rows]
    third_fold = Fold(
        place, lambda kz, kf, kg: g_third[place.block(kz, kf, kg)].astype(f32), t_stage, t_near, None, sems_ft
    )
    out_fold = Fold(
        place, lambda kz, kf, kg: g_out[place.block(kz, kf, kg)].astype(f32), o_stage, o_near, None, sems_fo
    )
    third_fold.stage_a()
    out_fold.stage_a()

    beta_grad = e_s[0]
    own = own_s[...]
    nxt = nxt_s[...]
    g_s[...] = beta_grad * own + jnp.where(lane_block >= 1, right(beta_grad * nxt, 1), 0.0)
    aligned = a_s[...]
    from_own = jnp.where(lane_block >= 1, beta_grad * aligned * own * (1.0 - own), 0.0)
    from_next = (
        beta_grad
        * jnp.where(lane_block < length - 1, left(aligned, 1), 0.0)
        * nxt
        * (1.0 - nxt)
    )
    d_s[1] = (from_own - left(from_own, 1) + from_next - right(from_next, 1)) * inside

    prob = prob_s[...]
    reach_d[...] = skewed(g_s[...])

    def retreat_step(k, after):
        d = diagonals - 1 - k
        grad_align = reach_d[d] + after
        total = sel_d[d] * grad_align + prob_d[d] * left(after, 1)
        reach_d[d] = grad_align
        back_d[d] = total
        return total

    lax.fori_loop(0, diagonals, retreat_step, jnp.zeros((8, LANES), f32))
    e_s[0] = straight(reach_d[...])
    e_s[1] = straight(back_d[...])
    reached = w_s[...]
    grad_select = reached * e_s[0]
    grad_prob = reached * jnp.where(lane_block < length - 1, left(e_s[1], 1), 0.0)
    chosen = sel_s[...]
    d_s[0] = grad_select * chosen * (1.0 - chosen) - grad_prob * prob * chosen

    dka_s[...] = jnp.zeros_like(dka_s)
    spots = lax.broadcasted_iota(jnp.int32, (LANES, length * LANES), 1) // LANES
    picks = (lax.broadcasted_iota(jnp.int32, (LANES, length * LANES), 0) == spots).astype(f32)
    for head in range(2):
        for u in range(utts):
            d_rows[u * length : (u + 1) * length] = d_s[head, :, u, :]
        bc_s[head] = jnp.dot(
            d_rows[...], picks, precision=lax.Precision.HIGHEST, preferred_element_type=f32
        )

    def energy_back(u, dvec):
        at = pl.multiple_of(u * length, 8)
        count = length // UNROLL
        for c in range(2 * width // tile):
            columns = slice(c * tile, (c + 1) * tile)
            head = c * tile // width
            q_now = q_s[pl.ds(at, length), columns]

            def back_step(block, sums, head=head, columns=columns, q_now=q_now):
                dq, dw = sums
                for offset in range(UNROLL):
                    j = block * UNROLL + offset
                    squash_all = jnp.tanh(q_now + k_s[pl.ds(at + j, 1), columns])
                    grad = bc_s[head, pl.ds(at, length), pl.ds(pl.multiple_of(j * LANES, LANES), LANES)]
                    grad = jnp.concatenate([grad] * (tile // LANES), -1)
                    scaled = grad * squash_all
                    dw = dw + scaled
                    moved = grad - scaled * squash_all
                    dq = dq + moved
                    dka_s[pl.ds(at + j, 1), columns] = jnp.sum(moved, 0, keepdims=True)
                return (dq, dw)

            zero = jnp.zeros((length, tile), f32)
            dq, dw = lax.fori_loop(0, count, back_step, (zero, zero))
            dq = dq * vec_ref[6:7, columns]
            dqa_s[pl.ds(at, length), columns] = dq
            dvec_ref[5:6, columns] += jnp.sum(dq, 0, keepdims=True)
            dvec_ref[6:7, columns] += jnp.sum(dw, 0, keepdims=True)
        return dvec

    lax.fori_loop(0, utts, energy_back, 0)
    for h in range(2):
        columns = slice(h * width, (h + 1) * width)
        dq_ref[h] = dqa_s[:, columns].astype(low)
        dk_ref[h] = (dka_s[:, columns] * vec_ref[6:7, columns]).astype(low)
        ddec_ref[...] += jnp.dot(dq_ref[h], mats_ref[0, columns], preferred_element_type=f32)
        mem_s[...] += jnp.dot(dk_ref[h], mats_ref[1, columns], preferred_element_type=f32)
    for u in range(utts):
        at = slice(u * length, (u + 1) * length)
        back_s[0, u] = mem_s[at].astype(low)
        back_s[1, u] = ddec_ref[at].astype(low)
    role = place.role
    mine = core == role
    guest = jnp.logical_not(mine)
    stay = pltpu.make_async_copy(back_s.at[role], outer_ref.at[core], back_sems.at[0, 0])
    cross = remote(back_s.at[role], outer_ref.at[core], back_sems.at[0, 0], back_sems.at[1, core], (role, chip))
    away = remote(
        back_s.at[1 - role],
        outer_ref.at[core],
        back_sems.at[0, 1],
        back_sems.at[1, core],
        (role, chip + place.along[1]),
    )
    away.start()
    pl.when(mine)(stay.start)
    pl.when(guest)(cross.start)
    third_fold.stage_half(third_half)
    out_fold.stage_half(out_half)
    logits_kept.wait()
    logits_away.wait()
    for copy in handed:
        copy.wait_send()
    away.wait_send()
    pl.when(mine)(stay.wait)
    pl.when(guest)(cross.wait_send)

    def arrived(slot):
        target = outer_ref.at[slot]
        remote(target, target, back_sems.at[0, 0], back_sems.at[1, slot], other).wait_recv()

    arrived(1 - core)
    pl.when(guest)(lambda: arrived(core))
    for moved in (third_fold, out_fold):
        moved.sent_all()


def attention(n_dp, frames, labels, pair, cotangent, vectors, pairs, third, outs):
    rows, width = pair.shape[1:]
    utts = frames.shape[0]
    length = rows // utts
    low, f32 = jnp.bfloat16, jnp.float32
    line, side = DP_LAYOUTS[n_dp][:2]
    vocab_pad = outs.shape[2]
    third_block, out_block = (width // n_dp, width), (width // n_dp, vocab_pad)
    vocab_half = cotangent.shape[2]
    small = (length, 8, LANES)
    diagonal = (2 * length - 1, 8, LANES)
    dma = pltpu.SemaphoreType.DMA
    return pl.pallas_call(
        functools.partial(attention_kernel, n_dp),
        out_shape=(
            jax.ShapeDtypeStruct((rows, width), low),
            jax.ShapeDtypeStruct((2, rows, width), low),
            jax.ShapeDtypeStruct((2, rows, width), low),
            jax.ShapeDtypeStruct((8, 2 * width), f32),
            jax.ShapeDtypeStruct((2, rows, vocab_pad), low),
            jax.ShapeDtypeStruct((2, utts, length, width), low),
            jax.ShapeDtypeStruct((side, line) + third_block, low),
            jax.ShapeDtypeStruct((side, line) + out_block, low),
        ),
        in_specs=[SMEM_SPEC] * 2 + [VMEM_SPEC] * 3 + [ANY_SPEC] * 3,
        out_specs=(VMEM_SPEC,) * 8,
        scratch_shapes=[
            pltpu.VMEM((rows, width), low),
            pltpu.VMEM((rows, width), low),
            pltpu.VMEM((rows, width), f32),
            pltpu.VMEM((utts, length, vocab_half), low),
            pltpu.VMEM((2, rows, vocab_pad), f32),
            pltpu.VMEM((2, rows, vocab_pad), low),
            pltpu.VMEM((2, rows, vocab_pad), low),
            pltpu.VMEM((2, 2 * width, width), low),
            pltpu.VMEM((2, width, width), low),
            pltpu.VMEM((2, width, vocab_pad), low),
            pltpu.VMEM((2, utts, length, width), low),
            pltpu.VMEM((4, rows, width), low),
            pltpu.VMEM((rows, vocab_pad), low),
            pltpu.VMEM((n_dp,) + third_block, low),
            pltpu.VMEM((n_dp,) + out_block, low),
        ]
        + fold_buffers(line, side, third_block, low)
        + fold_buffers(line, side, out_block, low)
        + [
            pltpu.VMEM((rows, 2 * width), f32),
            pltpu.VMEM((rows, 2 * width), f32),
            pltpu.VMEM((rows, width), f32),
            pltpu.VMEM((rows, width), f32),
            pltpu.VMEM((rows, 2 * width), f32),
            pltpu.VMEM((rows, 2 * width), f32),
            pltpu.VMEM((2,) + small, f32),
            pltpu.VMEM(small, f32),
            pltpu.VMEM(small, f32),
            pltpu.VMEM(diagonal, f32),
            pltpu.VMEM(diagonal, f32),
            pltpu.VMEM(diagonal, f32),
            pltpu.VMEM(diagonal, f32),
            pltpu.VMEM(small, f32),
            pltpu.VMEM(small, f32),
            pltpu.VMEM(small, f32),
            pltpu.VMEM(small, f32),
            pltpu.VMEM(small, f32),
            pltpu.VMEM((2,) + small, f32),
            pltpu.VMEM((rows, LANES), f32),
            pltpu.VMEM((2, rows, length * LANES), f32),
            dma((4,)),
            dma((2,)),
            dma((2, 5)),
            dma((3,)),
            dma((2, 2)),
        ]
        + [fold_sems(line, side)] * 2,
        compiler_params=pltpu.CompilerParams(
            collective_id=2, has_side_effects=True, vmem_limit_bytes=VMEM_LIMIT
        ),
    )(frames, labels, pair, cotangent, vectors, pairs, third, outs)


def backward_kernel(
    n_dp,
    cell_ref,
    outer_ref,
    pair_ref,
    third_half,
    out_half,
    spread_ref,
    vectors_ref,
    dvec_ref,
    dq_any,
    dk_any,
    act_any,
    wt_any,
    ht_any,
    w_any,
    base_any,
    sum_ref,
    gin_ref,
    vec_sum,
    mats_sum,
    third_sum,
    out_sum,
    act_ref,
    wt_ref,
    ht_ref,
    ht_other,
    dpre_ref,
    dpre_other,
    outer_s,
    state,
    held,
    facts,
    own,
    g_mats,
    k_ends,
    k_near,
    k_far,
    m_near,
    m_far,
    m_parts,
    m_end,
    t_far,
    t_parts,
    t_end,
    o_far,
    o_parts,
    o_end,
    vec_s,
    vec_other,
    vec_parts,
    v_stage,
    v_near,
    v_far,
    v_parts,
    v_end,
    load_sem,
    fact_sems,
    pre_sems,
    ht_sems,
    gin_sems,
    vec_sems,
    sems_k,
    sems_m,
    sems_t,
    sems_o,
    sems_v,
    *role,
):
    halves, half_batch, steps, width = outer_ref.shape
    batch = halves * half_batch
    low, f32 = jnp.bfloat16, jnp.float32
    mem_ref, dec_ref = pair_ref.at[0], pair_ref.at[1]
    place = Place(n_dp)
    loads = [
        pltpu.make_async_copy(act_any, act_ref, load_sem.at[0]),
        pltpu.make_async_copy(wt_any, wt_ref, load_sem.at[1]),
        pltpu.make_async_copy(ht_any, ht_ref, load_sem.at[2]),
    ]
    core = place.core
    own_loads = [
        pltpu.make_async_copy(source.at[core], own.at[n], load_sem.at[8 + n])
        for n, source in enumerate((dq_any, dk_any))
    ]
    for load in own_loads + loads:
        load.start()
    place.greet()
    other = (1 - core, place.chip)
    encoder = place.role == 0
    mine = core == place.role
    third, outs = FoldRest(place, third_half, t_far, sems_t), FoldRest(place, out_half, o_far, sems_o)
    third_line, out_line = FoldLine(place, t_parts, t_end, sems_t), FoldLine(place, o_parts, o_end, sems_o)
    mats_line = FoldLine(place, m_parts, m_end, sems_m)
    third.begin()
    outs.begin()
    sources = [dq_any.at[1 - core], dk_any.at[1 - core], dec_ref, mem_ref]
    handed = [
        remote(source, facts.at[n], fact_sems.at[0, n], fact_sems.at[1, n], other)
        for n, source in enumerate(sources)
    ]
    handed.append(remote(ht_any, ht_other, ht_sems.at[0], ht_sems.at[1], other))
    for copy in handed:
        copy.start()
    state[...] = jnp.zeros_like(state)
    held[...] = jnp.zeros_like(held)
    outer_s[:, batch:] = jnp.zeros((steps, ROWS - batch, width), f32)
    for u in range(batch):
        outer_s[:, u, :] = outer_ref[u // half_batch, u % half_batch].astype(f32)

    def step(k, carry):
        t = steps - 1 - k
        rows = pl.ds(pl.multiple_of(t * ROWS, ROWS), ROWS)
        after = pl.ds(pl.multiple_of((t + 1) * ROWS, ROWS), ROWS)
        hidden_total = outer_s[t]
        for q in range(4):
            hidden_total = hidden_total + jnp.dot(
                state[:, q * width : (q + 1) * width], wt_ref[q], preferred_element_type=f32
            )
        in_gate = act_ref[rows, :width]
        forget = act_ref[rows, width : 2 * width]
        candidate = act_ref[rows, 2 * width : 3 * width]
        out_gate = act_ref[rows, 3 * width :]
        squash = jnp.tanh(cell_ref[after])
        cell_total = held[...] + hidden_total * out_gate * (1.0 - squash * squash)
        held[...] = cell_total * forget
        grads = jnp.concatenate(
            [
                cell_total * candidate * in_gate * (1.0 - in_gate),
                cell_total * cell_ref[rows] * forget * (1.0 - forget),
                cell_total * in_gate * (1.0 - candidate * candidate),
                hidden_total * squash * out_gate * (1.0 - out_gate),
            ],
            -1,
        ).astype(low)
        state[...] = grads
        dpre_ref[rows] = grads
        return carry

    shares = 4
    share = steps // shares

    def hand_over(n):
        top = (steps - (n + 1) * share) * ROWS
        rows = slice(top, top + share * ROWS)
        columns = pl.ds(pl.multiple_of((1 - core) * 2 * width, 2 * width), 2 * width)
        copy = remote(
            dpre_ref.at[rows, columns], dpre_other.at[rows, :], pre_sems.at[0, n], pre_sems.at[1, n], other
        )
        copy.start()
        handed.append(copy)

    part_rows = g_mats.shape[2]

    def matrices():
        for copy in handed[:4]:
            copy.wait_recv()
        for load in own_loads:
            load.wait()
        pairs = [
            (own[0], dec_ref[...], facts[0], facts[2]),
            (own[1], mem_ref[...], facts[1], facts[3]),
        ]
        for m, (a, b, c, d) in enumerate(pairs):
            total = (contract(a, b, 0, 0) + contract(c, d, 0, 0)).astype(low)
            for block in range(n_dp):
                g_mats[m, block] = total[block * part_rows : (block + 1) * part_rows]

    mats = Fold(
        place,
        lambda kz, kf, kg: g_mats[0, place.block(kz, kf, kg)].astype(f32),
        lambda kz, kf, kg: g_mats.at[0, place.block(kz, kf, kg)],
        m_near,
        m_far,
        sems_m,
    )
    keys = FoldFirst(
        place, lambda kz, kf, kg: g_mats.at[1, place.block(kz, kf, kg)], k_ends, k_near, k_far, sems_k
    )
    lines = list(reversed(range(place.line)))
    matrices()
    keys.begin()
    mats.stage_a()
    for load in loads:
        load.wait()
    lax.fori_loop(0, share, step, 0)
    hand_over(0)
    for kz in lines:
        t_parts[kz] = third.summed(kz)
        o_parts[kz] = outs.summed(kz)
    third_line.begin()
    out_line.begin()
    lax.fori_loop(share, 2 * share, step, 0)
    hand_over(1)
    mats.stage_b(*lines[: place.line // 2])
    lax.fori_loop(2 * share, 3 * share, step, 0)
    hand_over(2)
    lax.fori_loop(3 * share, steps, step, 0)
    hand_over(3)

    late = [pltpu.make_async_copy(base_any, act_ref.at[:, :width], load_sem.at[3])]
    for q in range(4):
        late.append(
            pltpu.make_async_copy(w_any.at[:, q * width : (q + 1) * width], wt_ref.at[q], load_sem.at[4 + q])
        )
    for load in late:
        load.start()
    base_columns, gin_columns = slice(0, width), slice(width, 2 * width)
    block_rows = sum_ref.shape[0]
    half = pl.ds(pl.multiple_of(core * 2 * width, 2 * width), 2 * width)
    count = max(ROWS, block_rows // FOLDS)

    def part(first):
        def at(kz, kf, kg):
            rows = pl.ds(pl.multiple_of(place.block(kz, kf, kg) * block_rows + first, count), count)
            return jnp.dot(ht_ref[rows], dpre_ref[:, half], preferred_element_type=f32) + jnp.dot(
                ht_other[rows], dpre_other[...], preferred_element_type=f32
            )

        return at

    folds = [
        FoldRole(place, part(n * count), stage, near, far, end, sems)
        for n, (stage, near, far, end, sems) in enumerate(zip(*(role[k::5] for k in range(5))))
    ]
    items = [(fold, kz) for kz in lines for fold in folds]
    done = 0

    def advance(until):
        for n in range(done, until):
            if n < len(items):
                items[n][0].stage_a(items[n][1])
            if 0 <= n - LAG < len(items):
                items[n - LAG][0].stage_b(items[n - LAG][1])
            if 0 <= n - LAST_LAG < len(items):
                items[n - LAST_LAG][0].stage_c(items[n - LAST_LAG][1])
        return max(done, until)

    for copy in handed[4:]:
        copy.wait_recv()
    done = advance(LAG)
    mats.stage_b(*lines[place.line // 2 :])
    done = advance(LAG + 1)
    for load in late:
        load.wait()
    chunks = [slice(at, at + LANES) for at in range(0, steps * ROWS, LANES)]
    for rows in chunks:
        act_ref[rows, gin_columns] = contract(dpre_ref[rows, :width], wt_ref[0], 1, 1)
        for q in range(1, 4):
            act_ref[rows, gin_columns] += contract(dpre_ref[rows, q * width : (q + 1) * width], wt_ref[q], 1, 1)
    done = advance(LAG + 2)
    for kz in lines:
        m_parts[kz] = mats.summed(kz)
    mats_line.begin()
    vec_s[...] = dvec_ref[...]
    vec_s[4:5] = jnp.zeros((1, 2 * width), f32)
    for rows in chunks:
        input_grad = jnp.where(encoder, act_ref[rows, gin_columns], 0.0)
        vec_s[4:5, :width] += jnp.sum(input_grad * act_ref[rows, base_columns], 0, keepdims=True)
        vec_s[4:5, width:] += jnp.sum(input_grad, 0, keepdims=True)
    for q in range(4):
        columns = slice((q % 2) * width, (q % 2 + 1) * width)
        bias = jnp.sum(dpre_ref[:, q * width : (q + 1) * width].astype(f32), 0, keepdims=True)
        for role_index in range(2):
            row = 2 * role_index + q // 2
            vec_s[row : row + 1, columns] = jnp.where(place.role == role_index, bias, 0.0)

    @pl.when(encoder)
    def _():
        for rows in chunks:
            grads = act_ref[rows, gin_columns] * vectors_ref[4:5, :width]
            values = act_ref[rows, base_columns]
            act_ref[rows, gin_columns] = spread_ref[rows, :1] * (
                grads
                - jnp.mean(grads, -1, keepdims=True)
                - values * jnp.mean(grads * values, -1, keepdims=True)
            )

    done = advance(LAG + 3)
    gin_u = act_ref.at[: batch * steps, 2 * width : 3 * width]
    for u in range(batch):
        straight = outer_ref[u // half_batch, u % half_batch].astype(f32)
        gin_u[u * steps : (u + 1) * steps] = act_ref[:, gin_columns].reshape(steps, ROWS, width)[
            :, u, :
        ] + jnp.where(encoder, straight, 0.0)
    kept = pltpu.make_async_copy(gin_u, gin_ref, gin_sems.at[0])
    away = remote(gin_u, gin_ref, gin_sems.at[1], gin_sems.at[2], (1 - core, place.chip + place.along[1]))

    @pl.when(mine)
    def _():
        kept.start()

    @pl.when(jnp.logical_not(mine))
    def _():
        away.start()

    own_half = pl.ds(pl.multiple_of(core * width, width), width)
    other_half = pl.ds(pl.multiple_of((1 - core) * width, width), width)
    trade = remote(vec_s.at[:, other_half], vec_other, vec_sems.at[0], vec_sems.at[1], other)
    trade.start()
    trade.wait_recv()
    total = vec_s[:, own_half] + vec_other[...]
    piece = width // n_dp
    per_tile = LANES // piece
    for block in range(n_dp):
        tile = total[:, (block // per_tile) * LANES : (block // per_tile + 1) * LANES]
        turn = (block % per_tile) * piece
        vec_parts[block] = pltpu.roll(tile, LANES - turn, 1) if turn else tile
    vecs = Fold(place, lambda kz, kf, kg: vec_parts[place.block(kz, kf, kg)], v_stage, v_near, v_far, sems_v)
    vec_line = FoldLine(place, v_parts, v_end, sems_v)
    vecs.stage_a()
    done = advance(LAG + 5)
    keys.stage_line()
    done = advance(len(items) - 2)
    keys.stage_second()
    vecs.stage_b()
    done = advance(len(items) + LAG)
    for n in lines:
        v_parts[n] = vecs.summed(n)
    vec_line.begin()
    third_sum[...] = third_line.result()
    out_sum[...] = out_line.result()
    done = advance(len(items) + LAST_LAG)
    mats_sum[:part_rows] = mats_line.result()
    mats_sum[part_rows:] = keys.result()
    vec_sum[...] = vec_line.result()
    for n, fold in enumerate(folds):
        fold.result(sum_ref.at[n * count : (n + 1) * count])

    @pl.when(mine)
    def _():
        kept.wait()

    @pl.when(jnp.logical_not(mine))
    def _():
        away.wait()

    trade.wait_send()
    for copy in handed:
        copy.wait_send()
    for fold in (*folds, vecs, vec_line, mats, mats_line, keys, third, outs, third_line, out_line):
        fold.sent_all()


def backward(
    n_dp,
    act,
    cell,
    outer,
    dq,
    dk,
    pair,
    third_half,
    out_half,
    weight_t,
    ht,
    weight,
    base,
    spread,
    vectors,
    dvec,
):
    rows, width = base.shape
    half_batch, steps = outer.shape[1:3]
    batch = 2 * half_batch
    low, f32 = jnp.bfloat16, jnp.float32
    line, side = DP_LAYOUTS[n_dp][:2]
    utt_rows = pair.shape[1]
    mats_block = (width // n_dp, width)
    third_block, out_block = third_half.shape[2:], out_half.shape[2:]
    block_rows = 2 * width // n_dp
    block = (max(ROWS, block_rows // FOLDS), 2 * width)
    dma = pltpu.SemaphoreType.DMA
    rest = ((side - 1, line), (line,), (line - 1,))
    return pl.pallas_call(
        functools.partial(backward_kernel, n_dp),
        out_shape=(
            jax.ShapeDtypeStruct((block_rows, 4 * width), f32),
            jax.ShapeDtypeStruct((batch * steps, width), f32),
            jax.ShapeDtypeStruct((8, LANES), f32),
            jax.ShapeDtypeStruct((2 * mats_block[0], width), f32),
            jax.ShapeDtypeStruct(third_block, f32),
            jax.ShapeDtypeStruct(out_block, f32),
        ),
        in_specs=[VMEM_SPEC] * 8 + [ANY_SPEC] * 7,
        out_specs=(VMEM_SPEC, ANY_SPEC) + (VMEM_SPEC,) * 4,
        scratch_shapes=[
            pltpu.VMEM((rows, 4 * width), f32),
            pltpu.VMEM((4, width, width), low),
            pltpu.VMEM((2 * width, rows), low),
            pltpu.VMEM((2 * width, rows), low),
            pltpu.VMEM((rows, 4 * width), low),
            pltpu.VMEM((rows, 2 * width), low),
            pltpu.VMEM((steps, ROWS, width), f32),
            pltpu.VMEM((ROWS, 4 * width), low),
            pltpu.VMEM((ROWS, width), f32),
            pltpu.VMEM((4, utt_rows, width), low),
            pltpu.VMEM((2, utt_rows, width), low),
            pltpu.VMEM((2, n_dp) + mats_block, low),
            pltpu.VMEM((line - 1, side, side) + mats_block, low),
            pltpu.VMEM((side - 1, side) + mats_block, low),
            pltpu.VMEM((side - 1,) + mats_block, low),
            pltpu.VMEM((side - 1, side, line) + mats_block, low),
        ]
        + [
            pltpu.VMEM(shape + size, low)
            for size in (mats_block, third_block, out_block)
            for shape in rest
        ]
        + [
            pltpu.VMEM((8, 2 * width), f32),
            pltpu.VMEM((8, width), f32),
            pltpu.VMEM((n_dp, 8, LANES), f32),
        ]
        + fold_buffers(line, side, (8, LANES), f32)
        + [pltpu.VMEM(shape + (8, LANES), f32) for shape in rest]
        + [dma((10,)), dma((2, 4)), dma((2, 4)), dma((2,)), dma((3,)), dma((2,))]
        + [fold_sems(line, side, first=True)]
        + [fold_sems(line, side)] * 4
        + (
            fold_buffers(line, side, block, low)
            + [
                pltpu.VMEM((side - 1, line) + block, low),
                pltpu.VMEM((2, line // 2) + block, low),
                fold_sems(line, side),
            ]
        )
        * (block_rows // block[0]),
        compiler_params=pltpu.CompilerParams(
            collective_id=3, has_side_effects=True, vmem_limit_bytes=VMEM_LIMIT
        ),
    )(
        cell,
        outer,
        pair,
        third_half,
        out_half,
        spread,
        vectors,
        dvec,
        dq,
        dk,
        act,
        weight_t,
        ht,
        weight,
        base,
    )


STEP = 5
BETA_ONE = 0.9
BETA_TWO = 0.999
ADAM_EPS = 1e-08
WEIGHT_DECAY = 0.01
RATE_LSTM = 0.05
RATE_MATRIX = 0.02
RATE_VECTOR = 0.3


def adamw(master, first, second, grad, rate):
    first_new = BETA_ONE * first + (1.0 - BETA_ONE) * grad
    second_new = BETA_TWO * second + (1.0 - BETA_TWO) * grad * grad
    first_hat = first_new / (1.0 - BETA_ONE**STEP)
    second_hat = second_new / (1.0 - BETA_TWO**STEP)
    master_new = master - rate * (
        first_hat / (jnp.sqrt(second_hat) + ADAM_EPS) + WEIGHT_DECAY * master
    )
    return (master_new, first_new, second_new)


def local(
    inputs,
    counts,
    cotangent,
    lstm_master,
    lstm_copy,
    lstm_first,
    lstm_second,
    mats_master,
    mats_copy,
    mats_first,
    mats_second,
    out_master,
    out_copy,
    out_first,
    out_second,
    vec_master,
    vec_first,
    vec_second,
):
    low, f32 = jnp.bfloat16, jnp.float32
    n_dp = lax.axis_size("dp")
    on_first = lax.axis_index("section") == 0
    batch_size, length, model_width = inputs.shape[1:]
    half = batch_size // 2
    vocab_half = out_copy.shape[1]
    vocab_pad = -(-vocab_half // LANES) * LANES
    piece = vec_master.shape[1]

    kept = jnp.where(on_first, counts[0, :half], counts[0, half:])
    other = jnp.where(on_first, counts[0, half:], counts[0, :half])
    other = lax.ppermute(other, "section", [(0, 1), (1, 0)])
    frames, labels = jnp.where(on_first, kept, other), jnp.where(on_first, other, kept)

    mats_block = jnp.swapaxes(mats_copy, 1, 2)
    act, cell, ht, base, spread, vectors, pair, weight, weight_t, pairs, third, outs = forward(
        n_dp, inputs[0], lstm_copy[0], mats_block, out_copy, vec_master
    )
    pair = pair.reshape(2, half * length, model_width)
    pairs = pairs.reshape(2, 2 * model_width, model_width)
    third = third.reshape(2, model_width, model_width)
    outs = outs.reshape(2, model_width, vocab_pad)
    dz, dq, dk, vec_rows, logits, outer, third_half, out_half = attention(
        n_dp, frames, labels, pair, cotangent, vectors, pairs, third, outs
    )
    logits = logits.reshape(batch_size, length, vocab_pad)[..., :vocab_half]
    lstm_sum, inputs_grad, vec_sum, mats_sum, third_sum, out_sum = backward(
        n_dp,
        act,
        cell,
        outer,
        dq,
        dk,
        pair,
        third_half,
        out_half,
        weight_t,
        ht,
        weight,
        base.reshape(-1, model_width),
        spread.reshape(-1, LANES),
        vectors,
        vec_rows,
    )
    mats_sum = jnp.concatenate([mats_sum.reshape(2, -1, model_width), third_sum[None]], 0)
    mats_sum = jnp.swapaxes(mats_sum, 1, 2)
    lstm_new, lstm_first_new, lstm_second_new = adamw(
        lstm_master, lstm_first, lstm_second, lstm_sum[None], RATE_LSTM
    )
    mats_new, mats_first_new, mats_second_new = adamw(
        mats_master, mats_first, mats_second, mats_sum, RATE_MATRIX
    )
    out_new, out_first_new, out_second_new = adamw(
        out_master, out_first, out_second, out_sum[:, :vocab_half], RATE_MATRIX
    )
    vec_new, vec_first_new, vec_second_new = adamw(
        vec_master, vec_first, vec_second, vec_sum[:, :piece], RATE_VECTOR
    )
    return (
        logits,
        inputs_grad.reshape(inputs.shape),
        lstm_new,
        lstm_first_new,
        lstm_second_new,
        lstm_new.astype(low),
        mats_new,
        mats_first_new,
        mats_second_new,
        mats_new.astype(low),
        out_new,
        out_first_new,
        out_second_new,
        out_new.astype(low),
        vec_new,
        vec_first_new,
        vec_second_new,
    )


def solution(mesh):
    lstm = P("section", "dp", None)
    mats = P(None, None, ("section", "dp"))
    out = P("dp", "section")
    vec = P(None, ("section", "dp"))
    logits = P("dp", None, "section")
    rows = P("section", "dp", None, None)
    groups = (lstm,) * 4 + (mats,) * 4 + (out,) * 4 + (vec,) * 3
    return jax.shard_map(
        local,
        mesh=mesh,
        in_specs=(rows, P("section", "dp"), logits) + groups,
        out_specs=(logits, rows) + groups,
        check_vma=False,
    )
```
